32 devices in a mesh: req: 2 (over x), exp: 16 (over z, y, core).
Axes of the slice: x: 2, y: 2, z: 4, core: 2. Of those that a mesh axis runs over, the one named last changes fastest.
Arguments:
- attn_out: bfloat16 [4096, 2048], P(('req', 'exp')), may hold values from -6 to 6
- residual: bfloat16 [4096, 2048], P(('req', 'exp')), may hold values from -6 to 6
- out_weight: bfloat16 [2048, 2048], P('exp'), may hold values from -0.125 to 0.125
- norm_gain: float32 [2048], replicated, may hold values from 0.25 to 1.75
- expert_ids: int32 [4096, 6], P(('req', 'exp')), may hold values from 0 to 15, all different within a row; in each aligned block of 128 rows (0 to 127, 128 to 255, ...) at most 72 rows name the same one
- gate_weights: float32 [4096, 6], P(('req', 'exp')), may hold values from 0.05 to 0.5
- expert_gate: bfloat16 [16, 2048, 1408], P('exp'), may hold values from -0.125 to 0.125
- expert_up: bfloat16 [16, 2048, 1408], P('exp'), may hold values from -0.125 to 0.125
- expert_down: bfloat16 [16, 1408, 2048], P('exp'), may hold values from -0.15625 to 0.15625
- shared_gate: bfloat16 [2048, 1408], P(None, 'req'), may hold values from -0.125 to 0.125
- shared_up: bfloat16 [2048, 1408], P(None, 'req'), may hold values from -0.125 to 0.125
- shared_down: bfloat16 [2048, 1408], P(None, 'req'), may hold values from -0.15625 to 0.15625
Outputs:
- mixed: bfloat16 [4096, 2048], P(('req', 'exp'))
The draws below stay inside these ranges and needn't reach their ends.
Inputs may be any that keep to these rules, and one draw needn't show every extreme that they name: `expert_ids`: within the rows of one device no expert is named by more than 72 rows, and each row names 6 different experts.
All inputs are finite; a program needn't handle non-finite values.
Results may differ from the reference program's by a relative error of at most 0.012.
Values may be sent and summed in bfloat16 or wider, within the bound.
No kernel may reach another device: no remote copies, remote signals or barrier semaphores. Data moves between devices by JAX's collectives and lax.ppermute only.
A program may use at most 192 MiB of HBM per device.

```python
import math
import jax
import jax.numpy as jnp
import numpy as np
from jax import lax

D = 2048
FF = 1408
SHARED_FF = 1408
TOPK = 6
ROWS_DEV = 128
EXPERTS = 16
ROWS = 4096
CAP = 72
N_REQ = 2
N_EXP = 16


def steps_of(stream_key, shape, pieces, smallest, largest):
    level = 1.0
    for axis_at, blocks in pieces:
        steps = jax.random.uniform(jax.random.fold_in(jax.random.fold_in(stream_key, 6), axis_at), (blocks,), jnp.float32, smallest / len(pieces), largest / len(pieces))
        level = level * jnp.repeat(jnp.exp(steps), shape[axis_at] // blocks).reshape((-1,) + (1,) * (len(shape) - 1 - axis_at))
    return level


def shared_out(stream_key, own, number, rows, number_of, top, limit, slope):
    ranking = jax.random.permutation(stream_key, number_of)
    crowded, usual = shares(number_of, rows * top, limit, slope, True), shares(number_of, rows * top, limit, slope, False)
    places = jnp.arange(number_of)

    def named(lengths, rotation):
        used = int((lengths > 0).sum())
        fixed = max(1, used // 4)
        passed = fixed + (places - fixed + rotation * (used - fixed)) % max(1, number_of - fixed)
        return jnp.zeros((number_of,), jnp.int32).at[ranking[jnp.where(places < fixed, places, passed)]].set(jnp.asarray(lengths, jnp.int32))

    lengths = jnp.where(number % 4 == 0, named(crowded, number // 4), named(usual, number - number // 4 - 1))
    mixed = jax.random.permutation(jax.random.fold_in(own, 3), number_of)
    donor, taker = mixed[0:number_of // 2 * 2:2], mixed[1:number_of // 2 * 2:2]
    slack = jnp.minimum(lengths[donor] - 1, limit - lengths[taker]) // 2
    slack = jnp.where((donor == ranking[0]) | (taker == ranking[0]) | (lengths[taker] == 0), 0, jnp.maximum(slack, 0))
    passed = jax.random.randint(jax.random.fold_in(own, 4), (number_of // 2,), 0, 1 << 20) % (slack + 1)
    lengths = lengths.at[donor].add(-passed).at[taker].add(passed)
    members = jnp.searchsorted(jnp.cumsum(lengths), jnp.arange(rows * top), side="right").astype(jnp.int32)
    table = members.reshape(top, rows).T
    table = table[jax.random.permutation(jax.random.fold_in(own, 1), rows)]
    rotation = jax.random.randint(jax.random.fold_in(own, 2), (rows, 1), 0, top)
    return jnp.take_along_axis(table, (jnp.arange(top)[None, :] + rotation) % top, axis=1)


def shares(number_of, total, most, skew, full):
    loads = [(1 << 20) // math.isqrt(rank ** skew) + 1 for rank in range(1, number_of + 1)]
    largest = most if full else min(most, max(-(-total // number_of), total * loads[0] // sum(loads)))
    least = 1 if total - largest >= number_of - 1 else 0
    counts, spare = [largest] + [least] * (number_of - 1), total - largest - least * (number_of - 1)
    while spare > 0:
        candidates = [i for i in range(1, number_of) if counts[i] < largest] or [i for i in range(1, number_of) if counts[i] < most]
        mass, budget = sum([loads[i] for i in candidates]), spare
        for i in candidates:
            addition = min(most - counts[i], max(1, budget * loads[i] // mass), spare)
            counts[i] = counts[i] + addition
            spare = spare - addition
    return np.array(counts)


def scatter_about(own_key, shape, scale, most, shards=(), kind=jnp.bfloat16):
    loudness = steps_of(own_key, shape, shards, -0.22, 0.18) if shards else 1.0
    array = jax.random.normal(own_key, shape, jnp.float32) * scale * loudness
    return jnp.minimum(jnp.maximum(array, -most), most).astype(kind)


def setup_inputs(seed: int = 0) -> dict:
    key_of = jax.random.split(jax.random.key(seed), 13)
    attn_out = scatter_about(key_of[0], (ROWS, D), 1.0, 6.0, ((0, 32),))
    residual = scatter_about(key_of[1], (ROWS, D), 1.0, 6.0, ((0, 32),))
    out_weight = scatter_about(key_of[2], (D, D), D ** -0.5, 0.125, ((0, 16),))
    norm_gain = jnp.clip(1.0 + 0.15 * jax.random.normal(key_of[3], (D,), jnp.float32), 0.25, 1.75)
    expert_ids_keys = jax.random.split(jax.random.fold_in(key_of[4], 1), ROWS // ROWS_DEV)
    expert_ids_turns = jax.random.permutation(jax.random.fold_in(key_of[4], 3), ROWS // ROWS_DEV)
    expert_ids = jax.vmap(lambda own, number: shared_out(jax.random.fold_in(key_of[4], 2), own, number, ROWS_DEV, EXPERTS, TOPK, CAP, 3))(expert_ids_keys, expert_ids_turns).reshape((ROWS, TOPK))
    gate_weights = jnp.clip(0.05 + 0.45 * jax.random.uniform(key_of[5], (ROWS, TOPK), jnp.float32) ** steps_of(key_of[5], (ROWS, TOPK), ((0, 32),), -0.2, 0.2), 0.05, 0.5)
    expert_gate = scatter_about(key_of[6], (EXPERTS, D, FF), D ** -0.5, 0.125, ((0, 16),))
    expert_up = scatter_about(key_of[7], (EXPERTS, D, FF), D ** -0.5, 0.125, ((0, 16),))
    expert_down = scatter_about(key_of[8], (EXPERTS, FF, D), FF ** -0.5, 0.15625, ((0, 16),))
    shared_gate = scatter_about(key_of[9], (D, SHARED_FF), D ** -0.5, 0.125, ((1, 2),))
    shared_up = scatter_about(key_of[10], (D, SHARED_FF), D ** -0.5, 0.125, ((1, 2),))
    shared_down = scatter_about(key_of[11], (D, SHARED_FF), SHARED_FF ** -0.5, 0.15625, ((1, 2),))
    return dict(attn_out=attn_out, residual=residual, out_weight=out_weight, norm_gain=norm_gain, expert_ids=expert_ids, gate_weights=gate_weights, expert_gate=expert_gate, expert_up=expert_up, expert_down=expert_down, shared_gate=shared_gate, shared_up=shared_up, shared_down=shared_down)


def reference(attn_out, residual, out_weight, norm_gain, expert_ids, gate_weights, expert_gate, expert_up, expert_down, shared_gate, shared_up, shared_down):
    proj = jnp.dot(attn_out, out_weight, preferred_element_type=jnp.float32)
    stream = (residual.astype(jnp.float32) + proj).astype(jnp.bfloat16)
    stream_f = stream.astype(jnp.float32)
    scale = lax.rsqrt(lax.optimization_barrier(jnp.mean(stream_f * stream_f, axis=1, keepdims=True)) + 1e-06)
    normed = (stream_f * scale * norm_gain).astype(jnp.bfloat16)
    shared_g = jnp.dot(normed, shared_gate, preferred_element_type=jnp.float32)
    shared_u = jnp.dot(normed, shared_up, preferred_element_type=jnp.float32)
    shared_hidden = (jax.nn.silu(shared_g) * shared_u).astype(jnp.bfloat16)
    shared = lax.dot_general(shared_hidden, shared_down, (((1,), (1,)), ((), ())), preferred_element_type=jnp.float32)
    flat_ids = expert_ids.reshape(-1).astype(jnp.int32)
    weights = gate_weights.reshape(-1)
    pairs = ROWS * TOPK
    room = CAP * N_REQ * N_EXP
    pair_index = jnp.arange(pairs, dtype=jnp.int32)

    def one_expert(total, inputs):
        w_gate, w_up, w_down, which = inputs
        hit = flat_ids == which
        position = (jnp.cumsum(hit.astype(jnp.int32)) - 1).astype(jnp.int32)
        target = jnp.where(hit, position, room).astype(jnp.int32)
        table = jnp.full((room,), pairs, jnp.int32).at[target].set(pair_index, mode='drop')
        valid = table < pairs
        safe_pair = jnp.minimum(table, pairs - 1).astype(jnp.int32)
        row_index = (safe_pair // TOPK).astype(jnp.int32)
        taken = normed[row_index]
        gate_part = jnp.dot(taken, w_gate, preferred_element_type=jnp.float32)
        up_part = jnp.dot(taken, w_up, preferred_element_type=jnp.float32)
        hidden = (jax.nn.silu(gate_part) * up_part).astype(jnp.bfloat16)
        result = jnp.dot(hidden, w_down, preferred_element_type=jnp.float32).astype(jnp.bfloat16)
        factor = jnp.where(valid, weights[safe_pair], jnp.zeros((), weights.dtype))
        contrib = result.astype(jnp.float32) * factor[:, None]
        return (total.at[row_index].add(contrib), None)
    start_total = jnp.zeros((ROWS, D), jnp.float32)
    routed, _ = lax.scan(one_expert, start_total, (expert_gate, expert_up, expert_down, jnp.arange(EXPERTS, dtype=jnp.int32)))
    return (stream.astype(jnp.float32) + routed + shared).astype(jnp.bfloat16)
```

```python
import functools

import jax
import jax.numpy as jnp
from jax import lax
from jax.experimental import pallas as pl
from jax.experimental.pallas import tpu as pltpu
from jax.sharding import PartitionSpec as P

F32 = jnp.float32
BF16 = jnp.bfloat16
VMEM_BYTES = 48 * 1024 * 1024
TILE = 256


def ring_order(chips):
    slow = 4
    fast = chips // slow
    order = [a * fast for a in range(slow)]
    for turn, a in enumerate(reversed(range(slow))):
        inner = range(1, fast) if turn % 2 == 0 else range(fast - 1, 0, -1)
        order += [a * fast + b for b in inner]
    return order


def mm(a, b):
    return jnp.dot(a, b, preferred_element_type=F32)


def vmem():
    return pl.BlockSpec(memory_space=pltpu.VMEM)


def smem():
    return pl.BlockSpec(memory_space=pltpu.SMEM)


def hbm():
    return pl.BlockSpec(memory_space=pl.ANY)


def params():
    return pltpu.CompilerParams(vmem_limit_bytes=VMEM_BYTES)


def proj_kernel(depth, blocks, final, where_ref, attn_ref, *refs):
    total = None
    at = 0
    for slot, pieces in blocks:
        start = pl.multiple_of(where_ref[slot] * depth, 128)
        columns = attn_ref[:, pl.ds(start, depth)]
        parts = [refs[at + i][...] for i in range(pieces)]
        at += pieces
        weight = parts[0] if pieces == 1 else jnp.concatenate(parts, axis=0)
        term = mm(columns, weight)
        total = term if total is None else total + term
    if final:
        acc_ref, residual_ref, out_ref = refs[at:]
        total = total + acc_ref[...]
        out_ref[...] = (residual_ref[...].astype(F32) + total).astype(BF16)
    else:
        refs[at][...] = total


def proj(depth, blocks, where, attn, weights, acc=None, residual=None):
    final = acc is not None
    rows, half = attn.shape[0], weights[0].shape[1]
    extra = [acc, residual] if final else []
    operands = [where, attn] + weights + extra
    return pl.pallas_call(
        functools.partial(proj_kernel, depth, blocks, final),
        out_shape=jax.ShapeDtypeStruct((rows, half), BF16 if final else F32),
        in_specs=[smem()] + [vmem()] * (len(operands) - 1),
        out_specs=vmem(),
        compiler_params=params(),
        cost_estimate=pl.CostEstimate(
            flops=2 * rows * half * depth * len(blocks),
            bytes_accessed=2 * half * depth * len(blocks) + 8 * rows * half,
            transcendentals=0,
        ),
        name="proj_final" if final else "proj_part",
    )(*operands)


def expert_kernel(pieces, core_ref, gain_ref, pick_ref, put_ref, factor_ref, gate_hbm, up_hbm, down_hbm, *refs):
    blocks, slots, rows = pick_ref.shape
    own = rows // 2
    width = gain_ref.shape[1]
    half = width // 2
    hidden_units = gate_hbm.shape[2]
    inputs = refs[: 2 * pieces * blocks]
    outs = refs[2 * pieces * blocks : 2 * pieces * blocks + 2 * blocks]
    gate_buf, up_buf, down_buf, split, normed, hidden, in_sem, down_sem = refs[2 * pieces * blocks + 2 * blocks :]
    full = hidden_units // TILE
    tail = hidden_units - full * TILE
    steps = [(t * TILE, TILE) for t in range(full)] + ([(full * TILE, tail)] if tail else [])

    def in_copies(start, size, index):
        columns = pl.ds(start, size)
        return (
            pltpu.make_async_copy(gate_hbm.at[0, :, columns], gate_buf.at[:, columns], in_sem.at[0, index]),
            pltpu.make_async_copy(up_hbm.at[0, :, columns], up_buf.at[:, columns], in_sem.at[1, index]),
        )

    def down_copy(start, index):
        columns = pl.ds(start, TILE)
        return pltpu.make_async_copy(down_hbm.at[0, :, columns], down_buf.at[:, columns], down_sem.at[index])

    for index, (start, size) in enumerate(steps):
        for copy in in_copies(start, size, index):
            copy.start()
    for index in range(width // TILE):
        down_copy(index * TILE, index).start()

    core = core_ref[0]
    for b in range(blocks):
        pick = pick_ref[b]
        swapped = jnp.concatenate([pick[:, own:], pick[:, :own]], axis=1)
        for which, matrix in enumerate((pick, swapped)):
            parts = [inputs[(2 * b + which) * pieces + i][...] for i in range(pieces)]
            block = parts[0] if pieces == 1 else jnp.concatenate(parts, axis=0)
            place = core if which == 0 else 1 - core
            split[place, b * slots : (b + 1) * slots, :] = mm(matrix, block)
    left, right = split[0], split[1]
    square = jnp.sum(left * left, axis=1, keepdims=True) + jnp.sum(right * right, axis=1, keepdims=True)
    scale = lax.rsqrt(square * (1.0 / width) + 1e-06)
    normed[:, :half] = (left * scale * gain_ref[:, :half]).astype(BF16)
    normed[:, half:] = (right * scale * gain_ref[:, half:]).astype(BF16)

    def hidden_tile(start, size, index):
        for copy in in_copies(start, size, index):
            copy.wait()
        columns = pl.ds(start, size)
        gate_part = mm(normed[...], gate_buf[:, columns])
        up_part = mm(normed[...], up_buf[:, columns])
        hidden[:, columns] = (jax.nn.silu(gate_part) * up_part).astype(BF16)

    @pl.loop(0, full)
    def _(t):
        hidden_tile(pl.multiple_of(t * TILE, TILE), TILE, t)

    if tail:
        hidden_tile(full * TILE, tail, full)

    @pl.loop(0, width // TILE)
    def _(t):
        start = pl.multiple_of(t * TILE, TILE)
        down_copy(start, t).wait()
        columns = pl.ds(start, TILE)
        result = mm(hidden[...], down_buf[:, columns])
        for b in range(blocks):
            weighted = (result[b * slots : (b + 1) * slots] * factor_ref[b]).astype(BF16)
            placed = mm(put_ref[b], weighted).astype(BF16)
            outs[2 * b][:, columns] = placed[:own]
            outs[2 * b + 1][:, columns] = placed[own:]


def expert(first, blocks, pieces, core, gain, pick, put, factor, gate, up, down, inputs):
    slots, rows = pick.shape[1:]
    width, hidden_units = gate.shape[1:]
    own = rows // 2
    m = blocks * slots
    index = first // blocks
    tables = [
        pl.BlockSpec((blocks, slots, rows), lambda i: (index, 0, 0)),
        pl.BlockSpec((blocks, rows, slots), lambda i: (index, 0, 0)),
        pl.BlockSpec((blocks, slots, 1), lambda i: (index, 0, 0)),
    ]
    in_tiles = -(-hidden_units // TILE)
    return pl.pallas_call(
        functools.partial(expert_kernel, pieces),
        grid=(1,),
        out_shape=[jax.ShapeDtypeStruct((own, width), BF16)] * (2 * blocks),
        in_specs=[smem(), vmem()] + tables + [hbm()] * 3 + [vmem()] * len(inputs),
        out_specs=[vmem()] * (2 * blocks),
        scratch_shapes=[
            pltpu.VMEM((width, hidden_units), BF16),
            pltpu.VMEM((width, hidden_units), BF16),
            pltpu.VMEM((hidden_units, width), BF16),
            pltpu.VMEM((2, m, width // 2), F32),
            pltpu.VMEM((m, width), BF16),
            pltpu.VMEM((m, hidden_units), BF16),
            pltpu.SemaphoreType.DMA((2, in_tiles)),
            pltpu.SemaphoreType.DMA((width // TILE,)),
        ],
        compiler_params=params(),
        cost_estimate=pl.CostEstimate(
            flops=6 * m * width * hidden_units,
            bytes_accessed=6 * width * hidden_units + 8 * blocks * rows * width,
            transcendentals=m * hidden_units,
        ),
        name="expert",
    )(core, gain, pick, put, factor, gate, up, down, *inputs)


def body(
    req_size,
    exp_size,
    attn_out,
    residual,
    out_weight,
    norm_gain,
    expert_ids,
    gate_weights,
    expert_gate,
    expert_up,
    expert_down,
    shared_gate,
    shared_up,
    shared_down,
):
    rows, width = attn_out.shape
    half = width // 2
    topk = expert_ids.shape[1]
    wrows = out_weight.shape[0]
    capacity = min(rows, 3 * rows * topk // (2 * exp_size))
    slots = -(-2 * capacity // 16) * 16
    chips = exp_size // 2
    depth = chips // 2
    order = ring_order(chips)
    me = lax.axis_index("exp")
    core = me % 2
    chip = me // 2
    position = jnp.asarray([order.index(q) for q in range(chips)], jnp.int32)[chip]
    offsets = [0, depth]
    for k in range(1, depth):
        offsets += [-k, k]
    chip_at = jnp.asarray(order, jnp.int32)[(position + jnp.asarray(offsets, jnp.int32)) % chips]

    ahead = [(2 * order[i] + c, 2 * order[(i + 1) % chips] + c) for i in range(chips) for c in range(2)]
    behind = [(b, a) for a, b in ahead]
    cores = [(d, d ^ 1) for d in range(exp_size)]

    def to_ahead(x):
        return lax.ppermute(x, "exp", ahead)

    def to_behind(x):
        return lax.ppermute(x, "exp", behind)

    def to_core(x):
        return lax.ppermute(x, "exp", cores)

    def columns(x, which):
        return lax.dynamic_slice_in_dim(x, which * half, half, axis=1)

    weight_sent = to_core(columns(out_weight, 1 - core))
    weight_own = columns(out_weight, core)
    weight = jnp.where(
        core == 0,
        jnp.concatenate([weight_own, weight_sent], axis=0),
        jnp.concatenate([weight_sent, weight_own], axis=0),
    )
    attn = jnp.concatenate([attn_out, to_core(attn_out)], axis=0)
    res = jnp.concatenate([columns(residual, core), to_core(columns(residual, 1 - core))], axis=0)

    def ring(block):
        pairs = []
        low = high = block
        for _ in range(1, depth):
            low, high = to_ahead(low), to_behind(high)
            pairs.append((low, high))
        cut = block.shape[0] // 2
        return pairs, (to_ahead(low[:cut]), to_behind(high[cut:]))

    pairs, last = ring(weight)
    early = [weight] + [w for pair in pairs[:-1] for w in pair]
    early_slots = [(0, 1)] + [(2 * k + i, 1) for k in range(1, depth - 1) for i in range(2)]
    late = list(pairs[-1]) + list(last)
    late_slots = [(2 * depth - 2, 1), (2 * depth - 1, 1), (1, 2)]
    acc = proj(2 * wrows, early_slots, chip_at, attn, early)
    stream = proj(2 * wrows, late_slots, chip_at, attn, late, acc, res)

    named = jnp.concatenate([expert_ids.astype(F32), gate_weights], axis=1)
    everyone = lax.all_gather(named, "exp", axis=0)
    device_at = jnp.stack([2 * chip_at + core, 2 * chip_at + 1 - core], axis=1)
    ordered = everyone[device_at].reshape(chips, 2 * rows, 2 * topk)
    hit = ordered[..., :topk] == me.astype(F32)
    selected = jnp.any(hit, axis=-1)
    factor = jnp.sum(jnp.where(hit, ordered[..., topk:], 0.0), axis=-1)
    slot = jnp.where(selected, jnp.cumsum(selected.astype(jnp.int32), axis=1) - 1, -1)
    numbers = jnp.arange(slots, dtype=jnp.int32)
    chosen = slot[:, None, :] == numbers[None, :, None]
    pick = chosen.astype(BF16)
    put = (slot[:, :, None] == numbers[None, None, :]).astype(BF16)
    slot_factor = jnp.sum(jnp.where(chosen, factor[:, None, :], 0.0), axis=2)[..., None]

    core_arg = core.astype(jnp.int32).reshape(1)
    gain = norm_gain.reshape(1, width)

    def run_expert(first, blocks, pieces, inputs):
        return expert(
            first, blocks, pieces, core_arg, gain, pick, put, slot_factor, expert_gate, expert_up, expert_down, inputs
        )

    stream_other = to_core(stream)
    pairs, last = ring(stream)
    own_left = stream[:rows]
    own_right = stream_other[rows:]
    own_rows = jnp.where(
        core == 0,
        jnp.concatenate([own_left, own_right], axis=1),
        jnp.concatenate([own_right, own_left], axis=1),
    )
    results = {0: run_expert(0, 1, 1, [stream, stream_other])}
    for k in range(1, depth):
        low, high = pairs[k - 1]
        results[k] = run_expert(2 * k, 2, 1, [low, to_core(low), high, to_core(high)])
    results[depth] = run_expert(1, 1, 2, list(last) + [to_core(x) for x in last])

    def shared_part(x):
        xf = x.astype(F32)
        scale = lax.rsqrt(jnp.mean(xf * xf, axis=1, keepdims=True) + 1e-06)
        n = (xf * scale * norm_gain).astype(BF16)
        h = (jax.nn.silu(mm(n, shared_gate)) * mm(n, shared_up)).astype(BF16)
        return lax.dot_general(h, shared_down, (((1,), (1,)), ((), ())), preferred_element_type=F32)

    visits = [own_rows]
    for shift in range(1, req_size):
        visits.append(lax.ppermute(own_rows, "req", [(i, (i + shift) % req_size) for i in range(req_size)]))
    shared = shared_part(jnp.concatenate(visits, axis=0))
    base = own_rows.astype(F32) + shared[:rows]
    for shift in range(1, req_size):
        part = shared[shift * rows : (shift + 1) * rows].astype(BF16)
        back = lax.ppermute(part, "req", [((i + shift) % req_size, i) for i in range(req_size)])
        base = base + back.astype(F32)

    def chip_sum(mine, theirs):
        return mine.astype(F32) + to_core(theirs).astype(F32)

    far = chip_sum(*results[depth]).astype(BF16)
    cut = rows // 2
    up_part = to_ahead(far[:cut])
    down_part = to_behind(far[cut:])
    for k in range(depth - 1, 0, -1):
        low_mine, low_theirs, high_mine, high_theirs = results[k]
        to_high = chip_sum(high_mine, high_theirs)
        to_low = chip_sum(low_mine, low_theirs)
        if k == depth - 1:
            to_high = jnp.concatenate([to_high[:cut] + up_part.astype(F32), to_high[cut:]], axis=0)
            to_low = jnp.concatenate([to_low[:cut], to_low[cut:] + down_part.astype(F32)], axis=0)
        else:
            to_high = to_high + up_part.astype(F32)
            to_low = to_low + down_part.astype(F32)
        up_part = to_ahead(to_high.astype(BF16))
        down_part = to_behind(to_low.astype(BF16))
    routed = chip_sum(*results[0]) + up_part.astype(F32) + down_part.astype(F32)
    return (base + routed).astype(BF16)


def solution(mesh):
    return jax.shard_map(
        functools.partial(body, mesh.shape["req"], mesh.shape["exp"]),
        mesh=mesh,
        in_specs=(
            P(("req", "exp"), None),
            P(("req", "exp"), None),
            P("exp", None),
            P(),
            P(("req", "exp"), None),
            P(("req", "exp"), None),
            P("exp", None, None),
            P("exp", None, None),
            P("exp", None, None),
            P(None, "req"),
            P(None, "req"),
            P(None, "req"),
        ),
        out_specs=P(("req", "exp"), None),
        check_vma=False,
    )
```

```python
import functools

import jax
import jax.numpy as jnp
from jax import lax
from jax.experimental import pallas as pl
from jax.experimental.pallas import tpu as pltpu
from jax.sharding import PartitionSpec as P

F32 = jnp.float32
BF16 = jnp.bfloat16
VMEM_BYTES = 20 * 1024 * 1024
TILE = 256


def ring_order(chips):
    slow = 4
    fast = chips // slow
    order = [a * fast for a in range(slow)]
    for turn, a in enumerate(reversed(range(slow))):
        inner = range(1, fast) if turn % 2 == 0 else range(fast - 1, 0, -1)
        order += [a * fast + b for b in inner]
    return order


def mm(a, b):
    return jnp.dot(a, b, preferred_element_type=F32)


def vmem():
    return pl.BlockSpec(memory_space=pltpu.VMEM)


def smem():
    return pl.BlockSpec(memory_space=pltpu.SMEM)


def params():
    return pltpu.CompilerParams(vmem_limit_bytes=VMEM_BYTES)


def proj_kernel(depth, blocks, final, where_ref, attn_ref, *refs):
    total = None
    at = 0
    for slot, pieces in blocks:
        start = pl.multiple_of(where_ref[slot] * depth, 128)
        columns = attn_ref[:, pl.ds(start, depth)]
        parts = [refs[at + i][...] for i in range(pieces)]
        at += pieces
        weight = parts[0] if pieces == 1 else jnp.concatenate(parts, axis=0)
        term = mm(columns, weight)
        total = term if total is None else total + term
    if final:
        acc_ref, residual_ref, out_ref = refs[at:]
        total = total + acc_ref[...]
        out_ref[...] = (residual_ref[...].astype(F32) + total).astype(BF16)
    else:
        refs[at][...] = total


def proj(depth, blocks, where, attn, weights, acc=None, residual=None):
    final = acc is not None
    rows, half = attn.shape[0], weights[0].shape[1]
    extra = [acc, residual] if final else []
    operands = [where, attn] + weights + extra
    return pl.pallas_call(
        functools.partial(proj_kernel, depth, blocks, final),
        out_shape=jax.ShapeDtypeStruct((rows, half), BF16 if final else F32),
        in_specs=[smem()] + [vmem()] * (len(operands) - 1),
        out_specs=vmem(),
        compiler_params=params(),
        cost_estimate=pl.CostEstimate(
            flops=2 * rows * half * depth * len(blocks),
            bytes_accessed=2 * half * depth * len(blocks) + 8 * rows * half,
            transcendentals=0,
        ),
        name="proj_final" if final else "proj_part",
    )(*operands)


def tables_kernel(slots, topk, where_ref, named_ref, pick_ref, put_ref, factor_ref):
    rows = named_ref.shape[2]
    both = 2 * rows
    expert_id = where_ref[0].astype(F32)
    row_of = lax.broadcasted_iota(jnp.int32, (both, both), 0)
    row_at = lax.broadcasted_iota(jnp.int32, (both, both), 1)
    slot_of = lax.broadcasted_iota(jnp.int32, (slots, both), 0).astype(F32)
    slot_at = lax.broadcasted_iota(jnp.int32, (both, slots), 1).astype(F32)
    for block in range(pick_ref.shape[0]):
        parts = [named_ref[where_ref[1 + 2 * block + i]] for i in range(2)]
        hits = [p[:topk] == expert_id for p in parts]
        picked = [jnp.sum(h.astype(F32), axis=0, keepdims=True) for h in hits]
        chosen = [jnp.sum(jnp.where(h, p[topk : 2 * topk], 0.0), axis=0, keepdims=True) for h, p in zip(hits, parts)]
        selected = jnp.concatenate(picked, axis=1)
        factor = jnp.concatenate(chosen, axis=1)
        spread = jnp.broadcast_to(selected, (both, both))
        before = jnp.sum(jnp.where(row_at < row_of, spread, 0.0), axis=1, keepdims=True)
        selected_down = jnp.sum(jnp.where(row_at == row_of, spread, 0.0), axis=1, keepdims=True)
        slot_down = jnp.where(selected_down > 0.0, before, -1.0)
        put_ref[block] = (slot_at == slot_down).astype(F32).astype(BF16)
        slot = jnp.sum(jnp.where(row_at == row_of, jnp.broadcast_to(slot_down, (both, both)), 0.0), axis=0, keepdims=True)
        taken = slot_of == slot
        pick_ref[block] = taken.astype(F32).astype(BF16)
        factor_ref[block] = jnp.sum(jnp.where(taken, factor, 0.0), axis=1, keepdims=True)


def tables(chips, slots, topk, where, named):
    both = 2 * named.shape[2]
    return pl.pallas_call(
        functools.partial(tables_kernel, slots, topk),
        out_shape=[
            jax.ShapeDtypeStruct((chips, slots, both), BF16),
            jax.ShapeDtypeStruct((chips, both, slots), BF16),
            jax.ShapeDtypeStruct((chips, slots, 1), F32),
        ],
        in_specs=[smem(), vmem()],
        out_specs=[vmem()] * 3,
        compiler_params=params(),
        cost_estimate=pl.CostEstimate(flops=0, bytes_accessed=8 * chips * slots * both, transcendentals=0),
        name="tables",
    )(where, named)


def expert_kernel(first, pieces, merged, gain_ref, pick_ref, put_ref, factor_ref, gate_ref, up_ref, down_ref, *refs):
    blocks = sum(1 for _ in pieces)
    slots = pick_ref.shape[1]
    width = gain_ref.shape[1]
    hidden_units = gate_ref.shape[1]
    count = sum(pieces)
    inputs = refs[:count]
    outs = refs[count:-2]
    normed, hidden = refs[-2:]
    full = hidden_units // TILE
    tail = hidden_units - full * TILE

    at = 0
    for b in range(blocks):
        parts = [inputs[at + i][...] for i in range(pieces[b])]
        at += pieces[b]
        block = parts[0] if len(parts) == 1 else jnp.concatenate(parts, axis=0)
        taken = mm(pick_ref[first + b], block)
        scale = lax.rsqrt(jnp.sum(taken * taken, axis=1, keepdims=True) * (1.0 / width) + 1e-06)
        normed[b * slots : (b + 1) * slots, :] = (taken * scale * gain_ref[...]).astype(BF16)

    def hidden_tile(columns):
        gate_part = mm(normed[...], gate_ref[:, columns])
        up_part = mm(normed[...], up_ref[:, columns])
        hidden[:, columns] = (jax.nn.silu(gate_part) * up_part).astype(BF16)

    @pl.loop(0, full)
    def _(t):
        hidden_tile(pl.ds(pl.multiple_of(t * TILE, TILE), TILE))

    if tail:
        hidden_tile(pl.ds(full * TILE, tail))

    @pl.loop(0, width // TILE)
    def _(t):
        columns = pl.ds(pl.multiple_of(t * TILE, TILE), TILE)
        result = mm(hidden[...], down_ref[:, columns])
        for b in range(blocks):
            weighted = (result[b * slots : (b + 1) * slots] * factor_ref[first + b]).astype(BF16)
            placed = mm(put_ref[first + b], weighted).astype(BF16)
            if merged:
                outs[b][:, columns] = placed
            else:
                own = placed.shape[0] // 2
                outs[0][:, columns] = placed[:own]
                outs[1][:, columns] = placed[own:]


def expert(first, pieces, merged, tabs, gain, weights, inputs):
    slots, rows = tabs[0].shape[1:]
    width, hidden_units = weights[0].shape
    m = len(pieces) * slots
    shape = jax.ShapeDtypeStruct((rows if merged else rows // 2, width), BF16)
    outs = len(pieces) if merged else 2
    weights = [pltpu.with_memory_space_constraint(w, pltpu.VMEM) for w in weights]
    return pl.pallas_call(
        functools.partial(expert_kernel, first, pieces, merged),
        out_shape=[shape] * outs,
        in_specs=[vmem()] * (7 + len(inputs)),
        out_specs=[vmem()] * outs,
        scratch_shapes=[
            pltpu.VMEM((m, width), BF16),
            pltpu.VMEM((m, hidden_units), BF16),
        ],
        compiler_params=params(),
        cost_estimate=pl.CostEstimate(
            flops=6 * m * width * hidden_units,
            bytes_accessed=8 * len(pieces) * rows * width,
            transcendentals=m * hidden_units,
        ),
        name="expert",
    )(gain, *tabs, *weights, *inputs)


def body(
    req_size,
    exp_size,
    attn_out,
    residual,
    out_weight,
    norm_gain,
    expert_ids,
    gate_weights,
    expert_gate,
    expert_up,
    expert_down,
    shared_gate,
    shared_up,
    shared_down,
):
    rows, width = attn_out.shape
    half = width // 2
    topk = expert_ids.shape[1]
    wrows = out_weight.shape[0]
    capacity = min(rows, 3 * rows * topk // (2 * exp_size))
    slots = -(-2 * capacity // 16) * 16
    chips = exp_size // 2
    depth = chips // 2
    order = ring_order(chips)
    me = lax.axis_index("exp")
    core = me % 2
    first_core = core == 0
    position = jnp.asarray([order.index(q) for q in range(chips)], jnp.int32)[me // 2]
    offsets = [0, depth]
    for k in range(1, depth):
        offsets += [-k, k]
    offsets = jnp.asarray(offsets, jnp.int32)
    ringed = jnp.asarray(order, jnp.int32)
    weight_at = ringed[(position + offsets) % chips]
    chip_at = ringed[(position + jnp.where(first_core, offsets, -offsets)) % chips]

    steps = [(order[i], order[(i + 1) % chips]) for i in range(chips)]
    ahead = [(2 * a + c, 2 * b + c) for a, b in steps for c in range(2)]
    behind = [(b, a) for a, b in ahead]
    split = [(2 * a, 2 * b) for a, b in steps] + [(2 * b + 1, 2 * a + 1) for a, b in steps]

    def to_ahead(x):
        return lax.ppermute(x, "exp", ahead)

    def to_behind(x):
        return lax.ppermute(x, "exp", behind)

    def onward(x):
        return lax.ppermute(x, "exp", split)

    def to_core(x):
        return lax.ppermute(x, "exp", [(d, d ^ 1) for d in range(exp_size)])

    def columns(x, which):
        return lax.dynamic_slice_in_dim(x, which * half, half, axis=1)

    def rows_of(x, which):
        return lax.dynamic_slice_in_dim(x, which * rows, rows, axis=0)

    def by_core(mine, other, axis):
        return jnp.where(
            first_core, jnp.concatenate([mine, other], axis=axis), jnp.concatenate([other, mine], axis=axis)
        )

    weight = by_core(columns(out_weight, core), to_core(columns(out_weight, 1 - core)), 0)
    low = high = weight
    pairs = []
    for _ in range(1, depth):
        low, high = to_ahead(low), to_behind(high)
        pairs.append((low, high))
    last = [to_ahead(low[:wrows]), to_behind(high[wrows:])]
    attn = by_core(attn_out, to_core(attn_out), 0)
    res = by_core(columns(residual, core), to_core(columns(residual, 1 - core)), 0)
    early = [weight] + [w for pair in pairs[:-1] for w in pair]
    early_slots = [(0, 1)] + [(2 * k + i, 1) for k in range(1, depth - 1) for i in range(2)]
    late = list(pairs[-1]) + last
    late_slots = [(2 * depth - 2, 1), (2 * depth - 1, 1), (1, 2)]
    named = jnp.concatenate([expert_ids.astype(F32).T, gate_weights.T], axis=0)
    named = jnp.pad(named, ((0, -(2 * topk) % 8), (0, 0)))[None]
    distance = 1
    while distance < exp_size:
        far = lax.ppermute(named, "exp", [(d, d ^ distance) for d in range(exp_size)])
        named = jnp.concatenate([named, far], axis=0)
        distance *= 2
    device_at = jnp.stack([2 * chip_at, 2 * chip_at + 1], axis=1)
    device_at = device_at.at[1].set(2 * chip_at[1] + jnp.stack([core, 1 - core]))
    where = jnp.concatenate([me.reshape(1), (device_at ^ me).reshape(-1)]).astype(jnp.int32)
    tabs = tables(chips, slots, topk, where, named)

    tabs, weight_at = lax.optimization_barrier((tabs, weight_at))
    acc = proj(2 * wrows, early_slots, weight_at, attn, early)
    stream_half = proj(2 * wrows, late_slots, weight_at, attn, late, acc, res)

    gain = norm_gain.reshape(1, width)
    weights = [expert_gate[0], expert_up[0], expert_down[0]]

    stream = by_core(stream_half, to_core(stream_half), 1)
    own_rows = rows_of(stream, core)
    visits = [own_rows]
    for shift in range(1, req_size):
        visits.append(lax.ppermute(own_rows, "req", [(i, (i + shift) % req_size) for i in range(req_size)]))
    results = {0: expert(0, [1], True, tabs, gain, weights, [stream])}
    block = onward(stream)
    for k in range(1, depth):
        block, results[k - 1] = lax.optimization_barrier((block, results[k - 1]))
        other = to_core(block)
        results[k] = expert(2 * k, [1, 1], True, tabs, gain, weights, [block, other])
        block = onward(block if k < depth - 1 else rows_of(block, core))
    tip = block

    def shared_part(x):
        xf = x.astype(F32)
        scale = lax.rsqrt(jnp.mean(xf * xf, axis=1, keepdims=True) + 1e-06)
        n = (xf * scale * norm_gain).astype(BF16)
        h = (jax.nn.silu(mm(n, shared_gate)) * mm(n, shared_up)).astype(BF16)
        return lax.dot_general(h, shared_down, (((1,), (1,)), ((), ())), preferred_element_type=F32)

    shared = shared_part(jnp.concatenate(visits, axis=0))
    gain, shared = lax.optimization_barrier((gain, shared))
    base = own_rows.astype(F32) + shared[:rows]
    for shift in range(1, req_size):
        part = shared[shift * rows : (shift + 1) * rows].astype(BF16)
        back = lax.ppermute(part, "req", [((i + shift) % req_size, i) for i in range(req_size)])
        base = base + back.astype(F32)
    results[depth] = expert(1, [2], False, tabs, gain, weights, [tip, to_core(tip)])

    mine, theirs = results[depth]
    moving = onward((mine.astype(F32) + to_core(theirs).astype(F32)).astype(BF16))
    for k in range(depth - 1, 0, -1):
        theirs, mine = results[k]
        total = mine.astype(F32) + to_core(theirs).astype(F32)
        if k == depth - 1:
            moving = by_core(moving, jnp.zeros_like(moving), 0)
        if k == 1:
            moving, base = lax.optimization_barrier((moving, base))
        moving = onward((total + moving.astype(F32)).astype(BF16))
    total = results[0][0].astype(F32) + moving.astype(F32)
    routed = rows_of(total, core) + to_core(rows_of(total, 1 - core).astype(BF16)).astype(F32)
    return (base + routed).astype(BF16)


def solution(mesh):
    return jax.shard_map(
        functools.partial(body, mesh.shape["req"], mesh.shape["exp"]),
        mesh=mesh,
        in_specs=(
            P(("req", "exp"), None),
            P(("req", "exp"), None),
            P("exp", None),
            P(),
            P(("req", "exp"), None),
            P(("req", "exp"), None),
            P("exp", None, None),
            P("exp", None, None),
            P("exp", None, None),
            P(None, "req"),
            P(None, "req"),
            P(None, "req"),
        ),
        out_specs=P(("req", "exp"), None),
        check_vma=False,
    )
```

```python
import functools

import jax
import jax.numpy as jnp
from jax import lax
from jax.experimental import pallas as pl
from jax.experimental.pallas import tpu as pltpu
from jax.sharding import PartitionSpec as P

F32 = jnp.float32
BF16 = jnp.bfloat16
VMEM_BYTES = 12 * 1024 * 1024
TILE = 512
TABLE_ROWS = 16


def ring_order(chips):
    slow = 4
    fast = chips // slow
    order = [a * fast for a in range(slow)]
    for turn, a in enumerate(reversed(range(slow))):
        inner = range(1, fast) if turn % 2 == 0 else range(fast - 1, 0, -1)
        order += [a * fast + b for b in inner]
    return order


def mm(a, b):
    return jnp.dot(a, b, preferred_element_type=F32)


def vmem():
    return pl.BlockSpec(memory_space=pltpu.VMEM)


def smem():
    return pl.BlockSpec(memory_space=pltpu.SMEM)


def params():
    return pltpu.CompilerParams(vmem_limit_bytes=VMEM_BYTES)


def prepare_kernel(part, where_ref, ids_ref, factors_ref, weight_ref, own_ref, sent_ref):
    wrows, width = weight_ref.shape
    topk, rows = ids_ref.shape
    core, request = where_ref[1], where_ref[2]
    per_row = part // rows
    factors = factors_ref[...]
    big = factors.astype(BF16).astype(F32)
    middle = (factors - big).astype(BF16).astype(F32)
    named = (ids_ref[...].astype(F32), big, middle, factors - big - middle)
    items = [kind[k : k + 1] for kind in named for k in range(topk)]
    items += [jnp.zeros((1, rows), F32)] * (-len(items) % per_row)
    lines = [jnp.concatenate(items[i : i + per_row], axis=1) for i in range(0, len(items), per_row)]
    lines.append(jnp.zeros((TABLE_ROWS - len(lines), part), F32))
    table = jnp.concatenate(lines, axis=0).astype(BF16)
    for ref, which in ((own_ref, core), (sent_ref, 1 - core)):
        start = pl.multiple_of(which * (width // 2) + request * part, 128)
        ref[:wrows] = weight_ref[:, pl.ds(start, part)]
        ref[wrows:] = table


def prepare(part, where, ids, factors, weight):
    shape = jax.ShapeDtypeStruct((weight.shape[0] + TABLE_ROWS, part), BF16)
    return pl.pallas_call(
        functools.partial(prepare_kernel, part),
        out_shape=[shape] * 2,
        in_specs=[smem()] + [vmem()] * 3,
        out_specs=[vmem()] * 2,
        compiler_params=params(),
        cost_estimate=pl.CostEstimate(flops=0, bytes_accessed=2 * weight.size, transcendentals=0),
        name="prepare",
    )(where, ids, factors, weight)


def proj_kernel(wrows, part, blocks, visits, final, where_ref, *refs):
    total = None
    rows_refs = refs[:visits]
    width = rows_refs[0].shape[1] - 2 * part
    at = visits
    for slot, pieces in blocks:
        start = pl.multiple_of(where_ref[3 + slot] * 2 * wrows, 128)
        columns = jnp.concatenate([r[:, pl.ds(start, 2 * wrows)] for r in rows_refs], axis=0)
        step = wrows + TABLE_ROWS
        if pieces == 1:
            parts = [refs[at][i * step : i * step + wrows] for i in range(2)]
        else:
            parts = [refs[at + i][:wrows] for i in range(2)]
        at += pieces
        term = mm(columns, jnp.concatenate(parts, axis=0))
        total = term if total is None else total + term
    if final:
        total = total + refs[at][...]
        start = pl.multiple_of(width + where_ref[1] * part, 128)
        rows = rows_refs[0].shape[0]
        for i, out_ref in enumerate(refs[at + 1 :]):
            residual = rows_refs[i][:, pl.ds(start, part)].astype(F32)
            out_ref[...] = (residual + total[i * rows : (i + 1) * rows]).astype(BF16)
    else:
        refs[at][...] = total


def proj(wrows, blocks, where, visits, weights, acc=None):
    final = acc is not None
    rows, part = visits[0].shape[0], weights[0].shape[1]
    operands = [where] + visits + weights + ([acc] if final else [])
    count = len(visits)
    if final:
        outs = [jax.ShapeDtypeStruct((rows, part), BF16)] * count
    else:
        outs = [jax.ShapeDtypeStruct((rows * count, part), F32)]
    return pl.pallas_call(
        functools.partial(proj_kernel, wrows, part, blocks, count, final),
        out_shape=outs,
        in_specs=[smem()] + [vmem()] * (len(operands) - 1),
        out_specs=[vmem()] * len(outs),
        compiler_params=params(),
        cost_estimate=pl.CostEstimate(
            flops=8 * rows * count * part * wrows * len(blocks),
            bytes_accessed=4 * part * wrows * len(blocks) + 8 * rows * count * part,
            transcendentals=0,
        ),
        name="proj_final" if final else "proj_part",
    )(*operands)


def tables_kernel(wrows, slots, topk, rows, pieces, where_ref, *refs):
    pick_ref, put_ref, factor_ref = refs[-3:]
    both = 2 * rows
    expert_id = where_ref[0].astype(F32)
    first_core = where_ref[1] == 0
    row_of = lax.broadcasted_iota(jnp.int32, (both, both), 0)
    row_at = lax.broadcasted_iota(jnp.int32, (both, both), 1)
    slot_of = lax.broadcasted_iota(jnp.int32, (slots, both), 0).astype(F32)
    slot_at = lax.broadcasted_iota(jnp.int32, (both, slots), 1).astype(F32)
    step = wrows + TABLE_ROWS
    at = 0
    for block in range(pick_ref.shape[0]):
        if pieces[block] == 1:
            named = [refs[at][i * step + wrows : (i + 1) * step] for i in range(2)]
        else:
            named = [refs[at + i][wrows:] for i in range(2)]
        at += pieces[block]
        named = [n.astype(F32) for n in named]
        ordered = [jnp.where(first_core, named[0], named[1]), jnp.where(first_core, named[1], named[0])]
        per_row = named[0].shape[1] // rows
        selected, factor = [], []
        for n in ordered:
            item = [n[i // per_row : i // per_row + 1, (i % per_row) * rows : (i % per_row + 1) * rows] for i in range(4 * topk)]
            hits = [item[k] == expert_id for k in range(topk)]
            values = [item[topk + k] + item[2 * topk + k] + item[3 * topk + k] for k in range(topk)]
            selected.append(sum(h.astype(F32) for h in hits))
            factor.append(sum(jnp.where(h, v, 0.0) for h, v in zip(hits, values)))
        selected = jnp.concatenate(selected, axis=1)
        factor = jnp.concatenate(factor, axis=1)
        spread = jnp.broadcast_to(selected, (both, both))
        before = jnp.sum(jnp.where(row_at < row_of, spread, 0.0), axis=1, keepdims=True)
        selected_down = jnp.sum(jnp.where(row_at == row_of, spread, 0.0), axis=1, keepdims=True)
        slot_down = jnp.where(selected_down > 0.0, before, -1.0)
        put_ref[block] = (slot_at == slot_down).astype(F32).astype(BF16)
        slot = jnp.sum(jnp.where(row_at == row_of, jnp.broadcast_to(slot_down, (both, both)), 0.0), axis=0, keepdims=True)
        taken = slot_of == slot
        pick_ref[block] = taken.astype(F32).astype(BF16)
        factor_ref[block] = jnp.sum(jnp.where(taken, factor, 0.0), axis=1, keepdims=True)


def tables(wrows, slots, topk, rows, where, pieces, blocks):
    chips = len(pieces)
    both = 2 * rows
    return pl.pallas_call(
        functools.partial(tables_kernel, wrows, slots, topk, rows, pieces),
        out_shape=[
            jax.ShapeDtypeStruct((chips, slots, both), BF16),
            jax.ShapeDtypeStruct((chips, both, slots), BF16),
            jax.ShapeDtypeStruct((chips, slots, 1), F32),
        ],
        in_specs=[smem()] + [vmem()] * len(blocks),
        out_specs=[vmem()] * 3,
        compiler_params=params(),
        cost_estimate=pl.CostEstimate(flops=0, bytes_accessed=8 * chips * slots * both, transcendentals=0),
        name="tables",
    )(where, *blocks)


def expert_kernel(first, blocks, pieces, gain_ref, pick_ref, put_ref, factor_ref, gate_ref, up_ref, down_ref, *refs):
    slots, rows = pick_ref.shape[1:]
    own = rows // 2
    width = gain_ref.shape[1]
    hidden_units = gate_ref.shape[1]
    inputs = refs[: blocks * pieces]
    mine = refs[blocks * pieces : blocks * pieces + blocks]
    theirs, normed, hidden = refs[-3:]

    for b in range(blocks):
        block = jnp.concatenate([inputs[b * pieces + i][...] for i in range(pieces)], axis=0)
        taken = mm(pick_ref[first + b], block)
        scale = lax.rsqrt(jnp.sum(taken * taken, axis=1, keepdims=True) * (1.0 / width) + 1e-06)
        normed[b * slots : (b + 1) * slots, :] = (taken * scale * gain_ref[...]).astype(BF16)

    for start in range(0, hidden_units, TILE):
        columns = slice(start, min(start + TILE, hidden_units))
        gate_part = mm(normed[...], gate_ref[:, columns])
        up_part = mm(normed[...], up_ref[:, columns])
        hidden[:, columns] = (jax.nn.silu(gate_part) * up_part).astype(BF16)

    for start in range(0, width, TILE):
        columns = slice(start, start + TILE)
        result = mm(hidden[...], down_ref[:, columns])
        for b in range(blocks):
            weighted = (result[b * slots : (b + 1) * slots] * factor_ref[first + b]).astype(BF16)
            placed = mm(put_ref[first + b], weighted).astype(BF16)
            mine[b][:, columns] = placed[:own]
            theirs[b * own : (b + 1) * own, columns] = placed[own:]


def expert(first, blocks, tabs, gain, weights, inputs):
    slots, rows = tabs[0].shape[1:]
    width, hidden_units = weights[0].shape
    own = rows // 2
    m = blocks * slots
    weights = [pltpu.with_memory_space_constraint(w, pltpu.VMEM) for w in weights]
    out = pl.pallas_call(
        functools.partial(expert_kernel, first, blocks, len(inputs) // blocks),
        out_shape=[jax.ShapeDtypeStruct((own, width), BF16)] * blocks
        + [jax.ShapeDtypeStruct((blocks * own, width), BF16)],
        in_specs=[vmem()] * (7 + len(inputs)),
        out_specs=[vmem()] * (blocks + 1),
        scratch_shapes=[
            pltpu.VMEM((m, width), BF16),
            pltpu.VMEM((m, hidden_units), BF16),
        ],
        compiler_params=params(),
        cost_estimate=pl.CostEstimate(
            flops=12 * m * width * hidden_units,
            bytes_accessed=8 * blocks * rows * width,
            transcendentals=m * hidden_units,
        ),
        name="expert",
    )(gain, *tabs, *weights, *inputs)
    return out[:-1], out[-1]


def body(
    req_size,
    exp_size,
    attn_out,
    residual,
    out_weight,
    norm_gain,
    expert_ids,
    gate_weights,
    expert_gate,
    expert_up,
    expert_down,
    shared_gate,
    shared_up,
    shared_down,
):
    rows, width = attn_out.shape
    half = width // 2
    part = half // req_size
    topk = expert_ids.shape[1]
    wrows = out_weight.shape[0]
    capacity = min(rows, 3 * rows * topk // (2 * exp_size))
    slots = -(-2 * capacity // 16) * 16
    chips = exp_size // 2
    depth = chips // 2
    order = ring_order(chips)
    me = lax.axis_index("exp")
    request = lax.axis_index("req")
    core = me % 2
    first_core = core == 0
    position = jnp.asarray([order.index(q) for q in range(chips)], jnp.int32)[me // 2]
    offsets = [0, depth]
    for k in range(1, depth):
        offsets += [-k, k]
    chip_at = jnp.asarray(order, jnp.int32)[(position + jnp.asarray(offsets, jnp.int32)) % chips]

    steps = [(order[i], order[(i + 1) % chips]) for i in range(chips)]
    ahead = [(2 * a + c, 2 * b + c) for a, b in steps for c in range(2)]
    behind = [(b, a) for a, b in ahead]

    def to_ahead(x):
        return lax.ppermute(x, "exp", ahead)

    def to_behind(x):
        return lax.ppermute(x, "exp", behind)

    def to_core(x):
        return lax.ppermute(x, "exp", [(d, d ^ 1) for d in range(exp_size)])

    def to_request(x, shift, swap=0):
        pairs = [
            (i * exp_size + d, ((i + shift) % req_size) * exp_size + (d ^ swap))
            for i in range(req_size)
            for d in range(exp_size)
        ]
        return lax.ppermute(x, ("req", "exp"), pairs)

    def by_core(mine, other, axis):
        return jnp.where(
            first_core, jnp.concatenate([mine, other], axis=axis), jnp.concatenate([other, mine], axis=axis)
        )

    def quarter(x, which_core, which_request):
        return lax.dynamic_slice_in_dim(x, which_core * half + which_request * part, part, axis=1)

    where = jnp.concatenate([jnp.stack([me, core, request]), chip_at]).astype(jnp.int32)

    weight_own, weight_sent = prepare(part, where, expert_ids.T, gate_weights.T, out_weight)
    weight = by_core(weight_own, to_core(weight_sent), 0)
    low = high = weight
    pairs = []
    for _ in range(1, depth):
        low, high = to_ahead(low), to_behind(high)
        pairs.append((low, high))
    cut = wrows + TABLE_ROWS
    last = [to_ahead(low[:cut]), to_behind(high[cut:])]

    def for_request(which):
        return jnp.concatenate([attn_out, quarter(residual, 0, which), quarter(residual, 1, which)], axis=1)

    visits = [for_request(request)]
    for shift in range(1, req_size):
        visits.append(to_request(for_request((request + shift) % req_size), shift))
    passed = min(1, depth - 2)
    pairs[passed], visits[1:] = lax.optimization_barrier((pairs[passed], visits[1:]))
    visits += [to_core(v) for v in visits]

    early = [weight] + [w for pair in pairs[:-1] for w in pair]
    early_slots = [(0, 1)] + [(2 * k + i, 1) for k in range(1, depth - 1) for i in range(2)]
    late = list(pairs[-1]) + last
    late_slots = [(2 * depth - 2, 1), (2 * depth - 1, 1), (1, 2)]
    (acc,) = proj(wrows, early_slots, where, visits, early)
    product = proj(wrows, late_slots, where, visits, late, acc)

    got = {}
    for shift in reversed(range(req_size)):
        for swap in range(2):
            piece = product[swap * req_size + shift]
            if shift == 0:
                got[shift, swap] = piece if swap == 0 else to_core(piece)
            else:
                got[shift, swap] = to_request(piece, req_size - shift, swap)
    halves = []
    for swap in range(2):
        ordered = []
        for place in range(req_size):
            piece = got[place, swap]
            for r in range(1, req_size):
                piece = jnp.where(request == r, got[(place - r) % req_size, swap], piece)
            ordered.append(piece)
        halves.append(jnp.concatenate(ordered, axis=1))
    own_rows = by_core(halves[0], halves[1], 1)

    table_blocks = [weight] + last + [w for pair in pairs for w in pair]
    tabs = tables(wrows, slots, topk, rows, where, [1, 2] + [1] * (chips - 2), table_blocks)
    gain = norm_gain.reshape(1, width)
    weights = [expert_gate[0], expert_up[0], expert_down[0]]

    low, high = to_ahead(own_rows), to_behind(own_rows)
    results = {0: expert(0, 1, tabs, gain, weights, [own_rows, to_core(own_rows)])}
    shared_rows = [own_rows]
    for shift in range(1, req_size):
        shared_rows.append(to_request(own_rows, shift))
    for k in range(1, depth):
        low, high, results[k - 1] = lax.optimization_barrier((low, high, results[k - 1]))
        results[k] = expert(2 * k, 2, tabs, gain, weights, [low, to_core(low), high, to_core(high)])
        if k < depth - 1:
            low, high = to_ahead(low), to_behind(high)
        else:
            low, high = to_ahead(low[: rows // 2]), to_behind(high[rows // 2 :])
    tip = [low, high, to_core(low), to_core(high)]
    gain, results[depth - 1] = lax.optimization_barrier((gain, results[depth - 1]))
    results[depth] = expert(1, 1, tabs, gain, weights, tip)

    def shared_part(x):
        xf = x.astype(F32)
        scale = lax.rsqrt(jnp.mean(xf * xf, axis=1, keepdims=True) + 1e-06)
        n = (xf * scale * norm_gain).astype(BF16)
        h = (jax.nn.silu(mm(n, shared_gate)) * mm(n, shared_up)).astype(BF16)
        return lax.dot_general(h, shared_down, (((1,), (1,)), ((), ())), preferred_element_type=F32)

    shared_in = jnp.concatenate(shared_rows, axis=0)
    shared_in, results[depth] = lax.optimization_barrier((shared_in, results[depth]))
    shared = shared_part(shared_in)

    (mine,), theirs = results[depth]
    far = (mine.astype(F32) + to_core(theirs).astype(F32)).astype(BF16)
    low, high = to_behind(far[rows // 2 :]), to_ahead(far[: rows // 2])
    for k in range(depth - 1, 0, -1):
        (low_mine, high_mine), theirs = results[k]
        came = to_core(theirs)
        to_low = low_mine.astype(F32) + came[:rows].astype(F32)
        to_high = high_mine.astype(F32) + came[rows:].astype(F32)
        if k == depth - 1:
            nothing = jnp.zeros_like(low)
            low = jnp.concatenate([nothing, low], axis=0)
            high = jnp.concatenate([high, nothing], axis=0)
        elif k == depth - 2:
            low, high, shared = lax.optimization_barrier((low, high, shared))
        low = to_behind((to_low + low.astype(F32)).astype(BF16))
        high = to_ahead((to_high + high.astype(F32)).astype(BF16))
    (mine,), theirs = results[0]
    base = own_rows.astype(F32) + shared[:rows] + mine.astype(F32) + to_core(theirs).astype(F32)
    for shift in range(1, req_size):
        back = to_request(shared[shift * rows : (shift + 1) * rows].astype(BF16), req_size - shift)
        base = base + back.astype(F32)
    return (base + low.astype(F32) + high.astype(F32)).astype(BF16)


def solution(mesh):
    return jax.shard_map(
        functools.partial(body, mesh.shape["req"], mesh.shape["exp"]),
        mesh=mesh,
        in_specs=(
            P(("req", "exp"), None),
            P(("req", "exp"), None),
            P("exp", None),
            P(),
            P(("req", "exp"), None),
            P(("req", "exp"), None),
            P("exp", None, None),
            P("exp", None, None),
            P("exp", None, None),
            P(None, "req"),
            P(None, "req"),
            P(None, "req"),
        ),
        out_specs=P(("req", "exp"), None),
        check_vma=False,
    )
```

```python
import functools

import jax
import jax.numpy as jnp
from jax import lax
from jax.experimental import pallas as pl
from jax.experimental.pallas import tpu as pltpu
from jax.sharding import PartitionSpec as P

F32 = jnp.float32
BF16 = jnp.bfloat16
VMEM_BYTES = 12 * 1024 * 1024
TILE = 512
TABLE_ROWS = 16


def ring_order(chips):
    slow = 4
    fast = chips // slow
    order = [a * fast for a in range(slow)]
    for turn, a in enumerate(reversed(range(slow))):
        inner = range(1, fast) if turn % 2 == 0 else range(fast - 1, 0, -1)
        order += [a * fast + b for b in inner]
    return order


def mm(a, b):
    return jnp.dot(a, b, preferred_element_type=F32)


def vmem():
    return pl.BlockSpec(memory_space=pltpu.VMEM)


def smem():
    return pl.BlockSpec(memory_space=pltpu.SMEM)


def hbm():
    return pl.BlockSpec(memory_space=pl.ANY)


def params():
    return pltpu.CompilerParams(vmem_limit_bytes=VMEM_BYTES)


def prepare_kernel(part, where_ref, ids_ref, factors_ref, weight_hbm, own_ref, sent_ref, sems):
    wrows, width = weight_hbm.shape
    topk, rows = ids_ref.shape
    core, request = where_ref[1], where_ref[2]
    copies = []
    for i, (ref, which) in enumerate(((own_ref, core), (sent_ref, 1 - core))):
        start = pl.multiple_of(which * (width // 2) + request * part, 128)
        copies.append(pltpu.make_async_copy(weight_hbm.at[:, pl.ds(start, part)], ref.at[:wrows], sems.at[i]))
        copies[i].start()
    per_row = part // rows
    factors = factors_ref[...]
    big = factors.astype(BF16).astype(F32)
    middle = (factors - big).astype(BF16).astype(F32)
    named = (ids_ref[...].astype(F32), big, middle, factors - big - middle)
    items = [kind[k : k + 1] for kind in named for k in range(topk)]
    items += [jnp.zeros((1, rows), F32)] * (-len(items) % per_row)
    lines = [jnp.concatenate(items[i : i + per_row], axis=1) for i in range(0, len(items), per_row)]
    lines.append(jnp.zeros((TABLE_ROWS - len(lines), part), F32))
    table = jnp.concatenate(lines, axis=0).astype(BF16)
    own_ref[wrows:] = table
    sent_ref[wrows:] = table
    for copy in copies:
        copy.wait()


def prepare(part, where, ids, factors, weight):
    shape = jax.ShapeDtypeStruct((weight.shape[0] + TABLE_ROWS, part), BF16)
    return pl.pallas_call(
        functools.partial(prepare_kernel, part),
        out_shape=[shape] * 2,
        in_specs=[smem(), vmem(), vmem(), hbm()],
        out_specs=[vmem()] * 2,
        scratch_shapes=[pltpu.SemaphoreType.DMA((2,))],
        compiler_params=params(),
        cost_estimate=pl.CostEstimate(flops=0, bytes_accessed=2 * weight.size, transcendentals=0),
        name="prepare",
    )(where, ids, factors, weight)


def proj_kernel(wrows, part, blocks, visits, final, where_ref, *refs):
    total = None
    rows_refs = refs[:visits]
    width = rows_refs[0].shape[1] - 2 * part
    at = visits
    for slot, pieces in blocks:
        start = pl.multiple_of(where_ref[3 + slot] * 2 * wrows, 128)
        columns = jnp.concatenate([r[:, pl.ds(start, 2 * wrows)] for r in rows_refs], axis=0)
        step = wrows + TABLE_ROWS
        if pieces == 1:
            parts = [refs[at][i * step : i * step + wrows] for i in range(2)]
        else:
            parts = [refs[at + i][:wrows] for i in range(2)]
        at += pieces
        term = mm(columns, jnp.concatenate(parts, axis=0))
        total = term if total is None else total + term
    if final:
        total = total + refs[at][...]
        start = pl.multiple_of(width + where_ref[1] * part, 128)
        rows = rows_refs[0].shape[0]
        for i, out_ref in enumerate(refs[at + 1 :]):
            residual = rows_refs[i][:, pl.ds(start, part)].astype(F32)
            out_ref[...] = (residual + total[i * rows : (i + 1) * rows]).astype(BF16)
    else:
        refs[at][...] = total


def proj(wrows, blocks, where, visits, weights, acc=None):
    final = acc is not None
    rows, part = visits[0].shape[0], weights[0].shape[1]
    operands = [where] + visits + weights + ([acc] if final else [])
    count = len(visits)
    if final:
        outs = [jax.ShapeDtypeStruct((rows, part), BF16)] * count
    else:
        outs = [jax.ShapeDtypeStruct((rows * count, part), F32)]
    return pl.pallas_call(
        functools.partial(proj_kernel, wrows, part, blocks, count, final),
        out_shape=outs,
        in_specs=[smem()] + [vmem()] * (len(operands) - 1),
        out_specs=[vmem()] * len(outs),
        compiler_params=params(),
        cost_estimate=pl.CostEstimate(
            flops=8 * rows * count * part * wrows * len(blocks),
            bytes_accessed=4 * part * wrows * len(blocks) + 8 * rows * count * part,
            transcendentals=0,
        ),
        name="proj_final" if final else "proj_part",
    )(*operands)


def tables_kernel(wrows, slots, topk, rows, pieces, where_ref, *refs):
    pick_ref, put_ref, factor_ref = refs[-3:]
    both = 2 * rows
    expert_id = where_ref[0].astype(F32)
    first_core = where_ref[1] == 0
    row_of = lax.broadcasted_iota(jnp.int32, (both, both), 0)
    row_at = lax.broadcasted_iota(jnp.int32, (both, both), 1)
    slot_of = lax.broadcasted_iota(jnp.int32, (slots, both), 0).astype(F32)
    slot_at = lax.broadcasted_iota(jnp.int32, (both, slots), 1).astype(F32)
    step = wrows + TABLE_ROWS
    at = 0
    for block in range(pick_ref.shape[0]):
        if pieces[block] == 1:
            named = [refs[at][i * step + wrows : (i + 1) * step] for i in range(2)]
        else:
            named = [refs[at + i][wrows:] for i in range(2)]
        at += pieces[block]
        named = [n.astype(F32) for n in named]
        ordered = [jnp.where(first_core, named[0], named[1]), jnp.where(first_core, named[1], named[0])]
        per_row = named[0].shape[1] // rows
        selected, factor = [], []
        for n in ordered:
            item = [n[i // per_row : i // per_row + 1, (i % per_row) * rows : (i % per_row + 1) * rows] for i in range(4 * topk)]
            hits = [item[k] == expert_id for k in range(topk)]
            values = [item[topk + k] + item[2 * topk + k] + item[3 * topk + k] for k in range(topk)]
            selected.append(sum(h.astype(F32) for h in hits))
            factor.append(sum(jnp.where(h, v, 0.0) for h, v in zip(hits, values)))
        selected = jnp.concatenate(selected, axis=1)
        factor = jnp.concatenate(factor, axis=1)
        spread = jnp.broadcast_to(selected, (both, both))
        before = jnp.sum(jnp.where(row_at < row_of, spread, 0.0), axis=1, keepdims=True)
        selected_down = jnp.sum(jnp.where(row_at == row_of, spread, 0.0), axis=1, keepdims=True)
        slot_down = jnp.where(selected_down > 0.0, before, -1.0)
        put_ref[block] = (slot_at == slot_down).astype(F32).astype(BF16)
        slot = jnp.sum(jnp.where(row_at == row_of, jnp.broadcast_to(slot_down, (both, both)), 0.0), axis=0, keepdims=True)
        taken = slot_of == slot
        pick_ref[block] = taken.astype(F32).astype(BF16)
        factor_ref[block] = jnp.sum(jnp.where(taken, factor, 0.0), axis=1, keepdims=True)


def tables(wrows, slots, topk, rows, where, pieces, blocks):
    chips = len(pieces)
    both = 2 * rows
    return pl.pallas_call(
        functools.partial(tables_kernel, wrows, slots, topk, rows, pieces),
        out_shape=[
            jax.ShapeDtypeStruct((chips, slots, both), BF16),
            jax.ShapeDtypeStruct((chips, both, slots), BF16),
            jax.ShapeDtypeStruct((chips, slots, 1), F32),
        ],
        in_specs=[smem()] + [vmem()] * len(blocks),
        out_specs=[vmem()] * 3,
        compiler_params=params(),
        cost_estimate=pl.CostEstimate(flops=0, bytes_accessed=8 * chips * slots * both, transcendentals=0),
        name="tables",
    )(where, *blocks)


def expert_kernel(first, blocks, pieces, gain_ref, pick_ref, put_ref, factor_ref, gate_ref, up_ref, down_ref, *refs):
    slots, rows = pick_ref.shape[1:]
    own = rows // 2
    width = gain_ref.shape[1]
    hidden_units = gate_ref.shape[1]
    inputs = refs[: blocks * pieces]
    mine = refs[blocks * pieces : blocks * pieces + blocks]
    theirs, normed, hidden = refs[-3:]

    for b in range(blocks):
        block = jnp.concatenate([inputs[b * pieces + i][...] for i in range(pieces)], axis=0)
        taken = mm(pick_ref[first + b], block)
        scale = lax.rsqrt(jnp.sum(taken * taken, axis=1, keepdims=True) * (1.0 / width) + 1e-06)
        normed[b * slots : (b + 1) * slots, :] = (taken * scale * gain_ref[...]).astype(BF16)

    for start in range(0, hidden_units, TILE):
        columns = slice(start, min(start + TILE, hidden_units))
        gate_part = mm(normed[...], gate_ref[:, columns])
        up_part = mm(normed[...], up_ref[:, columns])
        hidden[:, columns] = (jax.nn.silu(gate_part) * up_part).astype(BF16)

    for start in range(0, width, TILE):
        columns = slice(start, start + TILE)
        result = mm(hidden[...], down_ref[:, columns])
        for b in range(blocks):
            weighted = (result[b * slots : (b + 1) * slots] * factor_ref[first + b]).astype(BF16)
            placed = mm(put_ref[first + b], weighted).astype(BF16)
            mine[b][:, columns] = placed[:own]
            theirs[b * own : (b + 1) * own, columns] = placed[own:]


def expert(first, blocks, tabs, gain, weights, inputs):
    slots, rows = tabs[0].shape[1:]
    width, hidden_units = weights[0].shape
    own = rows // 2
    m = blocks * slots
    weights = [pltpu.with_memory_space_constraint(w, pltpu.VMEM) for w in weights]
    out = pl.pallas_call(
        functools.partial(expert_kernel, first, blocks, len(inputs) // blocks),
        out_shape=[jax.ShapeDtypeStruct((own, width), BF16)] * blocks
        + [jax.ShapeDtypeStruct((blocks * own, width), BF16)],
        in_specs=[vmem()] * (7 + len(inputs)),
        out_specs=[vmem()] * (blocks + 1),
        scratch_shapes=[
            pltpu.VMEM((m, width), BF16),
            pltpu.VMEM((m, hidden_units), BF16),
        ],
        compiler_params=params(),
        cost_estimate=pl.CostEstimate(
            flops=12 * m * width * hidden_units,
            bytes_accessed=8 * blocks * rows * width,
            transcendentals=m * hidden_units,
        ),
        name="expert",
    )(gain, *tabs, *weights, *inputs)
    return out[:-1], out[-1]


def add_kernel(*refs):
    total = refs[0][...].astype(F32)
    for ref in refs[1:-1]:
        total = total + ref[...].astype(F32)
    refs[-1][...] = total.astype(BF16)


def add(rows, *terms):
    width = terms[0][0].shape[1]

    def block(index):
        return pl.BlockSpec((rows, width), lambda i: (index, 0))

    return pl.pallas_call(
        add_kernel,
        grid=(1,),
        out_shape=jax.ShapeDtypeStruct((rows, width), BF16),
        in_specs=[block(index) for _, index in terms],
        out_specs=block(0),
        compiler_params=params(),
        cost_estimate=pl.CostEstimate(
            flops=rows * width * len(terms), bytes_accessed=2 * rows * width * (len(terms) + 1), transcendentals=0
        ),
        name="add",
    )(*[array for array, _ in terms])


def body(
    req_size,
    exp_size,
    attn_out,
    residual,
    out_weight,
    norm_gain,
    expert_ids,
    gate_weights,
    expert_gate,
    expert_up,
    expert_down,
    shared_gate,
    shared_up,
    shared_down,
):
    rows, width = attn_out.shape
    half = width // 2
    part = half // req_size
    topk = expert_ids.shape[1]
    wrows = out_weight.shape[0]
    capacity = min(rows, 3 * rows * topk // (2 * exp_size))
    slots = -(-2 * capacity // 16) * 16
    chips = exp_size // 2
    depth = chips // 2
    order = ring_order(chips)
    me = lax.axis_index("exp")
    request = lax.axis_index("req")
    core = me % 2
    first_core = core == 0
    position = jnp.asarray([order.index(q) for q in range(chips)], jnp.int32)[me // 2]
    offsets = [0, depth]
    for k in range(1, depth):
        offsets += [-k, k]
    chip_at = jnp.asarray(order, jnp.int32)[(position + jnp.asarray(offsets, jnp.int32)) % chips]

    steps = [(order[i], order[(i + 1) % chips]) for i in range(chips)]
    ahead = [(2 * a + c, 2 * b + c) for a, b in steps for c in range(2)]
    behind = [(b, a) for a, b in ahead]

    def to_ahead(x):
        return lax.ppermute(x, "exp", ahead)

    def to_behind(x):
        return lax.ppermute(x, "exp", behind)

    def to_core(x):
        return lax.ppermute(x, "exp", [(d, d ^ 1) for d in range(exp_size)])

    def to_request(x, shift, swap=0):
        pairs = [
            (i * exp_size + d, ((i + shift) % req_size) * exp_size + (d ^ swap))
            for i in range(req_size)
            for d in range(exp_size)
        ]
        return lax.ppermute(x, ("req", "exp"), pairs)

    def by_core(mine, other, axis):
        return jnp.where(
            first_core, jnp.concatenate([mine, other], axis=axis), jnp.concatenate([other, mine], axis=axis)
        )

    def quarter(x, which_core, which_request):
        return lax.dynamic_slice_in_dim(x, which_core * half + which_request * part, part, axis=1)

    here = jnp.stack([me, core, request]).astype(jnp.int32)

    weight_own, weight_sent = prepare(part, here, expert_ids.T, gate_weights.T, out_weight)
    weight = by_core(weight_own, to_core(weight_sent), 0)
    weight, attn_out, residual = lax.optimization_barrier((weight, attn_out, residual))
    where = jnp.concatenate([here, chip_at])
    low = high = weight
    pairs = []
    for _ in range(1, depth):
        low, high = to_ahead(low), to_behind(high)
        pairs.append((low, high))
    cut = wrows + TABLE_ROWS
    last = [to_ahead(low[:cut]), to_behind(high[cut:])]

    def for_request(which):
        return jnp.concatenate([attn_out, quarter(residual, 0, which), quarter(residual, 1, which)], axis=1)

    visits = [for_request(request)]
    for shift in range(1, req_size):
        visits.append(to_request(for_request((request + shift) % req_size), shift))
    passed = min(1, depth - 2)
    pairs[passed], visits[1:] = lax.optimization_barrier((pairs[passed], visits[1:]))
    visits += [to_core(v) for v in visits]

    early = [weight] + [w for pair in pairs[:-1] for w in pair]
    late = last + list(pairs[-1])
    tabs_early = tables(wrows, slots, topk, rows, here, [1] * (chips - 3), early)
    whole = early + list(pairs[-1])
    whole_slots = [(0, 1)] + [(i, 1) for i in range(2, chips)]
    (acc,) = proj(wrows, whole_slots, where, visits, whole)
    acc, tabs_early = lax.optimization_barrier((acc, tabs_early))
    product = proj(wrows, [(1, 2)], where, visits, last, acc)
    tabs_late = tables(wrows, slots, topk, rows, here, [2, 1, 1], late)

    got = {}
    for shift in reversed(range(req_size)):
        for swap in range(2):
            piece = product[swap * req_size + shift]
            if shift == 0:
                got[shift, swap] = piece if swap == 0 else to_core(piece)
            else:
                got[shift, swap] = to_request(piece, req_size - shift, swap)
    got, tabs_late = lax.optimization_barrier((got, tabs_late))
    halves = []
    for swap in range(2):
        ordered = []
        for place in range(req_size):
            piece = got[place, swap]
            for r in range(1, req_size):
                piece = jnp.where(request == r, got[(place - r) % req_size, swap], piece)
            ordered.append(piece)
        halves.append(jnp.concatenate(ordered, axis=1))
    own_rows = by_core(halves[0], halves[1], 1)

    gain = norm_gain.reshape(1, width)
    weights = [expert_gate[0], expert_up[0], expert_down[0]]

    low, high = to_ahead(own_rows), to_behind(own_rows)
    results = {0: expert(0, 1, tabs_early, gain, weights, [own_rows, to_core(own_rows)])}
    shared_rows = [own_rows]
    for shift in range(1, req_size):
        shared_rows.append(to_request(own_rows, shift))
    for k in range(1, depth):
        low, high, results[k - 1] = lax.optimization_barrier((low, high, results[k - 1]))
        first, tabs = (2 * k - 1, tabs_early) if k < depth - 1 else (1, tabs_late)
        results[k] = expert(first, 2, tabs, gain, weights, [low, to_core(low), high, to_core(high)])
        if k < depth - 1:
            low, high = to_ahead(low), to_behind(high)
        else:
            low, high = to_ahead(low[: rows // 2]), to_behind(high[rows // 2 :])
    low, high, results[depth - 1] = lax.optimization_barrier((low, high, results[depth - 1]))
    results[depth] = expert(0, 1, tabs_late, gain, weights, [low, high, to_core(low), to_core(high)])

    def shared_part(x):
        xf = x.astype(F32)
        scale = lax.rsqrt(jnp.mean(xf * xf, axis=1, keepdims=True) + 1e-06)
        n = (xf * scale * norm_gain).astype(BF16)
        h = (jax.nn.silu(mm(n, shared_gate)) * mm(n, shared_up)).astype(BF16)
        return lax.dot_general(h, shared_down, (((1,), (1,)), ((), ())), preferred_element_type=F32)

    shared_in = jnp.concatenate(shared_rows, axis=0)
    shared_in, results[depth] = lax.optimization_barrier((shared_in, results[depth]))
    shared = shared_part(shared_in)

    cut = rows // 2
    low, high = [None, None], [None, None]
    for k in range(depth - 1, 0, -1):
        (low_mine, high_mine), theirs = results[k]
        came = to_core(theirs)

        def send_low(chunk):
            terms = [(low_mine, chunk), (came, chunk)] + [(low[chunk], 0)] * (low[chunk] is not None)
            low[chunk] = to_behind(add(cut, *terms))

        def send_high(chunk):
            terms = [(high_mine, chunk), (came, 2 + chunk)] + [(high[chunk], 0)] * (high[chunk] is not None)
            high[chunk] = to_ahead(add(cut, *terms))

        if k == depth - 1:
            send_low(0)
            send_high(1)
            results[depth], low[0], high[1] = lax.optimization_barrier((results[depth], low[0], high[1]))
            (mine,), theirs = results[depth]
            far = to_core(theirs)
            low[1] = to_behind(add(cut, (mine, 1), (far, 1)))
            high[0] = to_ahead(add(cut, (mine, 0), (far, 0)))
            send_low(1)
            send_high(0)
            continue
        if k == depth - 2:
            low[1], shared = lax.optimization_barrier((low[1], shared))
        for chunk in range(2):
            send_low(chunk)
            send_high(1 - chunk)
    low, high = jnp.concatenate(low, axis=0), jnp.concatenate(high, axis=0)
    (mine,), theirs = results[0]
    base = own_rows.astype(F32) + shared[:rows] + mine.astype(F32) + to_core(theirs).astype(F32)
    for shift in range(1, req_size):
        back = to_request(shared[shift * rows : (shift + 1) * rows].astype(BF16), req_size - shift)
        base = base + back.astype(F32)
    return (base + low.astype(F32) + high.astype(F32)).astype(BF16)


def solution(mesh):
    return jax.shard_map(
        functools.partial(body, mesh.shape["req"], mesh.shape["exp"]),
        mesh=mesh,
        in_specs=(
            P(("req", "exp"), None),
            P(("req", "exp"), None),
            P("exp", None),
            P(),
            P(("req", "exp"), None),
            P(("req", "exp"), None),
            P("exp", None, None),
            P("exp", None, None),
            P("exp", None, None),
            P(None, "req"),
            P(None, "req"),
            P(None, "req"),
        ),
        out_specs=P(("req", "exp"), None),
        check_vma=False,
    )
```

```python
import functools

import jax
import jax.numpy as jnp
from jax import lax
from jax.experimental import pallas as pl
from jax.experimental.pallas import tpu as pltpu
from jax.sharding import PartitionSpec as P

F32 = jnp.float32
BF16 = jnp.bfloat16
VMEM_BYTES = 12 * 1024 * 1024
TILE = 512
TABLE_ROWS = 16


def ring_order(chips):
    slow = 4
    fast = chips // slow
    order = [a * fast for a in range(slow)]
    for turn, a in enumerate(reversed(range(slow))):
        inner = range(1, fast) if turn % 2 == 0 else range(fast - 1, 0, -1)
        order += [a * fast + b for b in inner]
    return order


def mm(a, b):
    return jnp.dot(a, b, preferred_element_type=F32)


def vmem():
    return pl.BlockSpec(memory_space=pltpu.VMEM)


def smem():
    return pl.BlockSpec(memory_space=pltpu.SMEM)


def hbm():
    return pl.BlockSpec(memory_space=pl.ANY)


def params():
    return pltpu.CompilerParams(vmem_limit_bytes=VMEM_BYTES)


def prepare_kernel(part, where_ref, ids_hbm, factors_hbm, weight_hbm, own_ref, sent_ref, ids_ref, factors_ref, sems):
    wrows, width = weight_hbm.shape
    topk, rows = ids_ref.shape
    core, request = where_ref[1], where_ref[2]
    small = [
        pltpu.make_async_copy(ids_hbm, ids_ref, sems.at[2]),
        pltpu.make_async_copy(factors_hbm, factors_ref, sems.at[3]),
    ]
    large = []
    for i, (ref, which) in enumerate(((own_ref, core), (sent_ref, 1 - core))):
        start = pl.multiple_of(which * (width // 2) + request * part, 128)
        large.append(pltpu.make_async_copy(weight_hbm.at[:, pl.ds(start, part)], ref.at[:wrows], sems.at[i]))
    for copy in small + large:
        copy.start()
    for copy in small:
        copy.wait()
    per_row = part // rows
    factors = factors_ref[...]
    big = factors.astype(BF16).astype(F32)
    middle = (factors - big).astype(BF16).astype(F32)
    named = (ids_ref[...].astype(F32), big, middle, factors - big - middle)
    items = [kind[k : k + 1] for kind in named for k in range(topk)]
    items += [jnp.zeros((1, rows), F32)] * (-len(items) % per_row)
    lines = [jnp.concatenate(items[i : i + per_row], axis=1) for i in range(0, len(items), per_row)]
    lines.append(jnp.zeros((TABLE_ROWS - len(lines), part), F32))
    table = jnp.concatenate(lines, axis=0).astype(BF16)
    own_ref[wrows:] = table
    sent_ref[wrows:] = table
    for copy in large:
        copy.wait()


def prepare(part, where, ids, factors, weight):
    shape = jax.ShapeDtypeStruct((weight.shape[0] + TABLE_ROWS, part), BF16)
    arrays = [pltpu.with_memory_space_constraint(x, pltpu.HBM) for x in (ids, factors, weight)]
    return pl.pallas_call(
        functools.partial(prepare_kernel, part),
        out_shape=[shape] * 2,
        in_specs=[smem()] + [hbm()] * 3,
        out_specs=[vmem()] * 2,
        scratch_shapes=[
            pltpu.VMEM(ids.shape, ids.dtype),
            pltpu.VMEM(factors.shape, factors.dtype),
            pltpu.SemaphoreType.DMA((4,)),
        ],
        compiler_params=params(),
        cost_estimate=pl.CostEstimate(flops=0, bytes_accessed=2 * weight.size, transcendentals=0),
        name="prepare",
    )(where, *arrays)


def small_call(kernel, name, shapes, operands, moved):
    return pl.pallas_call(
        kernel,
        out_shape=shapes,
        in_specs=[smem()] + [vmem()] * (len(operands) - 1),
        out_specs=[vmem()] * len(shapes),
        compiler_params=params(),
        cost_estimate=pl.CostEstimate(flops=0, bytes_accessed=moved, transcendentals=0),
        name=name,
    )(*operands)


def join_kernel(where_ref, mine_ref, other_ref, out_ref):
    rows = mine_ref.shape[0]
    core = where_ref[1]
    out_ref[pl.ds(pl.multiple_of(core * rows, 16), rows)] = mine_ref[...]
    out_ref[pl.ds(pl.multiple_of((1 - core) * rows, 16), rows)] = other_ref[...]


def join(where, mine, other):
    shape = jax.ShapeDtypeStruct((2 * mine.shape[0], mine.shape[1]), mine.dtype)
    return small_call(join_kernel, "join", [shape], [where, mine, other], 8 * mine.size)[0]


def pack_kernel(count, part, where_ref, attn_hbm, residual_hbm, *refs):
    width = attn_hbm.shape[1]
    outs, sems = refs[:-1], refs[-1]
    copies = []
    for shift, out_ref in enumerate(outs):
        moves = [(attn_hbm, out_ref.at[:, :width])]
        request = lax.rem(where_ref[2] + shift, count)
        for core in range(2):
            start = pl.multiple_of(core * (width // 2) + request * part, 128)
            target = out_ref.at[:, width + core * part : width + (core + 1) * part]
            moves.append((residual_hbm.at[:, pl.ds(start, part)], target))
        for i, (source, target) in enumerate(moves):
            copies.append(pltpu.make_async_copy(source, target, sems.at[3 * shift + i]))
    for copy in copies:
        copy.start()
    for copy in copies:
        copy.wait()


def pack(count, part, where, attn, residual):
    rows, width = attn.shape
    arrays = [pltpu.with_memory_space_constraint(x, pltpu.HBM) for x in (attn, residual)]
    return pl.pallas_call(
        functools.partial(pack_kernel, count, part),
        out_shape=[jax.ShapeDtypeStruct((rows, width + 2 * part), BF16)] * count,
        in_specs=[smem(), hbm(), hbm()],
        out_specs=[vmem()] * count,
        scratch_shapes=[pltpu.SemaphoreType.DMA((3 * count,))],
        compiler_params=params(),
        cost_estimate=pl.CostEstimate(flops=0, bytes_accessed=4 * attn.size * count, transcendentals=0),
        name="pack",
    )(where, *arrays)


def assemble_kernel(count, where_ref, *refs):
    out_ref = refs[-1]
    part = refs[0].shape[1]
    for place in range(count):
        for swap in range(2):
            core = where_ref[1] if swap == 0 else 1 - where_ref[1]
            request = lax.rem(where_ref[2] + place, count)
            start = pl.multiple_of(core * (count * part) + request * part, 128)
            out_ref[:, pl.ds(start, part)] = refs[2 * place + swap][...]


def assemble(count, where, pieces):
    rows, part = pieces[0].shape
    shape = jax.ShapeDtypeStruct((rows, 2 * count * part), BF16)
    return small_call(
        functools.partial(assemble_kernel, count), "assemble", [shape], [where] + pieces, 8 * rows * count * part
    )[0]


def proj_kernel(wrows, part, blocks, visits, final, where_ref, ring_ref, *refs):
    total = None
    rows_refs = refs[:visits]
    width = rows_refs[0].shape[1] - 2 * part
    at = visits
    chips = ring_ref.shape[0] // 2
    position = ring_ref[where_ref[0] // 2]
    for offset, pieces in blocks:
        chip = ring_ref[chips + lax.rem(position + offset + chips, chips)]
        start = pl.multiple_of(chip * 2 * wrows, 128)
        columns = jnp.concatenate([r[:, pl.ds(start, 2 * wrows)] for r in rows_refs], axis=0)
        step = wrows + TABLE_ROWS
        if pieces == 1:
            parts = [refs[at][i * step : i * step + wrows] for i in range(2)]
        else:
            parts = [refs[at + i][:wrows] for i in range(2)]
        at += pieces
        term = mm(columns, jnp.concatenate(parts, axis=0))
        total = term if total is None else total + term
    if final:
        total = total + refs[at][...]
        start = pl.multiple_of(width + where_ref[1] * part, 128)
        rows = rows_refs[0].shape[0]
        for i, out_ref in enumerate(refs[at + 1 :]):
            residual = rows_refs[i][:, pl.ds(start, part)].astype(F32)
            out_ref[...] = (residual + total[i * rows : (i + 1) * rows]).astype(BF16)
    else:
        refs[at][...] = total


def proj(wrows, blocks, where, ring, visits, weights, acc=None):
    final = acc is not None
    rows, part = visits[0].shape[0], weights[0].shape[1]
    operands = [where, ring] + visits + weights + ([acc] if final else [])
    count = len(visits)
    if final:
        outs = [jax.ShapeDtypeStruct((rows, part), BF16)] * count
    else:
        outs = [jax.ShapeDtypeStruct((rows * count, part), F32)]
    return pl.pallas_call(
        functools.partial(proj_kernel, wrows, part, blocks, count, final),
        out_shape=outs,
        in_specs=[smem()] * 2 + [vmem()] * (len(operands) - 2),
        out_specs=[vmem()] * len(outs),
        compiler_params=params(),
        cost_estimate=pl.CostEstimate(
            flops=8 * rows * count * part * wrows * len(blocks),
            bytes_accessed=4 * part * wrows * len(blocks) + 8 * rows * count * part,
            transcendentals=0,
        ),
        name="proj_final" if final else "proj_part",
    )(*operands)


def tables_kernel(wrows, slots, topk, rows, pieces, where_ref, *refs):
    pick_ref, put_ref, factor_ref = refs[-3:]
    both = 2 * rows
    expert_id = where_ref[0].astype(F32)
    first_core = where_ref[1] == 0
    row_of = lax.broadcasted_iota(jnp.int32, (both, both), 0)
    row_at = lax.broadcasted_iota(jnp.int32, (both, both), 1)
    slot_of = lax.broadcasted_iota(jnp.int32, (slots, both), 0).astype(F32)
    slot_at = lax.broadcasted_iota(jnp.int32, (both, slots), 1).astype(F32)
    step = wrows + TABLE_ROWS
    at = 0
    for block in range(pick_ref.shape[0]):
        if pieces[block] == 1:
            named = [refs[at][i * step + wrows : (i + 1) * step] for i in range(2)]
        else:
            named = [refs[at + i][wrows:] for i in range(2)]
        at += pieces[block]
        named = [n.astype(F32) for n in named]
        ordered = [jnp.where(first_core, named[0], named[1]), jnp.where(first_core, named[1], named[0])]
        per_row = named[0].shape[1] // rows
        selected, factor = [], []
        for n in ordered:
            item = [n[i // per_row : i // per_row + 1, (i % per_row) * rows : (i % per_row + 1) * rows] for i in range(4 * topk)]
            hits = [item[k] == expert_id for k in range(topk)]
            values = [item[topk + k] + item[2 * topk + k] + item[3 * topk + k] for k in range(topk)]
            selected.append(sum(h.astype(F32) for h in hits))
            factor.append(sum(jnp.where(h, v, 0.0) for h, v in zip(hits, values)))
        selected = jnp.concatenate(selected, axis=1)
        factor = jnp.concatenate(factor, axis=1)
        spread = jnp.broadcast_to(selected, (both, both))
        before = jnp.sum(jnp.where(row_at < row_of, spread, 0.0), axis=1, keepdims=True)
        selected_down = jnp.sum(jnp.where(row_at == row_of, spread, 0.0), axis=1, keepdims=True)
        slot_down = jnp.where(selected_down > 0.0, before, -1.0)
        put_ref[block] = (slot_at == slot_down).astype(F32).astype(BF16)
        slot = jnp.sum(jnp.where(row_at == row_of, jnp.broadcast_to(slot_down, (both, both)), 0.0), axis=0, keepdims=True)
        taken = slot_of == slot
        pick_ref[block] = taken.astype(F32).astype(BF16)
        factor_ref[block] = jnp.sum(jnp.where(taken, factor, 0.0), axis=1, keepdims=True)


def tables(wrows, slots, topk, rows, where, pieces, blocks):
    chips = len(pieces)
    both = 2 * rows
    return pl.pallas_call(
        functools.partial(tables_kernel, wrows, slots, topk, rows, pieces),
        out_shape=[
            jax.ShapeDtypeStruct((chips, slots, both), BF16),
            jax.ShapeDtypeStruct((chips, both, slots), BF16),
            jax.ShapeDtypeStruct((chips, slots, 1), F32),
        ],
        in_specs=[smem()] + [vmem()] * len(blocks),
        out_specs=[vmem()] * 3,
        compiler_params=params(),
        cost_estimate=pl.CostEstimate(flops=0, bytes_accessed=8 * chips * slots * both, transcendentals=0),
        name="tables",
    )(where, *blocks)


def expert_kernel(first, blocks, pieces, gain_ref, pick_ref, put_ref, factor_ref, gate_ref, up_ref, down_ref, *refs):
    slots, rows = pick_ref.shape[1:]
    own = rows // 2
    width = gain_ref.shape[1]
    hidden_units = gate_ref.shape[1]
    inputs = refs[: blocks * pieces]
    mine = refs[blocks * pieces : blocks * pieces + blocks]
    theirs, normed, hidden = refs[-3:]

    for b in range(blocks):
        block = jnp.concatenate([inputs[b * pieces + i][...] for i in range(pieces)], axis=0)
        taken = mm(pick_ref[first + b], block)
        scale = lax.rsqrt(jnp.sum(taken * taken, axis=1, keepdims=True) * (1.0 / width) + 1e-06)
        normed[b * slots : (b + 1) * slots, :] = (taken * scale * gain_ref[...]).astype(BF16)

    for start in range(0, hidden_units, TILE):
        columns = slice(start, min(start + TILE, hidden_units))
        gate_part = mm(normed[...], gate_ref[:, columns])
        up_part = mm(normed[...], up_ref[:, columns])
        hidden[:, columns] = (jax.nn.silu(gate_part) * up_part).astype(BF16)

    for start in range(0, width, TILE):
        columns = slice(start, start + TILE)
        result = mm(hidden[...], down_ref[:, columns])
        for b in range(blocks):
            weighted = (result[b * slots : (b + 1) * slots] * factor_ref[first + b]).astype(BF16)
            placed = mm(put_ref[first + b], weighted).astype(BF16)
            mine[b][:, columns] = placed[:own]
            theirs[b * own : (b + 1) * own, columns] = placed[own:]


def expert(first, blocks, tabs, gain, weights, inputs):
    slots, rows = tabs[0].shape[1:]
    width, hidden_units = weights[0].shape
    own = rows // 2
    m = blocks * slots
    weights = [pltpu.with_memory_space_constraint(w, pltpu.VMEM) for w in weights]
    out = pl.pallas_call(
        functools.partial(expert_kernel, first, blocks, len(inputs) // blocks),
        out_shape=[jax.ShapeDtypeStruct((own, width), BF16)] * blocks
        + [jax.ShapeDtypeStruct((blocks * own, width), BF16)],
        in_specs=[vmem()] * (7 + len(inputs)),
        out_specs=[vmem()] * (blocks + 1),
        scratch_shapes=[
            pltpu.VMEM((m, width), BF16),
            pltpu.VMEM((m, hidden_units), BF16),
        ],
        compiler_params=params(),
        cost_estimate=pl.CostEstimate(
            flops=12 * m * width * hidden_units,
            bytes_accessed=8 * blocks * rows * width,
            transcendentals=m * hidden_units,
        ),
        name="expert",
    )(gain, *tabs, *weights, *inputs)
    return out[:-1], out[-1]


def shared_kernel(count, gain_ref, gate_hbm, up_hbm, down_hbm, *refs):
    inputs, outs = refs[:count], refs[count : 2 * count]
    gate_ref, up_ref, down_ref, normed, hidden, sems = refs[2 * count :]
    units, width = gate_ref.shape
    rows = inputs[0].shape[0]
    tiles = [(start, min(256, units - start)) for start in range(0, units, 256)]
    copies = []
    for i, (start, size) in enumerate(tiles):
        span = pl.ds(start, size)
        for j, (source, target) in enumerate(((gate_hbm, gate_ref), (up_hbm, up_ref))):
            copies.append(pltpu.make_async_copy(source.at[span], target.at[span], sems.at[2 * i + j]))
    copies.append(pltpu.make_async_copy(down_hbm, down_ref, sems.at[2 * len(tiles)]))
    for copy in copies:
        copy.start()
    for i, ref in enumerate(inputs):
        x = ref[...].astype(F32)
        scale = lax.rsqrt(jnp.sum(x * x, axis=1, keepdims=True) * (1.0 / width) + 1e-06)
        normed[i * rows : (i + 1) * rows] = (x * scale * gain_ref[...]).astype(BF16)
    across = (((1,), (1,)), ((), ()))
    for i, (start, size) in enumerate(tiles):
        span = slice(start, start + size)
        copies[2 * i].wait()
        copies[2 * i + 1].wait()
        gate_part = lax.dot_general(normed[...], gate_ref[span], across, preferred_element_type=F32)
        up_part = lax.dot_general(normed[...], up_ref[span], across, preferred_element_type=F32)
        hidden[:, span] = (jax.nn.silu(gate_part) * up_part).astype(BF16)
    copies[-1].wait()
    for start in range(0, width, TILE):
        span = slice(start, start + TILE)
        result = mm(hidden[...], down_ref[:, span])
        for i, ref in enumerate(outs):
            ref[:, span] = result[i * rows : (i + 1) * rows].astype(ref.dtype)


def shared_expert(gain, weights, inputs):
    count = len(inputs)
    rows, width = inputs[0].shape
    units = weights[0].shape[0]
    weights = [pltpu.with_memory_space_constraint(w, pltpu.HBM) for w in weights]
    shapes = [jax.ShapeDtypeStruct((rows, width), F32)] + [jax.ShapeDtypeStruct((rows, width), BF16)] * (count - 1)
    return pl.pallas_call(
        functools.partial(shared_kernel, count),
        out_shape=shapes,
        in_specs=[vmem()] + [hbm()] * 3 + [vmem()] * count,
        out_specs=[vmem()] * count,
        scratch_shapes=[pltpu.VMEM((units, width), BF16)] * 3
        + [
            pltpu.VMEM((count * rows, width), BF16),
            pltpu.VMEM((count * rows, units), BF16),
            pltpu.SemaphoreType.DMA((2 * -(-units // 256) + 1,)),
        ],
        compiler_params=pltpu.CompilerParams(vmem_limit_bytes=24 * 1024 * 1024),
        cost_estimate=pl.CostEstimate(
            flops=12 * count * rows * width * units,
            bytes_accessed=6 * units * width + 4 * count * rows * width,
            transcendentals=count * rows * units,
        ),
        name="shared",
    )(gain, *weights, *inputs)


def base_kernel(*refs):
    total = refs[0][...]
    for ref in refs[1:-1]:
        total = total + ref[...].astype(F32)
    refs[-1][...] = total


def final_kernel(chunks, base_ref, *refs):
    out_ref = refs[-1]
    rows = refs[0].shape[0]
    for chunk in range(chunks):
        span = slice(chunk * rows, (chunk + 1) * rows)
        total = base_ref[span] + refs[chunk][...].astype(F32) + refs[chunks + chunk][...].astype(F32)
        out_ref[span] = total.astype(BF16)


def plain_call(kernel, name, shape, operands):
    return pl.pallas_call(
        kernel,
        out_shape=shape,
        in_specs=[vmem()] * len(operands),
        out_specs=vmem(),
        compiler_params=params(),
        cost_estimate=pl.CostEstimate(flops=0, bytes_accessed=8 * operands[0].size, transcendentals=0),
        name=name,
    )(*operands)


def add_kernel(*refs):
    total = refs[0][...].astype(F32)
    for ref in refs[1:-1]:
        total = total + ref[...].astype(F32)
    refs[-1][...] = total.astype(BF16)


def add(rows, *terms):
    width = terms[0][0].shape[1]

    def block(index):
        return pl.BlockSpec((rows, width), lambda i: (index, 0))

    return pl.pallas_call(
        add_kernel,
        grid=(1,),
        out_shape=jax.ShapeDtypeStruct((rows, width), BF16),
        in_specs=[block(index) for _, index in terms],
        out_specs=block(0),
        compiler_params=params(),
        cost_estimate=pl.CostEstimate(
            flops=rows * width * len(terms), bytes_accessed=2 * rows * width * (len(terms) + 1), transcendentals=0
        ),
        name="add",
    )(*[array for array, _ in terms])


def body(
    req_size,
    exp_size,
    attn_out,
    residual,
    out_weight,
    norm_gain,
    expert_ids,
    gate_weights,
    expert_gate,
    expert_up,
    expert_down,
    shared_gate,
    shared_up,
    shared_down,
):
    rows, width = attn_out.shape
    half = width // 2
    part = half // req_size
    topk = expert_ids.shape[1]
    wrows = out_weight.shape[0]
    capacity = min(rows, 3 * rows * topk // (2 * exp_size))
    slots = -(-2 * capacity // 16) * 16
    chips = exp_size // 2
    depth = chips // 2
    order = ring_order(chips)
    me = lax.axis_index("exp")
    request = lax.axis_index("req")
    here = jnp.stack([me, me % 2, lax.axis_index("req")]).astype(jnp.int32)
    ring = jnp.asarray([order.index(q) for q in range(chips)] + order, jnp.int32)

    steps = [(order[i], order[(i + 1) % chips]) for i in range(chips)]
    ahead = [(2 * a + c, 2 * b + c) for a, b in steps for c in range(2)]
    behind = [(b, a) for a, b in ahead]

    def to_ahead(x):
        return lax.ppermute(x, "exp", ahead)

    def to_behind(x):
        return lax.ppermute(x, "exp", behind)

    def to_core(x):
        return lax.ppermute(x, "exp", [(d, d ^ 1) for d in range(exp_size)])

    def to_request(x, shift, swap=0):
        pairs = [
            (i * exp_size + d, ((i + shift) % req_size) * exp_size + (d ^ swap))
            for i in range(req_size)
            for d in range(exp_size)
        ]
        return lax.ppermute(x, ("req", "exp"), pairs)

    weight_own, weight_sent = prepare(part, here, expert_ids.T, gate_weights.T, out_weight)
    weight = join(here, weight_own, to_core(weight_sent))
    low = high = weight
    pairs = []
    for _ in range(1, depth):
        low, high = to_ahead(low), to_behind(high)
        pairs.append((low, high))
    cut = wrows + TABLE_ROWS
    last = [to_ahead(low[:cut]), to_behind(high[cut:])]

    weight, attn_out, residual = lax.optimization_barrier((weight, attn_out, residual))
    packed = pack(req_size, part, here, attn_out, residual)
    visits = [packed[0]] + [to_request(packed[shift], shift) for shift in range(1, req_size)]
    passed = min(1, depth - 2)
    pairs[passed], visits[1:] = lax.optimization_barrier((pairs[passed], visits[1:]))
    visits += [to_core(v) for v in visits]

    early = [weight] + [w for pair in pairs[:-1] for w in pair]
    late = last + list(pairs[-1])
    tabs_early = tables(wrows, slots, topk, rows, here, [1] * (chips - 3), early)
    whole = early + list(pairs[-1])
    places = [(0, 1)] + [(side * k, 1) for k in range(1, depth) for side in (-1, 1)]
    (acc,) = proj(wrows, places, here, ring, visits, whole)
    acc, tabs_early = lax.optimization_barrier((acc, tabs_early))
    product = proj(wrows, [(depth, 2)], here, ring, visits, last, acc)
    tabs_late = tables(wrows, slots, topk, rows, here, [2, 1, 1], late)

    got = {}
    for shift in reversed(range(req_size)):
        for swap in range(2):
            piece = product[swap * req_size + shift]
            if shift == 0:
                got[shift, swap] = piece if swap == 0 else to_core(piece)
            else:
                got[shift, swap] = to_request(piece, req_size - shift, swap)
    got, tabs_late = lax.optimization_barrier((got, tabs_late))
    own_rows = assemble(req_size, here, [got[place, swap] for place in range(req_size) for swap in range(2)])
    gain = norm_gain.reshape(1, width)
    weights = [expert_gate[0], expert_up[0], expert_down[0]]

    low, high = to_ahead(own_rows), to_behind(own_rows)
    results = {0: expert(0, 1, tabs_early, gain, weights, [own_rows, to_core(own_rows)])}
    shared_rows = [own_rows]
    for shift in range(1, req_size):
        shared_rows.append(to_request(own_rows, shift))
    for k in range(1, depth):
        low, high, results[k - 1] = lax.optimization_barrier((low, high, results[k - 1]))
        if k == depth - 1:
            low, high, shared_rows = lax.optimization_barrier((low, high, shared_rows))
        first, tabs = (2 * k - 1, tabs_early) if k < depth - 1 else (1, tabs_late)
        results[k] = expert(first, 2, tabs, gain, weights, [low, to_core(low), high, to_core(high)])
        if k < depth - 1:
            low, high = to_ahead(low), to_behind(high)
        else:
            low, high = to_ahead(low[: rows // 2]), to_behind(high[rows // 2 :])
    low, high, results[depth - 1] = lax.optimization_barrier((low, high, results[depth - 1]))
    results[depth] = expert(0, 1, tabs_late, gain, weights, [low, high, to_core(low), to_core(high)])

    shared_rows, results[depth] = lax.optimization_barrier((shared_rows, results[depth]))
    shared = shared_expert(gain, [shared_gate.T, shared_up.T, shared_down.T], shared_rows)

    cut = rows // 2
    low, high = [None, None], [None, None]
    for k in range(depth - 1, 0, -1):
        (low_mine, high_mine), theirs = results[k]
        came = to_core(theirs)

        def send_low(chunk):
            terms = [(low_mine, chunk), (came, chunk)] + [(low[chunk], 0)] * (low[chunk] is not None)
            low[chunk] = to_behind(add(cut, *terms))

        def send_high(chunk):
            terms = [(high_mine, chunk), (came, 2 + chunk)] + [(high[chunk], 0)] * (high[chunk] is not None)
            high[chunk] = to_ahead(add(cut, *terms))

        if k == depth - 1:
            send_low(0)
            send_high(1)
            results[depth], low[0], high[1] = lax.optimization_barrier((results[depth], low[0], high[1]))
            (mine,), theirs = results[depth]
            far = to_core(theirs)
            low[1] = to_behind(add(cut, (mine, 1), (far, 1)))
            high[0] = to_ahead(add(cut, (mine, 0), (far, 0)))
            send_low(1)
            send_high(0)
            continue
        if k == depth - 2:
            low[1], shared = lax.optimization_barrier((low[1], shared))
        for chunk in range(2):
            send_low(chunk)
            send_high(1 - chunk)
    (mine,), theirs = results[0]
    backs = [to_request(shared[shift], req_size - shift) for shift in range(1, req_size)]
    terms = [shared[0], own_rows, mine, to_core(theirs)] + backs
    base = plain_call(base_kernel, "base", jax.ShapeDtypeStruct((rows, width), F32), terms)
    return plain_call(
        functools.partial(final_kernel, 2), "final", jax.ShapeDtypeStruct((rows, width), BF16), [base] + low + high
    )


def solution(mesh):
    return jax.shard_map(
        functools.partial(body, mesh.shape["req"], mesh.shape["exp"]),
        mesh=mesh,
        in_specs=(
            P(("req", "exp"), None),
            P(("req", "exp"), None),
            P("exp", None),
            P(),
            P(("req", "exp"), None),
            P(("req", "exp"), None),
            P("exp", None, None),
            P("exp", None, None),
            P("exp", None, None),
            P(None, "req"),
            P(None, "req"),
            P(None, "req"),
        ),
        out_specs=P(("req", "exp"), None),
        check_vma=False,
    )
```

```python
import functools

import jax
import jax.numpy as jnp
from jax import lax
from jax.experimental import pallas as pl
from jax.experimental.pallas import tpu as pltpu
from jax.sharding import PartitionSpec as P

F32 = jnp.float32
BF16 = jnp.bfloat16
VMEM_BYTES = 12 * 1024 * 1024
TILE = 512
TABLE_ROWS = 16


def ring_order(chips):
    slow = 4
    fast = chips // slow
    order = [a * fast for a in range(slow)]
    for turn, a in enumerate(reversed(range(slow))):
        inner = range(1, fast) if turn % 2 == 0 else range(fast - 1, 0, -1)
        order += [a * fast + b for b in inner]
    return order


def mm(a, b):
    return jnp.dot(a, b, preferred_element_type=F32)


def vmem():
    return pl.BlockSpec(memory_space=pltpu.VMEM)


def smem():
    return pl.BlockSpec(memory_space=pltpu.SMEM)


def hbm():
    return pl.BlockSpec(memory_space=pl.ANY)


def params():
    return pltpu.CompilerParams(vmem_limit_bytes=VMEM_BYTES)


def prepare_kernel(part, where_ref, ids_hbm, factors_hbm, weight_hbm, own_ref, sent_ref, ids_ref, factors_ref, sems):
    wrows, width = weight_hbm.shape
    topk, rows = ids_ref.shape
    core, request = where_ref[1], where_ref[2]
    small = [
        pltpu.make_async_copy(ids_hbm, ids_ref, sems.at[2]),
        pltpu.make_async_copy(factors_hbm, factors_ref, sems.at[3]),
    ]
    large = []
    for i, (ref, which) in enumerate(((own_ref, core), (sent_ref, 1 - core))):
        start = pl.multiple_of(which * (width // 2) + request * part, 128)
        large.append(pltpu.make_async_copy(weight_hbm.at[:, pl.ds(start, part)], ref.at[:wrows], sems.at[i]))
    for copy in small + large:
        copy.start()
    for copy in small:
        copy.wait()
    per_row = part // rows
    factors = factors_ref[...]
    big = factors.astype(BF16).astype(F32)
    middle = (factors - big).astype(BF16).astype(F32)
    named = (ids_ref[...].astype(F32), big, middle, factors - big - middle)
    items = [kind[k : k + 1] for kind in named for k in range(topk)]
    items += [jnp.zeros((1, rows), F32)] * (-len(items) % per_row)
    lines = [jnp.concatenate(items[i : i + per_row], axis=1) for i in range(0, len(items), per_row)]
    lines.append(jnp.zeros((TABLE_ROWS - len(lines), part), F32))
    table = jnp.concatenate(lines, axis=0).astype(BF16)
    own_ref[wrows:] = table
    sent_ref[wrows:] = table
    for copy in large:
        copy.wait()


def prepare(part, where, ids, factors, weight):
    shape = jax.ShapeDtypeStruct((weight.shape[0] + TABLE_ROWS, part), BF16)
    arrays = [pltpu.with_memory_space_constraint(x, pltpu.HBM) for x in (ids, factors, weight)]
    return pl.pallas_call(
        functools.partial(prepare_kernel, part),
        out_shape=[shape] * 2,
        in_specs=[smem()] + [hbm()] * 3,
        out_specs=[vmem()] * 2,
        scratch_shapes=[
            pltpu.VMEM(ids.shape, ids.dtype),
            pltpu.VMEM(factors.shape, factors.dtype),
            pltpu.SemaphoreType.DMA((4,)),
        ],
        compiler_params=params(),
        cost_estimate=pl.CostEstimate(flops=0, bytes_accessed=2 * weight.size, transcendentals=0),
        name="prepare",
    )(where, *arrays)


def small_call(kernel, name, shapes, operands, moved):
    return pl.pallas_call(
        kernel,
        out_shape=shapes,
        in_specs=[smem()] + [vmem()] * (len(operands) - 1),
        out_specs=[vmem()] * len(shapes),
        compiler_params=params(),
        cost_estimate=pl.CostEstimate(flops=0, bytes_accessed=moved, transcendentals=0),
        name=name,
    )(*operands)


def join_kernel(where_ref, mine_ref, other_ref, out_ref):
    rows = mine_ref.shape[0]
    core = where_ref[1]
    out_ref[pl.ds(pl.multiple_of(core * rows, 16), rows)] = mine_ref[...]
    out_ref[pl.ds(pl.multiple_of((1 - core) * rows, 16), rows)] = other_ref[...]


def join(where, mine, other):
    shape = jax.ShapeDtypeStruct((2 * mine.shape[0], mine.shape[1]), mine.dtype)
    return small_call(join_kernel, "join", [shape], [where, mine, other], 8 * mine.size)[0]


def pack_kernel(count, part, where_ref, attn_hbm, residual_hbm, *refs):
    width = attn_hbm.shape[1]
    outs, sems = refs[:-1], refs[-1]
    copies = []
    for shift, out_ref in enumerate(outs):
        moves = [(attn_hbm, out_ref.at[:, :width])]
        request = lax.rem(where_ref[2] + shift, count)
        for core in range(2):
            start = pl.multiple_of(core * (width // 2) + request * part, 128)
            target = out_ref.at[:, width + core * part : width + (core + 1) * part]
            moves.append((residual_hbm.at[:, pl.ds(start, part)], target))
        for i, (source, target) in enumerate(moves):
            copies.append(pltpu.make_async_copy(source, target, sems.at[3 * shift + i]))
    for copy in copies:
        copy.start()
    for copy in copies:
        copy.wait()


def pack(count, part, where, attn, residual):
    rows, width = attn.shape
    arrays = [pltpu.with_memory_space_constraint(x, pltpu.HBM) for x in (attn, residual)]
    return pl.pallas_call(
        functools.partial(pack_kernel, count, part),
        out_shape=[jax.ShapeDtypeStruct((rows, width + 2 * part), BF16)] * count,
        in_specs=[smem(), hbm(), hbm()],
        out_specs=[vmem()] * count,
        scratch_shapes=[pltpu.SemaphoreType.DMA((3 * count,))],
        compiler_params=params(),
        cost_estimate=pl.CostEstimate(flops=0, bytes_accessed=4 * attn.size * count, transcendentals=0),
        name="pack",
    )(where, *arrays)


def beside_kernel(where_ref, *refs):
    part = refs[0].shape[1]
    for i, ref in enumerate(refs[:-1]):
        refs[-1][:, i * part : (i + 1) * part] = ref[...]


def beside(where, pieces):
    rows, part = pieces[0].shape
    shape = jax.ShapeDtypeStruct((rows, len(pieces) * part), BF16)
    return small_call(beside_kernel, "beside", [shape], [where] + pieces, 4 * rows * part * len(pieces))[0]


def weave_kernel(count, where_ref, *refs):
    out_ref = refs[-1]
    part = out_ref.shape[1] // (2 * count)
    place = 0
    for ref in refs[:-1]:
        for at in range(ref.shape[1] // (2 * part)):
            request = lax.rem(where_ref[2] + place, count)
            place += 1
            for swap in range(2):
                core = where_ref[1] if swap == 0 else 1 - where_ref[1]
                start = pl.multiple_of(core * (count * part) + request * part, 128)
                out_ref[:, pl.ds(start, part)] = ref[:, (2 * at + swap) * part : (2 * at + swap + 1) * part]


def weave(count, where, pieces):
    rows = pieces[0].shape[0]
    width = sum(p.shape[1] for p in pieces)
    shape = jax.ShapeDtypeStruct((rows, width), BF16)
    return small_call(functools.partial(weave_kernel, count), "weave", [shape], [where] + pieces, 4 * rows * width)[0]


def proj_kernel(wrows, part, blocks, visits, final, where_ref, ring_ref, *refs):
    total = None
    rows_refs = refs[:visits]
    width = rows_refs[0].shape[1] - 2 * part
    at = visits
    chips = ring_ref.shape[0] // 2
    position = ring_ref[where_ref[0] // 2]
    for offset, pieces in blocks:
        chip = ring_ref[chips + lax.rem(position + offset + chips, chips)]
        start = pl.multiple_of(chip * 2 * wrows, 128)
        columns = jnp.concatenate([r[:, pl.ds(start, 2 * wrows)] for r in rows_refs], axis=0)
        step = wrows + TABLE_ROWS
        if pieces == 1:
            parts = [refs[at][i * step : i * step + wrows] for i in range(2)]
        else:
            parts = [refs[at + i][:wrows] for i in range(2)]
        at += pieces
        term = mm(columns, jnp.concatenate(parts, axis=0))
        total = term if total is None else total + term
    if final:
        total = total + refs[at][...]
        start = pl.multiple_of(width + where_ref[1] * part, 128)
        rows = rows_refs[0].shape[0]
        for i, out_ref in enumerate(refs[at + 1 :]):
            residual = rows_refs[i][:, pl.ds(start, part)].astype(F32)
            out_ref[...] = (residual + total[i * rows : (i + 1) * rows]).astype(BF16)
    else:
        refs[at][...] = total


def proj(wrows, blocks, where, ring, visits, weights, acc=None):
    final = acc is not None
    rows, part = visits[0].shape[0], weights[0].shape[1]
    operands = [where, ring] + visits + weights + ([acc] if final else [])
    count = len(visits)
    if final:
        outs = [jax.ShapeDtypeStruct((rows, part), BF16)] * count
    else:
        outs = [jax.ShapeDtypeStruct((rows * count, part), F32)]
    return pl.pallas_call(
        functools.partial(proj_kernel, wrows, part, blocks, count, final),
        out_shape=outs,
        in_specs=[smem()] * 2 + [vmem()] * (len(operands) - 2),
        out_specs=[vmem()] * len(outs),
        compiler_params=params(),
        cost_estimate=pl.CostEstimate(
            flops=8 * rows * count * part * wrows * len(blocks),
            bytes_accessed=4 * part * wrows * len(blocks) + 8 * rows * count * part,
            transcendentals=0,
        ),
        name="proj_final" if final else "proj_part",
    )(*operands)


def tables_kernel(wrows, slots, topk, rows, pieces, where_ref, *refs):
    pick_ref, put_ref, factor_ref = refs[-3:]
    both = 2 * rows
    expert_id = where_ref[0].astype(F32)
    first_core = where_ref[1] == 0
    row_of = lax.broadcasted_iota(jnp.int32, (both, both), 0)
    row_at = lax.broadcasted_iota(jnp.int32, (both, both), 1)
    slot_of = lax.broadcasted_iota(jnp.int32, (slots, both), 0).astype(F32)
    slot_at = lax.broadcasted_iota(jnp.int32, (both, slots), 1).astype(F32)
    step = wrows + TABLE_ROWS
    at = 0
    for block in range(pick_ref.shape[0]):
        if pieces[block] == 1:
            named = [refs[at][i * step + wrows : (i + 1) * step] for i in range(2)]
        else:
            named = [refs[at + i][wrows:] for i in range(2)]
        at += pieces[block]
        named = [n.astype(F32) for n in named]
        ordered = [jnp.where(first_core, named[0], named[1]), jnp.where(first_core, named[1], named[0])]
        per_row = named[0].shape[1] // rows
        selected, factor = [], []
        for n in ordered:
            item = [n[i // per_row : i // per_row + 1, (i % per_row) * rows : (i % per_row + 1) * rows] for i in range(4 * topk)]
            hits = [item[k] == expert_id for k in range(topk)]
            values = [item[topk + k] + item[2 * topk + k] + item[3 * topk + k] for k in range(topk)]
            selected.append(sum(h.astype(F32) for h in hits))
            factor.append(sum(jnp.where(h, v, 0.0) for h, v in zip(hits, values)))
        selected = jnp.concatenate(selected, axis=1)
        factor = jnp.concatenate(factor, axis=1)
        spread = jnp.broadcast_to(selected, (both, both))
        before = jnp.sum(jnp.where(row_at < row_of, spread, 0.0), axis=1, keepdims=True)
        selected_down = jnp.sum(jnp.where(row_at == row_of, spread, 0.0), axis=1, keepdims=True)
        slot_down = jnp.where(selected_down > 0.0, before, -1.0)
        put_ref[block] = (slot_at == slot_down).astype(F32).astype(BF16)
        slot = jnp.sum(jnp.where(row_at == row_of, jnp.broadcast_to(slot_down, (both, both)), 0.0), axis=0, keepdims=True)
        taken = slot_of == slot
        pick_ref[block] = taken.astype(F32).astype(BF16)
        factor_ref[block] = jnp.sum(jnp.where(taken, factor, 0.0), axis=1, keepdims=True)


def tables(wrows, slots, topk, rows, where, pieces, blocks):
    chips = len(pieces)
    both = 2 * rows
    return pl.pallas_call(
        functools.partial(tables_kernel, wrows, slots, topk, rows, pieces),
        out_shape=[
            jax.ShapeDtypeStruct((chips, slots, both), BF16),
            jax.ShapeDtypeStruct((chips, both, slots), BF16),
            jax.ShapeDtypeStruct((chips, slots, 1), F32),
        ],
        in_specs=[smem()] + [vmem()] * len(blocks),
        out_specs=[vmem()] * 3,
        compiler_params=params(),
        cost_estimate=pl.CostEstimate(flops=0, bytes_accessed=8 * chips * slots * both, transcendentals=0),
        name="tables",
    )(where, *blocks)


def expert_kernel(first, blocks, pieces, gain_ref, pick_ref, put_ref, factor_ref, gate_ref, up_ref, down_ref, *refs):
    slots, rows = pick_ref.shape[1:]
    own = rows // 2
    width = gain_ref.shape[1]
    hidden_units = gate_ref.shape[1]
    inputs = refs[: blocks * pieces]
    mine = refs[blocks * pieces : blocks * pieces + blocks]
    theirs, normed, hidden = refs[-3:]

    for b in range(blocks):
        block = jnp.concatenate([inputs[b * pieces + i][...] for i in range(pieces)], axis=0)
        taken = mm(pick_ref[first + b], block)
        scale = lax.rsqrt(jnp.sum(taken * taken, axis=1, keepdims=True) * (1.0 / width) + 1e-06)
        normed[b * slots : (b + 1) * slots, :] = (taken * scale * gain_ref[...]).astype(BF16)

    for start in range(0, hidden_units, TILE):
        columns = slice(start, min(start + TILE, hidden_units))
        gate_part = mm(normed[...], gate_ref[:, columns])
        up_part = mm(normed[...], up_ref[:, columns])
        hidden[:, columns] = (jax.nn.silu(gate_part) * up_part).astype(BF16)

    for start in range(0, width, TILE):
        columns = slice(start, start + TILE)
        result = mm(hidden[...], down_ref[:, columns])
        for b in range(blocks):
            weighted = (result[b * slots : (b + 1) * slots] * factor_ref[first + b]).astype(BF16)
            placed = mm(put_ref[first + b], weighted).astype(BF16)
            mine[b][:, columns] = placed[:own]
            theirs[b * own : (b + 1) * own, columns] = placed[own:]


def expert(first, blocks, tabs, gain, weights, inputs):
    slots, rows = tabs[0].shape[1:]
    width, hidden_units = weights[0].shape
    own = rows // 2
    m = blocks * slots
    weights = [pltpu.with_memory_space_constraint(w, pltpu.VMEM) for w in weights]
    out = pl.pallas_call(
        functools.partial(expert_kernel, first, blocks, len(inputs) // blocks),
        out_shape=[jax.ShapeDtypeStruct((own, width), BF16)] * blocks
        + [jax.ShapeDtypeStruct((blocks * own, width), BF16)],
        in_specs=[vmem()] * (7 + len(inputs)),
        out_specs=[vmem()] * (blocks + 1),
        scratch_shapes=[
            pltpu.VMEM((m, width), BF16),
            pltpu.VMEM((m, hidden_units), BF16),
        ],
        compiler_params=params(),
        cost_estimate=pl.CostEstimate(
            flops=12 * m * width * hidden_units,
            bytes_accessed=8 * blocks * rows * width,
            transcendentals=m * hidden_units,
        ),
        name="expert",
    )(gain, *tabs, *weights, *inputs)
    return out[:-1], out[-1]


def shared_kernel(count, gain_ref, gate_hbm, up_hbm, down_hbm, *refs):
    inputs, outs = refs[:count], refs[count : 2 * count]
    gate_ref, up_ref, down_ref, normed, hidden, sems = refs[2 * count :]
    units, width = gate_ref.shape
    rows = inputs[0].shape[0]
    tiles = [(start, min(256, units - start)) for start in range(0, units, 256)]
    copies = []
    for i, (start, size) in enumerate(tiles):
        span = pl.ds(start, size)
        for j, (source, target) in enumerate(((gate_hbm, gate_ref), (up_hbm, up_ref))):
            copies.append(pltpu.make_async_copy(source.at[span], target.at[span], sems.at[2 * i + j]))
    copies.append(pltpu.make_async_copy(down_hbm, down_ref, sems.at[2 * len(tiles)]))
    for copy in copies:
        copy.start()
    for i, ref in enumerate(inputs):
        x = ref[...].astype(F32)
        scale = lax.rsqrt(jnp.sum(x * x, axis=1, keepdims=True) * (1.0 / width) + 1e-06)
        normed[i * rows : (i + 1) * rows] = (x * scale * gain_ref[...]).astype(BF16)
    across = (((1,), (1,)), ((), ()))
    for i, (start, size) in enumerate(tiles):
        span = slice(start, start + size)
        copies[2 * i].wait()
        copies[2 * i + 1].wait()
        gate_part = lax.dot_general(normed[...], gate_ref[span], across, preferred_element_type=F32)
        up_part = lax.dot_general(normed[...], up_ref[span], across, preferred_element_type=F32)
        hidden[:, span] = (jax.nn.silu(gate_part) * up_part).astype(BF16)
    copies[-1].wait()
    for start in range(0, width, TILE):
        span = slice(start, start + TILE)
        result = mm(hidden[...], down_ref[:, span])
        for i, ref in enumerate(outs):
            ref[:, span] = result[i * rows : (i + 1) * rows].astype(ref.dtype)


def shared_expert(gain, weights, inputs):
    count = len(inputs)
    rows, width = inputs[0].shape
    units = weights[0].shape[0]
    weights = [pltpu.with_memory_space_constraint(w, pltpu.HBM) for w in weights]
    shapes = [jax.ShapeDtypeStruct((rows, width), F32)] + [jax.ShapeDtypeStruct((rows, width), BF16)] * (count - 1)
    return pl.pallas_call(
        functools.partial(shared_kernel, count),
        out_shape=shapes,
        in_specs=[vmem()] + [hbm()] * 3 + [vmem()] * count,
        out_specs=[vmem()] * count,
        scratch_shapes=[pltpu.VMEM((units, width), BF16)] * 3
        + [
            pltpu.VMEM((count * rows, width), BF16),
            pltpu.VMEM((count * rows, units), BF16),
            pltpu.SemaphoreType.DMA((2 * -(-units // 256) + 1,)),
        ],
        compiler_params=pltpu.CompilerParams(vmem_limit_bytes=24 * 1024 * 1024),
        cost_estimate=pl.CostEstimate(
            flops=12 * count * rows * width * units,
            bytes_accessed=6 * units * width + 4 * count * rows * width,
            transcendentals=count * rows * units,
        ),
        name="shared",
    )(gain, *weights, *inputs)


def base_kernel(*refs):
    total = refs[0][...]
    for ref in refs[1:-1]:
        total = total + ref[...].astype(F32)
    refs[-1][...] = total


def final_kernel(chunks, base_ref, *refs):
    out_ref = refs[-1]
    rows = refs[0].shape[0]
    for chunk in range(chunks):
        span = slice(chunk * rows, (chunk + 1) * rows)
        total = base_ref[span] + refs[chunk][...].astype(F32) + refs[chunks + chunk][...].astype(F32)
        out_ref[span] = total.astype(BF16)


def plain_call(kernel, name, shape, operands):
    return pl.pallas_call(
        kernel,
        out_shape=shape,
        in_specs=[vmem()] * len(operands),
        out_specs=vmem(),
        compiler_params=params(),
        cost_estimate=pl.CostEstimate(flops=0, bytes_accessed=8 * operands[0].size, transcendentals=0),
        name=name,
    )(*operands)


def add_kernel(*refs):
    total = refs[0][...].astype(F32)
    for ref in refs[1:-1]:
        total = total + ref[...].astype(F32)
    refs[-1][...] = total.astype(BF16)


def add(rows, *terms):
    width = terms[0][0].shape[1]

    def block(index):
        return pl.BlockSpec((rows, width), lambda i: (index, 0))

    return pl.pallas_call(
        add_kernel,
        grid=(1,),
        out_shape=jax.ShapeDtypeStruct((rows, width), BF16),
        in_specs=[block(index) for _, index in terms],
        out_specs=block(0),
        compiler_params=params(),
        cost_estimate=pl.CostEstimate(
            flops=rows * width * len(terms), bytes_accessed=2 * rows * width * (len(terms) + 1), transcendentals=0
        ),
        name="add",
    )(*[array for array, _ in terms])


def body(
    req_size,
    exp_size,
    attn_out,
    residual,
    out_weight,
    norm_gain,
    expert_ids,
    gate_weights,
    expert_gate,
    expert_up,
    expert_down,
    shared_gate,
    shared_up,
    shared_down,
):
    rows, width = attn_out.shape
    half = width // 2
    part = half // req_size
    topk = expert_ids.shape[1]
    wrows = out_weight.shape[0]
    capacity = min(rows, 3 * rows * topk // (2 * exp_size))
    slots = -(-2 * capacity // 16) * 16
    chips = exp_size // 2
    depth = chips // 2
    order = ring_order(chips)
    me = lax.axis_index("exp")
    request = lax.axis_index("req")
    here = jnp.stack([me, me % 2, lax.axis_index("req")]).astype(jnp.int32)
    ring = jnp.asarray([order.index(q) for q in range(chips)] + order, jnp.int32)

    steps = [(order[i], order[(i + 1) % chips]) for i in range(chips)]
    ahead = [(2 * a + c, 2 * b + c) for a, b in steps for c in range(2)]
    behind = [(b, a) for a, b in ahead]

    def to_ahead(x):
        return lax.ppermute(x, "exp", ahead)

    def to_behind(x):
        return lax.ppermute(x, "exp", behind)

    def to_core(x):
        return lax.ppermute(x, "exp", [(d, d ^ 1) for d in range(exp_size)])

    def to_request(x, shift, swap=0):
        pairs = [
            (i * exp_size + d, ((i + shift) % req_size) * exp_size + (d ^ swap))
            for i in range(req_size)
            for d in range(exp_size)
        ]
        return lax.ppermute(x, ("req", "exp"), pairs)

    weight_own, weight_sent = prepare(part, here, expert_ids.T, gate_weights.T, out_weight)
    weight = join(here, weight_own, to_core(weight_sent))
    low = high = weight
    pairs = []
    for _ in range(1, depth):
        low, high = to_ahead(low), to_behind(high)
        pairs.append((low, high))
    cut = wrows + TABLE_ROWS
    last = [to_ahead(low[:cut]), to_behind(high[cut:])]

    weight, attn_out, residual = lax.optimization_barrier((weight, attn_out, residual))
    packed = pack(req_size, part, here, attn_out, residual)
    visits = [packed[0]] + [to_request(packed[shift], shift) for shift in range(1, req_size)]
    passed = min(1, depth - 2)
    pairs[passed], visits[1:] = lax.optimization_barrier((pairs[passed], visits[1:]))
    visits += [to_core(v) for v in visits]

    early = [weight] + [w for pair in pairs[:-1] for w in pair]
    late = last + list(pairs[-1])
    tabs_early = tables(wrows, slots, topk, rows, here, [1] * (chips - 3), early)
    whole = early + list(pairs[-1])
    places = [(0, 1)] + [(side * k, 1) for k in range(1, depth) for side in (-1, 1)]
    (acc,) = proj(wrows, places, here, ring, visits, whole)
    acc, tabs_early = lax.optimization_barrier((acc, tabs_early))
    product = proj(wrows, [(depth, 2)], here, ring, visits, last, acc)
    tabs_late = tables(wrows, slots, topk, rows, here, [2, 1, 1], late)

    got = {}
    for shift in reversed(range(req_size)):
        for swap in range(2):
            piece = product[swap * req_size + shift]
            if shift == 0:
                got[shift, swap] = piece if swap == 0 else to_core(piece)
            else:
                got[shift, swap] = to_request(piece, req_size - shift, swap)
    near = beside(here, [got[0, 0], got[0, 1]])
    far, tabs_late = lax.optimization_barrier(
        ([got[place, swap] for place in range(1, req_size) for swap in range(2)], tabs_late)
    )
    far = beside(here, far)
    gain = norm_gain.reshape(1, width)
    weights = [expert_gate[0], expert_up[0], expert_down[0]]

    lows, highs = [to_ahead(near)], [to_behind(near)]
    lows, highs, far = lax.optimization_barrier((lows, highs, far))
    lows.append(to_ahead(far))
    highs.append(to_behind(far))
    own_rows = weave(req_size, here, [near, far])
    results = {0: expert(0, 1, tabs_early, gain, weights, [own_rows, to_core(own_rows)])}
    lows, highs, results[0] = lax.optimization_barrier((lows, highs, results[0]))
    low, high = weave(req_size, here, lows), weave(req_size, here, highs)
    shared_rows = [own_rows]
    for shift in range(1, req_size):
        shared_rows.append(to_request(own_rows, shift))
    for k in range(1, depth):
        if k > 1:
            low, high, results[k - 1] = lax.optimization_barrier((low, high, results[k - 1]))
        if k == depth - 1:
            low, high, shared_rows = lax.optimization_barrier((low, high, shared_rows))
        first, tabs = (2 * k - 1, tabs_early) if k < depth - 1 else (1, tabs_late)
        results[k] = expert(first, 2, tabs, gain, weights, [low, to_core(low), high, to_core(high)])
        if k < depth - 1:
            low, high = to_ahead(low), to_behind(high)
        else:
            low, high = to_ahead(low[: rows // 2]), to_behind(high[rows // 2 :])
    low, high, results[depth - 1] = lax.optimization_barrier((low, high, results[depth - 1]))
    results[depth] = expert(0, 1, tabs_late, gain, weights, [low, high, to_core(low), to_core(high)])

    shared_rows, results[depth] = lax.optimization_barrier((shared_rows, results[depth]))
    shared = shared_expert(gain, [shared_gate.T, shared_up.T, shared_down.T], shared_rows)

    cut = rows // 2
    low, high = [None, None], [None, None]
    for k in range(depth - 1, 0, -1):
        (low_mine, high_mine), theirs = results[k]
        came = to_core(theirs)

        def send_low(chunk):
            terms = [(low_mine, chunk), (came, chunk)] + [(low[chunk], 0)] * (low[chunk] is not None)
            low[chunk] = to_behind(add(cut, *terms))

        def send_high(chunk):
            terms = [(high_mine, chunk), (came, 2 + chunk)] + [(high[chunk], 0)] * (high[chunk] is not None)
            high[chunk] = to_ahead(add(cut, *terms))

        if k == depth - 1:
            send_low(0)
            send_high(1)
            results[depth], low[0], high[1] = lax.optimization_barrier((results[depth], low[0], high[1]))
            (mine,), theirs = results[depth]
            far = to_core(theirs)
            low[1] = to_behind(add(cut, (mine, 1), (far, 1)))
            high[0] = to_ahead(add(cut, (mine, 0), (far, 0)))
            send_low(1)
            send_high(0)
            continue
        if k == depth - 2:
            low[1], shared = lax.optimization_barrier((low[1], shared))
        for chunk in range(2):
            send_low(chunk)
            send_high(1 - chunk)
    (mine,), theirs = results[0]
    backs = [to_request(shared[shift], req_size - shift) for shift in range(1, req_size)]
    terms = [shared[0], own_rows, mine, to_core(theirs)] + backs
    base = plain_call(base_kernel, "base", jax.ShapeDtypeStruct((rows, width), F32), terms)
    return plain_call(
        functools.partial(final_kernel, 2), "final", jax.ShapeDtypeStruct((rows, width), BF16), [base] + low + high
    )


def solution(mesh):
    return jax.shard_map(
        functools.partial(body, mesh.shape["req"], mesh.shape["exp"]),
        mesh=mesh,
        in_specs=(
            P(("req", "exp"), None),
            P(("req", "exp"), None),
            P("exp", None),
            P(),
            P(("req", "exp"), None),
            P(("req", "exp"), None),
            P("exp", None, None),
            P("exp", None, None),
            P("exp", None, None),
            P(None, "req"),
            P(None, "req"),
            P(None, "req"),
        ),
        out_specs=P(("req", "exp"), None),
        check_vma=False,
    )
```

```python
import functools

import jax
import jax.numpy as jnp
from jax import lax
from jax.experimental import pallas as pl
from jax.experimental.pallas import tpu as pltpu
from jax.sharding import PartitionSpec as P

F32 = jnp.float32
BF16 = jnp.bfloat16
VMEM_BYTES = 12 * 1024 * 1024
TILE = 512
TABLE_ROWS = 16


def ring_order(chips):
    slow = 4
    fast = chips // slow
    order = [a * fast for a in range(slow)]
    for turn, a in enumerate(reversed(range(slow))):
        inner = range(1, fast) if turn % 2 == 0 else range(fast - 1, 0, -1)
        order += [a * fast + b for b in inner]
    return order


def mm(a, b):
    return jnp.dot(a, b, preferred_element_type=F32)


def vmem():
    return pl.BlockSpec(memory_space=pltpu.VMEM)


def smem():
    return pl.BlockSpec(memory_space=pltpu.SMEM)


def hbm():
    return pl.BlockSpec(memory_space=pl.ANY)


def params():
    return pltpu.CompilerParams(vmem_limit_bytes=VMEM_BYTES)


def prepare_kernel(part, where_ref, ids_hbm, factors_hbm, weight_hbm, own_ref, sent_ref, ids_ref, factors_ref, sems):
    wrows, width = weight_hbm.shape
    topk, rows = ids_ref.shape
    core, request = where_ref[1], where_ref[2]
    small = [
        pltpu.make_async_copy(ids_hbm, ids_ref, sems.at[2]),
        pltpu.make_async_copy(factors_hbm, factors_ref, sems.at[3]),
    ]
    large = []
    for i, (ref, which) in enumerate(((own_ref, core), (sent_ref, 1 - core))):
        start = pl.multiple_of(which * (width // 2) + request * part, 128)
        large.append(pltpu.make_async_copy(weight_hbm.at[:, pl.ds(start, part)], ref.at[:wrows], sems.at[i]))
    for copy in small + large:
        copy.start()
    for copy in small:
        copy.wait()
    per_row = part // rows
    factors = factors_ref[...]
    big = factors.astype(BF16).astype(F32)
    middle = (factors - big).astype(BF16).astype(F32)
    named = (ids_ref[...].astype(F32), big, middle, factors - big - middle)
    items = [kind[k : k + 1] for kind in named for k in range(topk)]
    items += [jnp.zeros((1, rows), F32)] * (-len(items) % per_row)
    lines = [jnp.concatenate(items[i : i + per_row], axis=1) for i in range(0, len(items), per_row)]
    lines.append(jnp.zeros((TABLE_ROWS - len(lines), part), F32))
    table = jnp.concatenate(lines, axis=0).astype(BF16)
    own_ref[wrows:] = table
    sent_ref[wrows:] = table
    for copy in large:
        copy.wait()


def prepare(part, where, ids, factors, weight):
    shape = jax.ShapeDtypeStruct((weight.shape[0] + TABLE_ROWS, part), BF16)
    arrays = [pltpu.with_memory_space_constraint(x, pltpu.HBM) for x in (ids, factors, weight)]
    return pl.pallas_call(
        functools.partial(prepare_kernel, part),
        out_shape=[shape] * 2,
        in_specs=[smem()] + [hbm()] * 3,
        out_specs=[vmem()] * 2,
        scratch_shapes=[
            pltpu.VMEM(ids.shape, ids.dtype),
            pltpu.VMEM(factors.shape, factors.dtype),
            pltpu.SemaphoreType.DMA((4,)),
        ],
        compiler_params=params(),
        cost_estimate=pl.CostEstimate(flops=0, bytes_accessed=2 * weight.size, transcendentals=0),
        name="prepare",
    )(where, *arrays)


def small_call(kernel, name, shapes, operands, moved):
    return pl.pallas_call(
        kernel,
        out_shape=shapes,
        in_specs=[smem()] + [vmem()] * (len(operands) - 1),
        out_specs=[vmem()] * len(shapes),
        compiler_params=params(),
        cost_estimate=pl.CostEstimate(flops=0, bytes_accessed=moved, transcendentals=0),
        name=name,
    )(*operands)


def pack_kernel(count, part, where_ref, attn_hbm, residual_hbm, *refs):
    width = attn_hbm.shape[1]
    outs, sems = refs[:-1], refs[-1]
    copies = []
    for shift, out_ref in enumerate(outs):
        moves = [(attn_hbm, out_ref.at[:, :width])]
        request = lax.rem(where_ref[2] + shift, count)
        for core in range(2):
            start = pl.multiple_of(core * (width // 2) + request * part, 128)
            target = out_ref.at[:, width + core * part : width + (core + 1) * part]
            moves.append((residual_hbm.at[:, pl.ds(start, part)], target))
        for i, (source, target) in enumerate(moves):
            copies.append(pltpu.make_async_copy(source, target, sems.at[3 * shift + i]))
    for copy in copies:
        copy.start()
    for copy in copies:
        copy.wait()


def pack(count, part, where, attn, residual):
    rows, width = attn.shape
    arrays = [pltpu.with_memory_space_constraint(x, pltpu.HBM) for x in (attn, residual)]
    return pl.pallas_call(
        functools.partial(pack_kernel, count, part),
        out_shape=[jax.ShapeDtypeStruct((rows, width + 2 * part), BF16)] * count,
        in_specs=[smem(), hbm(), hbm()],
        out_specs=[vmem()] * count,
        scratch_shapes=[pltpu.SemaphoreType.DMA((3 * count,))],
        compiler_params=params(),
        cost_estimate=pl.CostEstimate(flops=0, bytes_accessed=4 * attn.size * count, transcendentals=0),
        name="pack",
    )(where, *arrays)


def beside_kernel(where_ref, *refs):
    part = refs[0].shape[1]
    for i, ref in enumerate(refs[:-1]):
        refs[-1][:, i * part : (i + 1) * part] = ref[...]


def beside(where, pieces):
    rows, part = pieces[0].shape
    shape = jax.ShapeDtypeStruct((rows, len(pieces) * part), BF16)
    return small_call(beside_kernel, "beside", [shape], [where] + pieces, 4 * rows * part * len(pieces))[0]


def weave_kernel(count, where_ref, *refs):
    out_ref = refs[-1]
    part = out_ref.shape[1] // (2 * count)
    place = 0
    for ref in refs[:-1]:
        for at in range(ref.shape[1] // (2 * part)):
            request = lax.rem(where_ref[2] + place, count)
            place += 1
            for swap in range(2):
                core = where_ref[1] if swap == 0 else 1 - where_ref[1]
                start = pl.multiple_of(core * (count * part) + request * part, 128)
                out_ref[:, pl.ds(start, part)] = ref[:, (2 * at + swap) * part : (2 * at + swap + 1) * part]


def weave(count, where, pieces):
    rows = pieces[0].shape[0]
    width = sum(p.shape[1] for p in pieces)
    shape = jax.ShapeDtypeStruct((rows, width), BF16)
    return small_call(functools.partial(weave_kernel, count), "weave", [shape], [where] + pieces, 4 * rows * width)[0]


def proj_kernel(wrows, part, blocks, visits, final, where_ref, ring_ref, *refs):
    total = None
    rows_refs = refs[:visits]
    width = rows_refs[0].shape[1] - 2 * part
    at = visits
    chips = ring_ref.shape[0] // 2
    position = ring_ref[where_ref[0] // 2]
    first_core = where_ref[1] == 0
    for offset in blocks:
        chip = ring_ref[chips + lax.rem(position + offset + chips, chips)]
        start = pl.multiple_of(chip * 2 * wrows, 128)
        columns = jnp.concatenate([r[:, pl.ds(start, 2 * wrows)] for r in rows_refs], axis=0)
        mine, other = refs[at][:wrows], refs[at + 1][:wrows]
        at += 2
        weight = jnp.concatenate([jnp.where(first_core, mine, other), jnp.where(first_core, other, mine)], axis=0)
        term = mm(columns, weight)
        total = term if total is None else total + term
    if final:
        total = total + refs[at][...]
        start = pl.multiple_of(width + where_ref[1] * part, 128)
        rows = rows_refs[0].shape[0]
        for i, out_ref in enumerate(refs[at + 1 :]):
            residual = rows_refs[i][:, pl.ds(start, part)].astype(F32)
            out_ref[...] = (residual + total[i * rows : (i + 1) * rows]).astype(BF16)
    else:
        refs[at][...] = total


def proj(wrows, blocks, where, ring, visits, weights, acc=None):
    final = acc is not None
    rows, part = visits[0].shape[0], weights[0].shape[1]
    operands = [where, ring] + visits + weights + ([acc] if final else [])
    count = len(visits)
    if final:
        outs = [jax.ShapeDtypeStruct((rows, part), BF16)] * count
    else:
        outs = [jax.ShapeDtypeStruct((rows * count, part), F32)]
    return pl.pallas_call(
        functools.partial(proj_kernel, wrows, part, blocks, count, final),
        out_shape=outs,
        in_specs=[smem()] * 2 + [vmem()] * (len(operands) - 2),
        out_specs=[vmem()] * len(outs),
        compiler_params=params(),
        cost_estimate=pl.CostEstimate(
            flops=8 * rows * count * part * wrows * len(blocks),
            bytes_accessed=4 * part * wrows * len(blocks) + 8 * rows * count * part,
            transcendentals=0,
        ),
        name="proj_final" if final else "proj_part",
    )(*operands)


def tables_kernel(wrows, slots, topk, rows, where_ref, *refs):
    pick_ref, put_ref, factor_ref = refs[-3:]
    both = 2 * rows
    expert_id = where_ref[0].astype(F32)
    row_of = lax.broadcasted_iota(jnp.int32, (both, both), 0)
    row_at = lax.broadcasted_iota(jnp.int32, (both, both), 1)
    slot_of = lax.broadcasted_iota(jnp.int32, (slots, both), 0).astype(F32)
    slot_at = lax.broadcasted_iota(jnp.int32, (both, slots), 1).astype(F32)
    for block in range(pick_ref.shape[0]):
        named = [refs[2 * block + i][wrows:].astype(F32) for i in range(2)]
        per_row = named[0].shape[1] // rows
        selected, factor = [], []
        for n in named:
            item = [n[i // per_row : i // per_row + 1, (i % per_row) * rows : (i % per_row + 1) * rows] for i in range(4 * topk)]
            hits = [item[k] == expert_id for k in range(topk)]
            values = [item[topk + k] + item[2 * topk + k] + item[3 * topk + k] for k in range(topk)]
            selected.append(sum(h.astype(F32) for h in hits))
            factor.append(sum(jnp.where(h, v, 0.0) for h, v in zip(hits, values)))
        selected = jnp.concatenate(selected, axis=1)
        factor = jnp.concatenate(factor, axis=1)
        spread = jnp.broadcast_to(selected, (both, both))
        before = jnp.sum(jnp.where(row_at < row_of, spread, 0.0), axis=1, keepdims=True)
        selected_down = jnp.sum(jnp.where(row_at == row_of, spread, 0.0), axis=1, keepdims=True)
        slot_down = jnp.where(selected_down > 0.0, before, -1.0)
        put_ref[block] = (slot_at == slot_down).astype(F32).astype(BF16)
        slot = jnp.sum(jnp.where(row_at == row_of, jnp.broadcast_to(slot_down, (both, both)), 0.0), axis=0, keepdims=True)
        taken = slot_of == slot
        pick_ref[block] = taken.astype(F32).astype(BF16)
        factor_ref[block] = jnp.sum(jnp.where(taken, factor, 0.0), axis=1, keepdims=True)


def tables(wrows, slots, topk, rows, where, blocks):
    chips = len(blocks) // 2
    both = 2 * rows
    return pl.pallas_call(
        functools.partial(tables_kernel, wrows, slots, topk, rows),
        out_shape=[
            jax.ShapeDtypeStruct((chips, slots, both), BF16),
            jax.ShapeDtypeStruct((chips, both, slots), BF16),
            jax.ShapeDtypeStruct((chips, slots, 1), F32),
        ],
        in_specs=[smem()] + [vmem()] * len(blocks),
        out_specs=[vmem()] * 3,
        compiler_params=params(),
        cost_estimate=pl.CostEstimate(flops=0, bytes_accessed=8 * chips * slots * both, transcendentals=0),
        name="tables",
    )(where, *blocks)


def expert_kernel(first, blocks, pieces, gain_ref, pick_ref, put_ref, factor_ref, gate_ref, up_ref, down_ref, *refs):
    slots, rows = pick_ref.shape[1:]
    own = rows // 2
    width = gain_ref.shape[1]
    hidden_units = gate_ref.shape[1]
    inputs = refs[: blocks * pieces]
    mine = refs[blocks * pieces : blocks * pieces + blocks]
    theirs, normed, hidden = refs[-3:]

    for b in range(blocks):
        block = jnp.concatenate([inputs[b * pieces + i][...] for i in range(pieces)], axis=0)
        taken = mm(pick_ref[first + b], block)
        scale = lax.rsqrt(jnp.sum(taken * taken, axis=1, keepdims=True) * (1.0 / width) + 1e-06)
        normed[b * slots : (b + 1) * slots, :] = (taken * scale * gain_ref[...]).astype(BF16)

    for start in range(0, hidden_units, TILE):
        columns = slice(start, min(start + TILE, hidden_units))
        gate_part = mm(normed[...], gate_ref[:, columns])
        up_part = mm(normed[...], up_ref[:, columns])
        hidden[:, columns] = (jax.nn.silu(gate_part) * up_part).astype(BF16)

    for start in range(0, width, TILE):
        columns = slice(start, start + TILE)
        result = mm(hidden[...], down_ref[:, columns])
        for b in range(blocks):
            weighted = (result[b * slots : (b + 1) * slots] * factor_ref[first + b]).astype(BF16)
            placed = mm(put_ref[first + b], weighted).astype(BF16)
            mine[b][:, columns] = placed[:own]
            theirs[b * own : (b + 1) * own, columns] = placed[own:]


def expert(first, blocks, tabs, gain, weights, inputs):
    slots, rows = tabs[0].shape[1:]
    width, hidden_units = weights[0].shape
    own = rows // 2
    m = blocks * slots
    weights = [pltpu.with_memory_space_constraint(w, pltpu.VMEM) for w in weights]
    out = pl.pallas_call(
        functools.partial(expert_kernel, first, blocks, len(inputs) // blocks),
        out_shape=[jax.ShapeDtypeStruct((own, width), BF16)] * blocks
        + [jax.ShapeDtypeStruct((blocks * own, width), BF16)],
        in_specs=[vmem()] * (7 + len(inputs)),
        out_specs=[vmem()] * (blocks + 1),
        scratch_shapes=[
            pltpu.VMEM((m, width), BF16),
            pltpu.VMEM((m, hidden_units), BF16),
        ],
        compiler_params=params(),
        cost_estimate=pl.CostEstimate(
            flops=12 * m * width * hidden_units,
            bytes_accessed=8 * blocks * rows * width,
            transcendentals=m * hidden_units,
        ),
        name="expert",
    )(gain, *tabs, *weights, *inputs)
    return out[:-1], out[-1]


def shared_kernel(count, gain_ref, gate_hbm, up_hbm, down_hbm, *refs):
    inputs, outs = refs[:count], refs[count : 2 * count]
    gate_ref, up_ref, down_ref, normed, hidden, sems = refs[2 * count :]
    units, width = gate_ref.shape
    rows = inputs[0].shape[0]
    tiles = [(start, min(256, units - start)) for start in range(0, units, 256)]
    copies = []
    for i, (start, size) in enumerate(tiles):
        span = pl.ds(start, size)
        for j, (source, target) in enumerate(((gate_hbm, gate_ref), (up_hbm, up_ref))):
            copies.append(pltpu.make_async_copy(source.at[span], target.at[span], sems.at[2 * i + j]))
    copies.append(pltpu.make_async_copy(down_hbm, down_ref, sems.at[2 * len(tiles)]))
    for copy in copies:
        copy.start()
    for i, ref in enumerate(inputs):
        x = ref[...].astype(F32)
        scale = lax.rsqrt(jnp.sum(x * x, axis=1, keepdims=True) * (1.0 / width) + 1e-06)
        normed[i * rows : (i + 1) * rows] = (x * scale * gain_ref[...]).astype(BF16)
    across = (((1,), (1,)), ((), ()))
    for i, (start, size) in enumerate(tiles):
        span = slice(start, start + size)
        copies[2 * i].wait()
        copies[2 * i + 1].wait()
        gate_part = lax.dot_general(normed[...], gate_ref[span], across, preferred_element_type=F32)
        up_part = lax.dot_general(normed[...], up_ref[span], across, preferred_element_type=F32)
        hidden[:, span] = (jax.nn.silu(gate_part) * up_part).astype(BF16)
    copies[-1].wait()
    for start in range(0, width, TILE):
        span = slice(start, start + TILE)
        result = mm(hidden[...], down_ref[:, span])
        for i, ref in enumerate(outs):
            ref[:, span] = result[i * rows : (i + 1) * rows].astype(ref.dtype)


def shared_expert(gain, weights, inputs):
    count = len(inputs)
    rows, width = inputs[0].shape
    units = weights[0].shape[0]
    weights = [pltpu.with_memory_space_constraint(w, pltpu.HBM) for w in weights]
    shapes = [jax.ShapeDtypeStruct((rows, width), F32)] + [jax.ShapeDtypeStruct((rows, width), BF16)] * (count - 1)
    return pl.pallas_call(
        functools.partial(shared_kernel, count),
        out_shape=shapes,
        in_specs=[vmem()] + [hbm()] * 3 + [vmem()] * count,
        out_specs=[vmem()] * count,
        scratch_shapes=[pltpu.VMEM((units, width), BF16)] * 3
        + [
            pltpu.VMEM((count * rows, width), BF16),
            pltpu.VMEM((count * rows, units), BF16),
            pltpu.SemaphoreType.DMA((2 * -(-units // 256) + 1,)),
        ],
        compiler_params=pltpu.CompilerParams(vmem_limit_bytes=24 * 1024 * 1024),
        cost_estimate=pl.CostEstimate(
            flops=12 * count * rows * width * units,
            bytes_accessed=6 * units * width + 4 * count * rows * width,
            transcendentals=count * rows * units,
        ),
        name="shared",
    )(gain, *weights, *inputs)


def base_kernel(*refs):
    total = refs[0][...]
    for ref in refs[1:-1]:
        total = total + ref[...].astype(F32)
    refs[-1][...] = total


def final_kernel(chunks, base_ref, *refs):
    out_ref = refs[-1]
    rows = refs[0].shape[0]
    for chunk in range(chunks):
        span = slice(chunk * rows, (chunk + 1) * rows)
        total = base_ref[span] + refs[chunk][...].astype(F32) + refs[chunks + chunk][...].astype(F32)
        out_ref[span] = total.astype(BF16)


def plain_call(kernel, name, shape, operands):
    return pl.pallas_call(
        kernel,
        out_shape=shape,
        in_specs=[vmem()] * len(operands),
        out_specs=vmem(),
        compiler_params=params(),
        cost_estimate=pl.CostEstimate(flops=0, bytes_accessed=8 * operands[0].size, transcendentals=0),
        name=name,
    )(*operands)


def add_kernel(*refs):
    total = refs[0][...].astype(F32)
    for ref in refs[1:-1]:
        total = total + ref[...].astype(F32)
    refs[-1][...] = total.astype(BF16)


def add(rows, *terms):
    width = terms[0][0].shape[1]

    def block(index):
        return pl.BlockSpec((rows, width), lambda i: (index, 0))

    return pl.pallas_call(
        add_kernel,
        grid=(1,),
        out_shape=jax.ShapeDtypeStruct((rows, width), BF16),
        in_specs=[block(index) for _, index in terms],
        out_specs=block(0),
        compiler_params=params(),
        cost_estimate=pl.CostEstimate(
            flops=rows * width * len(terms), bytes_accessed=2 * rows * width * (len(terms) + 1), transcendentals=0
        ),
        name="add",
    )(*[array for array, _ in terms])


def body(
    req_size,
    exp_size,
    attn_out,
    residual,
    out_weight,
    norm_gain,
    expert_ids,
    gate_weights,
    expert_gate,
    expert_up,
    expert_down,
    shared_gate,
    shared_up,
    shared_down,
):
    rows, width = attn_out.shape
    half = width // 2
    part = half // req_size
    topk = expert_ids.shape[1]
    wrows = out_weight.shape[0]
    capacity = min(rows, 3 * rows * topk // (2 * exp_size))
    slots = -(-2 * capacity // 16) * 16
    chips = exp_size // 2
    depth = chips // 2
    order = ring_order(chips)
    me = lax.axis_index("exp")
    request = lax.axis_index("req")
    here = jnp.stack([me, me % 2, lax.axis_index("req")]).astype(jnp.int32)
    ring = jnp.asarray([order.index(q) for q in range(chips)] + order, jnp.int32)

    steps = [(order[i], order[(i + 1) % chips]) for i in range(chips)]
    ahead = [(2 * a + c, 2 * b + c) for a, b in steps for c in range(2)]
    behind = [(b, a) for a, b in ahead]

    def to_ahead(x):
        return lax.ppermute(x, "exp", ahead)

    def to_behind(x):
        return lax.ppermute(x, "exp", behind)

    def to_core(x):
        return lax.ppermute(x, "exp", [(d, d ^ 1) for d in range(exp_size)])

    def to_request(x, shift, swap=0):
        pairs = [
            (i * exp_size + d, ((i + shift) % req_size) * exp_size + (d ^ swap))
            for i in range(req_size)
            for d in range(exp_size)
        ]
        return lax.ppermute(x, ("req", "exp"), pairs)

    weight_own, weight_sent = prepare(part, here, expert_ids.T, gate_weights.T, out_weight)
    weight_met = to_core(weight_sent)
    chains = [(weight_own, weight_own), (weight_met, weight_met)]
    arrived = [[weight_own, weight_met]]
    for _ in range(1, depth):
        chains = [(to_ahead(low), to_behind(high)) for low, high in chains]
        (low_own, high_own), (low_met, high_met) = chains
        arrived += [[low_own, low_met], [high_own, high_met]]

    weight_met, attn_out, residual = lax.optimization_barrier((weight_met, attn_out, residual))
    packed = pack(req_size, part, here, attn_out, residual)
    visits = [packed[0]] + [to_request(packed[shift], shift) for shift in range(1, req_size)]
    arrived[-2:], visits[1:] = lax.optimization_barrier((arrived[-2:], visits[1:]))
    visits += [to_core(v) for v in visits]
    last = [to_ahead(arrived[-2][0]), to_behind(arrived[-1][1])]

    early = [w for block in arrived[:-2] for w in block]
    late = last + [w for block in arrived[-2:] for w in block]
    tabs_early = tables(wrows, slots, topk, rows, here, early)
    whole = [w for block in arrived for w in block]
    places = [0] + [side * k for k in range(1, depth) for side in (-1, 1)]
    (acc,) = proj(wrows, places, here, ring, visits, whole)
    acc, tabs_early = lax.optimization_barrier((acc, tabs_early))
    product = proj(wrows, [depth], here, ring, visits, last, acc)
    tabs_late = tables(wrows, slots, topk, rows, here, late)

    got = {}
    for shift in reversed(range(req_size)):
        for swap in range(2):
            piece = product[swap * req_size + shift]
            if shift == 0:
                got[shift, swap] = piece if swap == 0 else to_core(piece)
            else:
                got[shift, swap] = to_request(piece, req_size - shift, swap)
    near = beside(here, [got[0, 0], got[0, 1]])
    far, tabs_late = lax.optimization_barrier(
        ([got[place, swap] for place in range(1, req_size) for swap in range(2)], tabs_late)
    )
    far = beside(here, far)
    gain = norm_gain.reshape(1, width)
    weights = [expert_gate[0], expert_up[0], expert_down[0]]

    lows, highs = [to_ahead(near)], [to_behind(near)]
    lows, highs, far = lax.optimization_barrier((lows, highs, far))
    lows.append(to_ahead(far))
    highs.append(to_behind(far))
    own_rows = weave(req_size, here, [near, far])
    results = {0: expert(0, 1, tabs_early, gain, weights, [own_rows, to_core(own_rows)])}
    lows, highs, results[0] = lax.optimization_barrier((lows, highs, results[0]))
    low, high = weave(req_size, here, lows), weave(req_size, here, highs)
    shared_rows = [own_rows]
    for shift in range(1, req_size):
        shared_rows.append(to_request(own_rows, shift))
    for k in range(1, depth):
        if k > 1:
            low, high, results[k - 1] = lax.optimization_barrier((low, high, results[k - 1]))
        if k == depth - 1:
            low, high, shared_rows = lax.optimization_barrier((low, high, shared_rows))
        first, tabs = (2 * k - 1, tabs_early) if k < depth - 1 else (1, tabs_late)
        results[k] = expert(first, 2, tabs, gain, weights, [low, to_core(low), high, to_core(high)])
        if k < depth - 1:
            low, high = to_ahead(low), to_behind(high)
        else:
            low, high = to_ahead(low[: rows // 2]), to_behind(high[rows // 2 :])
    low, high, results[depth - 1] = lax.optimization_barrier((low, high, results[depth - 1]))
    results[depth] = expert(0, 1, tabs_late, gain, weights, [low, high, to_core(low), to_core(high)])

    shared_rows, results[depth] = lax.optimization_barrier((shared_rows, results[depth]))
    shared = shared_expert(gain, [shared_gate.T, shared_up.T, shared_down.T], shared_rows)

    cut = rows // 2
    low, high = [None, None], [None, None]
    for k in range(depth - 1, 0, -1):
        (low_mine, high_mine), theirs = results[k]
        came = to_core(theirs)

        def send_low(chunk):
            terms = [(low_mine, chunk), (came, chunk)] + [(low[chunk], 0)] * (low[chunk] is not None)
            low[chunk] = to_behind(add(cut, *terms))

        def send_high(chunk):
            terms = [(high_mine, chunk), (came, 2 + chunk)] + [(high[chunk], 0)] * (high[chunk] is not None)
            high[chunk] = to_ahead(add(cut, *terms))

        if k == depth - 1:
            send_low(0)
            send_high(1)
            results[depth], low[0], high[1] = lax.optimization_barrier((results[depth], low[0], high[1]))
            (mine,), theirs = results[depth]
            far = to_core(theirs)
            low[1] = to_behind(add(cut, (mine, 1), (far, 1)))
            high[0] = to_ahead(add(cut, (mine, 0), (far, 0)))
            send_low(1)
            send_high(0)
            continue
        if k == depth - 2:
            low[1], shared = lax.optimization_barrier((low[1], shared))
        for chunk in range(2):
            send_low(chunk)
            send_high(1 - chunk)
    (mine,), theirs = results[0]
    backs = [to_request(shared[shift], req_size - shift) for shift in range(1, req_size)]
    terms = [shared[0], own_rows, mine, to_core(theirs)] + backs
    base = plain_call(base_kernel, "base", jax.ShapeDtypeStruct((rows, width), F32), terms)
    return plain_call(
        functools.partial(final_kernel, 2), "final", jax.ShapeDtypeStruct((rows, width), BF16), [base] + low + high
    )


def solution(mesh):
    return jax.shard_map(
        functools.partial(body, mesh.shape["req"], mesh.shape["exp"]),
        mesh=mesh,
        in_specs=(
            P(("req", "exp"), None),
            P(("req", "exp"), None),
            P("exp", None),
            P(),
            P(("req", "exp"), None),
            P(("req", "exp"), None),
            P("exp", None, None),
            P("exp", None, None),
            P("exp", None, None),
            P(None, "req"),
            P(None, "req"),
            P(None, "req"),
        ),
        out_specs=P(("req", "exp"), None),
        check_vma=False,
    )
```

```python
import functools

import jax
import jax.numpy as jnp
from jax import lax
from jax.experimental import pallas as pl
from jax.experimental.pallas import tpu as pltpu
from jax.sharding import PartitionSpec as P

F32 = jnp.float32
BF16 = jnp.bfloat16
VMEM_BYTES = 12 * 1024 * 1024
TILE = 512
TABLE_ROWS = 16


def ring_order(chips):
    slow = 4
    fast = chips // slow
    order = [a * fast for a in range(slow)]
    for turn, a in enumerate(reversed(range(slow))):
        inner = range(1, fast) if turn % 2 == 0 else range(fast - 1, 0, -1)
        order += [a * fast + b for b in inner]
    return order


def mm(a, b):
    return jnp.dot(a, b, preferred_element_type=F32)


def vmem():
    return pl.BlockSpec(memory_space=pltpu.VMEM)


def smem():
    return pl.BlockSpec(memory_space=pltpu.SMEM)


def hbm():
    return pl.BlockSpec(memory_space=pl.ANY)


def params():
    return pltpu.CompilerParams(vmem_limit_bytes=VMEM_BYTES)


def prepare_kernel(part, where_ref, ids_hbm, factors_hbm, weight_hbm, own_ref, sent_ref, ids_ref, factors_ref, sems):
    wrows, width = weight_hbm.shape
    topk, rows = ids_ref.shape
    core, request = where_ref[1], where_ref[2]
    small = [
        pltpu.make_async_copy(ids_hbm, ids_ref, sems.at[2]),
        pltpu.make_async_copy(factors_hbm, factors_ref, sems.at[3]),
    ]
    large = []
    for i, (ref, which) in enumerate(((own_ref, core), (sent_ref, 1 - core))):
        start = pl.multiple_of(which * (width // 2) + request * part, 128)
        large.append(pltpu.make_async_copy(weight_hbm.at[:, pl.ds(start, part)], ref.at[:wrows], sems.at[i]))
    for copy in small + large:
        copy.start()
    for copy in small:
        copy.wait()
    per_row = part // rows
    factors = factors_ref[...]
    big = factors.astype(BF16).astype(F32)
    middle = (factors - big).astype(BF16).astype(F32)
    named = (ids_ref[...].astype(F32), big, middle, factors - big - middle)
    items = [kind[k : k + 1] for kind in named for k in range(topk)]
    items += [jnp.zeros((1, rows), F32)] * (-len(items) % per_row)
    lines = [jnp.concatenate(items[i : i + per_row], axis=1) for i in range(0, len(items), per_row)]
    lines.append(jnp.zeros((TABLE_ROWS - len(lines), part), F32))
    table = jnp.concatenate(lines, axis=0).astype(BF16)
    own_ref[wrows:] = table
    sent_ref[wrows:] = table
    for copy in large:
        copy.wait()


def prepare(part, where, ids, factors, weight):
    shape = jax.ShapeDtypeStruct((weight.shape[0] + TABLE_ROWS, part), BF16)
    arrays = [pltpu.with_memory_space_constraint(x, pltpu.HBM) for x in (ids, factors, weight)]
    return pl.pallas_call(
        functools.partial(prepare_kernel, part),
        out_shape=[shape] * 2,
        in_specs=[smem()] + [hbm()] * 3,
        out_specs=[vmem()] * 2,
        scratch_shapes=[
            pltpu.VMEM(ids.shape, ids.dtype),
            pltpu.VMEM(factors.shape, factors.dtype),
            pltpu.SemaphoreType.DMA((4,)),
        ],
        compiler_params=params(),
        cost_estimate=pl.CostEstimate(flops=0, bytes_accessed=2 * weight.size, transcendentals=0),
        name="prepare",
    )(where, *arrays)


def small_call(kernel, name, shapes, operands, moved):
    return pl.pallas_call(
        kernel,
        out_shape=shapes,
        in_specs=[smem()] + [vmem()] * (len(operands) - 1),
        out_specs=[vmem()] * len(shapes),
        compiler_params=params(),
        cost_estimate=pl.CostEstimate(flops=0, bytes_accessed=moved, transcendentals=0),
        name=name,
    )(*operands)


def pack_kernel(count, part, where_ref, attn_hbm, residual_hbm, *refs):
    width = attn_hbm.shape[1]
    outs, sems = refs[:-1], refs[-1]
    copies = []
    for shift, out_ref in enumerate(outs):
        moves = [(attn_hbm, out_ref.at[:, :width])]
        request = lax.rem(where_ref[2] + shift, count)
        for core in range(2):
            start = pl.multiple_of(core * (width // 2) + request * part, 128)
            target = out_ref.at[:, width + core * part : width + (core + 1) * part]
            moves.append((residual_hbm.at[:, pl.ds(start, part)], target))
        for i, (source, target) in enumerate(moves):
            copies.append(pltpu.make_async_copy(source, target, sems.at[3 * shift + i]))
    for copy in copies:
        copy.start()
    for copy in copies:
        copy.wait()


def pack(count, part, where, attn, residual):
    rows, width = attn.shape
    arrays = [pltpu.with_memory_space_constraint(x, pltpu.HBM) for x in (attn, residual)]
    return pl.pallas_call(
        functools.partial(pack_kernel, count, part),
        out_shape=[jax.ShapeDtypeStruct((rows, width + 2 * part), BF16)] * count,
        in_specs=[smem(), hbm(), hbm()],
        out_specs=[vmem()] * count,
        scratch_shapes=[pltpu.SemaphoreType.DMA((3 * count,))],
        compiler_params=params(),
        cost_estimate=pl.CostEstimate(flops=0, bytes_accessed=4 * attn.size * count, transcendentals=0),
        name="pack",
    )(where, *arrays)


def beside_kernel(where_ref, *refs):
    part = refs[0].shape[1]
    for i, ref in enumerate(refs[:-1]):
        refs[-1][:, i * part : (i + 1) * part] = ref[...]


def beside(where, pieces):
    rows, part = pieces[0].shape
    shape = jax.ShapeDtypeStruct((rows, len(pieces) * part), BF16)
    return small_call(beside_kernel, "beside", [shape], [where] + pieces, 4 * rows * part * len(pieces))[0]


def weave_kernel(count, where_ref, *refs):
    out_ref = refs[-1]
    part = out_ref.shape[1] // (2 * count)
    place = 0
    for ref in refs[:-1]:
        for at in range(ref.shape[1] // (2 * part)):
            request = lax.rem(where_ref[2] + place, count)
            place += 1
            for swap in range(2):
                core = where_ref[1] if swap == 0 else 1 - where_ref[1]
                start = pl.multiple_of(core * (count * part) + request * part, 128)
                out_ref[:, pl.ds(start, part)] = ref[:, (2 * at + swap) * part : (2 * at + swap + 1) * part]


def weave(count, where, pieces):
    rows = pieces[0].shape[0]
    width = sum(p.shape[1] for p in pieces)
    shape = jax.ShapeDtypeStruct((rows, width), BF16)
    return small_call(functools.partial(weave_kernel, count), "weave", [shape], [where] + pieces, 4 * rows * width)[0]


def proj_kernel(wrows, part, blocks, visits, final, where_ref, ring_ref, *refs):
    total = None
    rows_refs = refs[:visits]
    width = rows_refs[0].shape[1] - 2 * part
    at = visits
    chips = ring_ref.shape[0] // 2
    position = ring_ref[where_ref[0] // 2]
    first_core = where_ref[1] == 0
    for offset in blocks:
        chip = ring_ref[chips + lax.rem(position + offset + chips, chips)]
        start = pl.multiple_of(chip * 2 * wrows, 128)
        columns = jnp.concatenate([r[:, pl.ds(start, 2 * wrows)] for r in rows_refs], axis=0)
        mine, other = refs[at][:wrows], refs[at + 1][:wrows]
        at += 2
        weight = jnp.concatenate([jnp.where(first_core, mine, other), jnp.where(first_core, other, mine)], axis=0)
        term = mm(columns, weight)
        total = term if total is None else total + term
    if final:
        total = total + refs[at][...]
        start = pl.multiple_of(width + where_ref[1] * part, 128)
        rows = rows_refs[0].shape[0]
        for i, out_ref in enumerate(refs[at + 1 :]):
            residual = rows_refs[i][:, pl.ds(start, part)].astype(F32)
            out_ref[...] = (residual + total[i * rows : (i + 1) * rows]).astype(BF16)
    else:
        refs[at][...] = total


def proj(wrows, blocks, where, ring, visits, weights, acc=None):
    final = acc is not None
    rows, part = visits[0].shape[0], weights[0].shape[1]
    operands = [where, ring] + visits + weights + ([acc] if final else [])
    count = len(visits)
    if final:
        outs = [jax.ShapeDtypeStruct((rows, part), BF16)] * count
    else:
        outs = [jax.ShapeDtypeStruct((rows * count, part), F32)]
    return pl.pallas_call(
        functools.partial(proj_kernel, wrows, part, blocks, count, final),
        out_shape=outs,
        in_specs=[smem()] * 2 + [vmem()] * (len(operands) - 2),
        out_specs=[vmem()] * len(outs),
        compiler_params=params(),
        cost_estimate=pl.CostEstimate(
            flops=8 * rows * count * part * wrows * len(blocks),
            bytes_accessed=4 * part * wrows * len(blocks) + 8 * rows * count * part,
            transcendentals=0,
        ),
        name="proj_final" if final else "proj_part",
    )(*operands)


def tables_kernel(wrows, slots, topk, rows, where_ref, *refs):
    pick_ref, put_ref, factor_ref = refs[-3:]
    both = 2 * rows
    expert_id = where_ref[0].astype(F32)
    row_of = lax.broadcasted_iota(jnp.int32, (both, both), 0)
    row_at = lax.broadcasted_iota(jnp.int32, (both, both), 1)
    slot_of = lax.broadcasted_iota(jnp.int32, (slots, both), 0).astype(F32)
    slot_at = lax.broadcasted_iota(jnp.int32, (both, slots), 1).astype(F32)
    for block in range(pick_ref.shape[0]):
        named = [refs[2 * block + i][wrows:].astype(F32) for i in range(2)]
        per_row = named[0].shape[1] // rows
        selected, factor = [], []
        for n in named:
            item = [n[i // per_row : i // per_row + 1, (i % per_row) * rows : (i % per_row + 1) * rows] for i in range(4 * topk)]
            hits = [item[k] == expert_id for k in range(topk)]
            values = [item[topk + k] + item[2 * topk + k] + item[3 * topk + k] for k in range(topk)]
            selected.append(sum(h.astype(F32) for h in hits))
            factor.append(sum(jnp.where(h, v, 0.0) for h, v in zip(hits, values)))
        selected = jnp.concatenate(selected, axis=1)
        factor = jnp.concatenate(factor, axis=1)
        spread = jnp.broadcast_to(selected, (both, both))
        before = jnp.sum(jnp.where(row_at < row_of, spread, 0.0), axis=1, keepdims=True)
        selected_down = jnp.sum(jnp.where(row_at == row_of, spread, 0.0), axis=1, keepdims=True)
        slot_down = jnp.where(selected_down > 0.0, before, -1.0)
        put_ref[block] = (slot_at == slot_down).astype(F32).astype(BF16)
        slot = jnp.sum(jnp.where(row_at == row_of, jnp.broadcast_to(slot_down, (both, both)), 0.0), axis=0, keepdims=True)
        taken = slot_of == slot
        pick_ref[block] = taken.astype(F32).astype(BF16)
        factor_ref[block] = jnp.sum(jnp.where(taken, factor, 0.0), axis=1, keepdims=True)


def tables(wrows, slots, topk, rows, where, blocks):
    chips = len(blocks) // 2
    both = 2 * rows
    return pl.pallas_call(
        functools.partial(tables_kernel, wrows, slots, topk, rows),
        out_shape=[
            jax.ShapeDtypeStruct((chips, slots, both), BF16),
            jax.ShapeDtypeStruct((chips, both, slots), BF16),
            jax.ShapeDtypeStruct((chips, slots, 1), F32),
        ],
        in_specs=[smem()] + [vmem()] * len(blocks),
        out_specs=[vmem()] * 3,
        compiler_params=params(),
        cost_estimate=pl.CostEstimate(flops=0, bytes_accessed=8 * chips * slots * both, transcendentals=0),
        name="tables",
    )(where, *blocks)


def expert_kernel(first, blocks, pieces, gain_ref, pick_ref, put_ref, factor_ref, gate_ref, up_ref, down_ref, *refs):
    slots, rows = pick_ref.shape[1:]
    own = rows // 2
    width = gain_ref.shape[1]
    hidden_units = gate_ref.shape[1]
    inputs = refs[: blocks * pieces]
    mine = refs[blocks * pieces : blocks * pieces + blocks]
    theirs, normed, hidden = refs[-3:]

    for b in range(blocks):
        block = jnp.concatenate([inputs[b * pieces + i][...] for i in range(pieces)], axis=0)
        taken = mm(pick_ref[first + b], block)
        scale = lax.rsqrt(jnp.sum(taken * taken, axis=1, keepdims=True) * (1.0 / width) + 1e-06)
        normed[b * slots : (b + 1) * slots, :] = (taken * scale * gain_ref[...]).astype(BF16)

    for start in range(0, hidden_units, TILE):
        columns = slice(start, min(start + TILE, hidden_units))
        gate_part = mm(normed[...], gate_ref[:, columns])
        up_part = mm(normed[...], up_ref[:, columns])
        hidden[:, columns] = (jax.nn.silu(gate_part) * up_part).astype(BF16)

    for start in range(0, width, TILE):
        columns = slice(start, start + TILE)
        result = mm(hidden[...], down_ref[:, columns])
        for b in range(blocks):
            weighted = (result[b * slots : (b + 1) * slots] * factor_ref[first + b]).astype(BF16)
            placed = mm(put_ref[first + b], weighted).astype(BF16)
            mine[b][:, columns] = placed[:own]
            theirs[b * own : (b + 1) * own, columns] = placed[own:]


def expert(first, blocks, tabs, gain, weights, inputs):
    slots, rows = tabs[0].shape[1:]
    width, hidden_units = weights[0].shape
    own = rows // 2
    m = blocks * slots
    weights = [pltpu.with_memory_space_constraint(w, pltpu.VMEM) for w in weights]
    out = pl.pallas_call(
        functools.partial(expert_kernel, first, blocks, len(inputs) // blocks),
        out_shape=[jax.ShapeDtypeStruct((own, width), BF16)] * blocks
        + [jax.ShapeDtypeStruct((blocks * own, width), BF16)],
        in_specs=[vmem()] * (7 + len(inputs)),
        out_specs=[vmem()] * (blocks + 1),
        scratch_shapes=[
            pltpu.VMEM((m, width), BF16),
            pltpu.VMEM((m, hidden_units), BF16),
        ],
        compiler_params=params(),
        cost_estimate=pl.CostEstimate(
            flops=12 * m * width * hidden_units,
            bytes_accessed=8 * blocks * rows * width,
            transcendentals=m * hidden_units,
        ),
        name="expert",
    )(gain, *tabs, *weights, *inputs)
    return out[:-1], out[-1]


def shared_kernel(count, gain_ref, gate_hbm, up_hbm, down_hbm, *refs):
    inputs, outs = refs[:count], refs[count : 2 * count]
    gate_ref, up_ref, down_ref, normed, hidden, sems = refs[2 * count :]
    units, width = gate_ref.shape
    rows = inputs[0].shape[0]
    tiles = [(start, min(256, units - start)) for start in range(0, units, 256)]
    copies = []
    for i, (start, size) in enumerate(tiles):
        span = pl.ds(start, size)
        for j, (source, target) in enumerate(((gate_hbm, gate_ref), (up_hbm, up_ref))):
            copies.append(pltpu.make_async_copy(source.at[span], target.at[span], sems.at[2 * i + j]))
    copies.append(pltpu.make_async_copy(down_hbm, down_ref, sems.at[2 * len(tiles)]))
    for copy in copies:
        copy.start()
    for i, ref in enumerate(inputs):
        x = ref[...].astype(F32)
        scale = lax.rsqrt(jnp.sum(x * x, axis=1, keepdims=True) * (1.0 / width) + 1e-06)
        normed[i * rows : (i + 1) * rows] = (x * scale * gain_ref[...]).astype(BF16)
    across = (((1,), (1,)), ((), ()))
    for i, (start, size) in enumerate(tiles):
        span = slice(start, start + size)
        copies[2 * i].wait()
        copies[2 * i + 1].wait()
        gate_part = lax.dot_general(normed[...], gate_ref[span], across, preferred_element_type=F32)
        up_part = lax.dot_general(normed[...], up_ref[span], across, preferred_element_type=F32)
        hidden[:, span] = (jax.nn.silu(gate_part) * up_part).astype(BF16)
    copies[-1].wait()
    for start in range(0, width, TILE):
        span = slice(start, start + TILE)
        result = mm(hidden[...], down_ref[:, span])
        for i, ref in enumerate(outs):
            ref[:, span] = result[i * rows : (i + 1) * rows].astype(ref.dtype)


def shared_expert(gain, weights, inputs):
    count = len(inputs)
    rows, width = inputs[0].shape
    units = weights[0].shape[0]
    weights = [pltpu.with_memory_space_constraint(w, pltpu.HBM) for w in weights]
    shapes = [jax.ShapeDtypeStruct((rows, width), F32)] + [jax.ShapeDtypeStruct((rows, width), BF16)] * (count - 1)
    return pl.pallas_call(
        functools.partial(shared_kernel, count),
        out_shape=shapes,
        in_specs=[vmem()] + [hbm()] * 3 + [vmem()] * count,
        out_specs=[vmem()] * count,
        scratch_shapes=[pltpu.VMEM((units, width), BF16)] * 3
        + [
            pltpu.VMEM((count * rows, width), BF16),
            pltpu.VMEM((count * rows, units), BF16),
            pltpu.SemaphoreType.DMA((2 * -(-units // 256) + 1,)),
        ],
        compiler_params=pltpu.CompilerParams(vmem_limit_bytes=24 * 1024 * 1024),
        cost_estimate=pl.CostEstimate(
            flops=12 * count * rows * width * units,
            bytes_accessed=6 * units * width + 4 * count * rows * width,
            transcendentals=count * rows * units,
        ),
        name="shared",
    )(gain, *weights, *inputs)


def base_kernel(*refs):
    total = refs[0][...]
    for ref in refs[1:-1]:
        total = total + ref[...].astype(F32)
    refs[-1][...] = total


def final_kernel(chunks, base_ref, *refs):
    out_ref = refs[-1]
    rows = refs[0].shape[0]
    for chunk in range(chunks):
        span = slice(chunk * rows, (chunk + 1) * rows)
        total = base_ref[span] + refs[chunk][...].astype(F32) + refs[chunks + chunk][...].astype(F32)
        out_ref[span] = total.astype(BF16)


def plain_call(kernel, name, shape, operands):
    return pl.pallas_call(
        kernel,
        out_shape=shape,
        in_specs=[vmem()] * len(operands),
        out_specs=vmem(),
        compiler_params=params(),
        cost_estimate=pl.CostEstimate(flops=0, bytes_accessed=8 * operands[0].size, transcendentals=0),
        name=name,
    )(*operands)


def add_kernel(*refs):
    total = refs[0][...].astype(F32)
    for ref in refs[1:-1]:
        total = total + ref[...].astype(F32)
    refs[-1][...] = total.astype(BF16)


def add(rows, *terms):
    width = terms[0][0].shape[1]

    def block(index):
        return pl.BlockSpec((rows, width), lambda i: (index, 0))

    return pl.pallas_call(
        add_kernel,
        grid=(1,),
        out_shape=jax.ShapeDtypeStruct((rows, width), BF16),
        in_specs=[block(index) for _, index in terms],
        out_specs=block(0),
        compiler_params=params(),
        cost_estimate=pl.CostEstimate(
            flops=rows * width * len(terms), bytes_accessed=2 * rows * width * (len(terms) + 1), transcendentals=0
        ),
        name="add",
    )(*[array for array, _ in terms])


def body(
    req_size,
    exp_size,
    attn_out,
    residual,
    out_weight,
    norm_gain,
    expert_ids,
    gate_weights,
    expert_gate,
    expert_up,
    expert_down,
    shared_gate,
    shared_up,
    shared_down,
):
    rows, width = attn_out.shape
    half = width // 2
    part = half // req_size
    topk = expert_ids.shape[1]
    wrows = out_weight.shape[0]
    capacity = min(rows, 3 * rows * topk // (2 * exp_size))
    slots = -(-2 * capacity // 16) * 16
    chips = exp_size // 2
    depth = chips // 2
    order = ring_order(chips)
    me = lax.axis_index("exp")
    request = lax.axis_index("req")
    here = jnp.stack([me, me % 2, lax.axis_index("req")]).astype(jnp.int32)
    ring = jnp.asarray([order.index(q) for q in range(chips)] + order, jnp.int32)

    steps = [(order[i], order[(i + 1) % chips]) for i in range(chips)]
    ahead = [(2 * a + c, 2 * b + c) for a, b in steps for c in range(2)]
    behind = [(b, a) for a, b in ahead]

    def to_ahead(x):
        return lax.ppermute(x, "exp", ahead)

    def to_behind(x):
        return lax.ppermute(x, "exp", behind)

    def to_core(x):
        return lax.ppermute(x, "exp", [(d, d ^ 1) for d in range(exp_size)])

    def to_request(x, shift, swap=0):
        pairs = [
            (i * exp_size + d, ((i + shift) % req_size) * exp_size + (d ^ swap))
            for i in range(req_size)
            for d in range(exp_size)
        ]
        return lax.ppermute(x, ("req", "exp"), pairs)

    weight_own, weight_sent = prepare(part, here, expert_ids.T, gate_weights.T, out_weight)
    weight_met = to_core(weight_sent)
    chains = [(weight_own, weight_own), (weight_met, weight_met)]
    arrived = [[weight_own, weight_met]]
    for _ in range(1, depth):
        chains = [(to_ahead(low), to_behind(high)) for low, high in chains]
        (low_own, high_own), (low_met, high_met) = chains
        arrived += [[low_own, low_met], [high_own, high_met]]

    weight_own, attn_out, residual = lax.optimization_barrier((weight_own, attn_out, residual))
    packed = pack(req_size, part, here, attn_out, residual)
    visits = [packed[0]] + [to_request(packed[shift], shift) for shift in range(1, req_size)]
    last = [to_ahead(arrived[-2][0]), to_behind(arrived[-1][1])]
    arrived[-2:], visits[1:] = lax.optimization_barrier((arrived[-2:], visits[1:]))
    visits += [to_core(v) for v in visits]

    early = [w for block in arrived[:-2] for w in block]
    late = last + [w for block in arrived[-2:] for w in block]
    tabs_early = tables(wrows, slots, topk, rows, here, early)
    whole = [w for block in arrived for w in block]
    places = [0] + [side * k for k in range(1, depth) for side in (-1, 1)]
    (acc,) = proj(wrows, places, here, ring, visits, whole)
    acc, tabs_early = lax.optimization_barrier((acc, tabs_early))
    product = proj(wrows, [depth], here, ring, visits, last, acc)
    tabs_late = tables(wrows, slots, topk, rows, here, late)

    got = {}
    for shift in reversed(range(req_size)):
        for swap in range(2):
            piece = product[swap * req_size + shift]
            if shift == 0:
                got[shift, swap] = piece if swap == 0 else to_core(piece)
            else:
                got[shift, swap] = to_request(piece, req_size - shift, swap)
    near = beside(here, [got[0, 0], got[0, 1]])
    far, tabs_late = lax.optimization_barrier(
        ([got[place, swap] for place in range(1, req_size) for swap in range(2)], tabs_late)
    )
    far = beside(here, far)
    gain = norm_gain.reshape(1, width)
    weights = [expert_gate[0], expert_up[0], expert_down[0]]

    lows, highs = [to_ahead(near)], [to_behind(near)]
    lows, highs, far = lax.optimization_barrier((lows, highs, far))
    lows.append(to_ahead(far))
    highs.append(to_behind(far))
    own_rows = weave(req_size, here, [near, far])
    results = {0: expert(0, 1, tabs_early, gain, weights, [own_rows, to_core(own_rows)])}
    lows, highs, results[0] = lax.optimization_barrier((lows, highs, results[0]))
    low, high = weave(req_size, here, lows), weave(req_size, here, highs)
    shared_rows = [own_rows]
    for shift in range(1, req_size):
        shared_rows.append(to_request(own_rows, shift))
    for k in range(1, depth):
        if k > 1:
            low, high, results[k - 1] = lax.optimization_barrier((low, high, results[k - 1]))
        if k == depth - 1:
            low, high, shared_rows = lax.optimization_barrier((low, high, shared_rows))
        first, tabs = (2 * k - 1, tabs_early) if k < depth - 1 else (1, tabs_late)
        results[k] = expert(first, 2, tabs, gain, weights, [low, to_core(low), high, to_core(high)])
        if k < depth - 1:
            low, high = to_ahead(low), to_behind(high)
        else:
            low, high = to_ahead(low[: rows // 2]), to_behind(high[rows // 2 :])
    low, high, results[depth - 1] = lax.optimization_barrier((low, high, results[depth - 1]))
    results[depth] = expert(0, 1, tabs_late, gain, weights, [low, high, to_core(low), to_core(high)])

    shared_rows, results[depth] = lax.optimization_barrier((shared_rows, results[depth]))
    shared = shared_expert(gain, [shared_gate.T, shared_up.T, shared_down.T], shared_rows)

    cut = rows // 2
    low, high = [None, None], [None, None]
    for k in range(depth - 1, 0, -1):
        (low_mine, high_mine), theirs = results[k]
        came = to_core(theirs)

        def send_low(chunk):
            terms = [(low_mine, chunk), (came, chunk)] + [(low[chunk], 0)] * (low[chunk] is not None)
            low[chunk] = to_behind(add(cut, *terms))

        def send_high(chunk):
            terms = [(high_mine, chunk), (came, 2 + chunk)] + [(high[chunk], 0)] * (high[chunk] is not None)
            high[chunk] = to_ahead(add(cut, *terms))

        if k == depth - 1:
            send_low(0)
            send_high(1)
            (mine,), theirs = results[depth]
            far = to_core(theirs)
            low[1] = to_behind(add(cut, (mine, 1), (far, 1)))
            high[0] = to_ahead(add(cut, (mine, 0), (far, 0)))
            low[1], shared = lax.optimization_barrier((low[1], shared))
            send_low(1)
            send_high(0)
            continue
        for chunk in range(2):
            send_low(chunk)
            send_high(1 - chunk)
    (mine,), theirs = results[0]
    backs = [to_request(shared[shift], req_size - shift) for shift in range(1, req_size)]
    terms = [shared[0], own_rows, mine, to_core(theirs)] + backs
    base = plain_call(base_kernel, "base", jax.ShapeDtypeStruct((rows, width), F32), terms)
    return plain_call(
        functools.partial(final_kernel, 2), "final", jax.ShapeDtypeStruct((rows, width), BF16), [base] + low + high
    )


def solution(mesh):
    return jax.shard_map(
        functools.partial(body, mesh.shape["req"], mesh.shape["exp"]),
        mesh=mesh,
        in_specs=(
            P(("req", "exp"), None),
            P(("req", "exp"), None),
            P("exp", None),
            P(),
            P(("req", "exp"), None),
            P(("req", "exp"), None),
            P("exp", None, None),
            P("exp", None, None),
            P("exp", None, None),
            P(None, "req"),
            P(None, "req"),
            P(None, "req"),
        ),
        out_specs=P(("req", "exp"), None),
        check_vma=False,
    )
```

```python
import functools

import jax
import jax.numpy as jnp
from jax import lax
from jax.experimental import pallas as pl
from jax.experimental.pallas import tpu as pltpu
from jax.sharding import PartitionSpec as P

F32 = jnp.float32
BF16 = jnp.bfloat16
VMEM_BYTES = 12 * 1024 * 1024
TILE = 512
TABLE_ROWS = 16


def ring_order(chips):
    slow = 4
    fast = chips // slow
    order = [a * fast for a in range(slow)]
    for turn, a in enumerate(reversed(range(slow))):
        inner = range(1, fast) if turn % 2 == 0 else range(fast - 1, 0, -1)
        order += [a * fast + b for b in inner]
    return order


def mm(a, b):
    return jnp.dot(a, b, preferred_element_type=F32)


def vmem():
    return pl.BlockSpec(memory_space=pltpu.VMEM)


def smem():
    return pl.BlockSpec(memory_space=pltpu.SMEM)


def hbm():
    return pl.BlockSpec(memory_space=pl.ANY)


def params():
    return pltpu.CompilerParams(vmem_limit_bytes=VMEM_BYTES)


def prepare_kernel(part, where_ref, ids_hbm, factors_hbm, weight_hbm, own_ref, sent_ref, ids_ref, factors_ref, sems):
    wrows, width = weight_hbm.shape
    topk, rows = ids_ref.shape
    core, request = where_ref[1], where_ref[2]
    small = [
        pltpu.make_async_copy(ids_hbm, ids_ref, sems.at[2]),
        pltpu.make_async_copy(factors_hbm, factors_ref, sems.at[3]),
    ]
    large = []
    for i, (ref, which) in enumerate(((own_ref, core), (sent_ref, 1 - core))):
        start = pl.multiple_of(which * (width // 2) + request * part, 128)
        large.append(pltpu.make_async_copy(weight_hbm.at[:, pl.ds(start, part)], ref.at[:wrows], sems.at[i]))
    for copy in small + large:
        copy.start()
    for copy in small:
        copy.wait()
    per_row = part // rows
    factors = factors_ref[...]
    big = factors.astype(BF16).astype(F32)
    middle = (factors - big).astype(BF16).astype(F32)
    named = (ids_ref[...].astype(F32), big, middle, factors - big - middle)
    items = [kind[k : k + 1] for kind in named for k in range(topk)]
    items += [jnp.zeros((1, rows), F32)] * (-len(items) % per_row)
    lines = [jnp.concatenate(items[i : i + per_row], axis=1) for i in range(0, len(items), per_row)]
    lines.append(jnp.zeros((TABLE_ROWS - len(lines), part), F32))
    table = jnp.concatenate(lines, axis=0).astype(BF16)
    own_ref[wrows:] = table
    sent_ref[wrows:] = table
    for copy in large:
        copy.wait()


def prepare(part, where, ids, factors, weight):
    shape = jax.ShapeDtypeStruct((weight.shape[0] + TABLE_ROWS, part), BF16)
    arrays = [pltpu.with_memory_space_constraint(x, pltpu.HBM) for x in (ids, factors, weight)]
    return pl.pallas_call(
        functools.partial(prepare_kernel, part),
        out_shape=[shape] * 2,
        in_specs=[smem()] + [hbm()] * 3,
        out_specs=[vmem()] * 2,
        scratch_shapes=[
            pltpu.VMEM(ids.shape, ids.dtype),
            pltpu.VMEM(factors.shape, factors.dtype),
            pltpu.SemaphoreType.DMA((4,)),
        ],
        compiler_params=params(),
        cost_estimate=pl.CostEstimate(flops=0, bytes_accessed=2 * weight.size, transcendentals=0),
        name="prepare",
    )(where, *arrays)


def small_call(kernel, name, shapes, operands, moved):
    return pl.pallas_call(
        kernel,
        out_shape=shapes,
        in_specs=[smem()] + [vmem()] * (len(operands) - 1),
        out_specs=[vmem()] * len(shapes),
        compiler_params=params(),
        cost_estimate=pl.CostEstimate(flops=0, bytes_accessed=moved, transcendentals=0),
        name=name,
    )(*operands)


def pack_kernel(count, part, where_ref, attn_hbm, residual_hbm, *refs):
    width = attn_hbm.shape[1]
    outs, sems = refs[:-1], refs[-1]
    copies = []
    for shift, out_ref in enumerate(outs):
        moves = [(attn_hbm, out_ref.at[:, :width])]
        request = lax.rem(where_ref[2] + shift, count)
        for core in range(2):
            start = pl.multiple_of(core * (width // 2) + request * part, 128)
            target = out_ref.at[:, width + core * part : width + (core + 1) * part]
            moves.append((residual_hbm.at[:, pl.ds(start, part)], target))
        for i, (source, target) in enumerate(moves):
            copies.append(pltpu.make_async_copy(source, target, sems.at[3 * shift + i]))
    for copy in copies:
        copy.start()
    for copy in copies:
        copy.wait()


def pack(count, part, where, attn, residual):
    rows, width = attn.shape
    arrays = [pltpu.with_memory_space_constraint(x, pltpu.HBM) for x in (attn, residual)]
    return pl.pallas_call(
        functools.partial(pack_kernel, count, part),
        out_shape=[jax.ShapeDtypeStruct((rows, width + 2 * part), BF16)] * count,
        in_specs=[smem(), hbm(), hbm()],
        out_specs=[vmem()] * count,
        scratch_shapes=[pltpu.SemaphoreType.DMA((3 * count,))],
        compiler_params=params(),
        cost_estimate=pl.CostEstimate(flops=0, bytes_accessed=4 * attn.size * count, transcendentals=0),
        name="pack",
    )(where, *arrays)


def beside_kernel(where_ref, *refs):
    part = refs[0].shape[1]
    for i, ref in enumerate(refs[:-1]):
        refs[-1][:, i * part : (i + 1) * part] = ref[...]


def beside(where, pieces):
    rows, part = pieces[0].shape
    shape = jax.ShapeDtypeStruct((rows, len(pieces) * part), BF16)
    return small_call(beside_kernel, "beside", [shape], [where] + pieces, 4 * rows * part * len(pieces))[0]


def weave_kernel(count, where_ref, *refs):
    out_ref = refs[-1]
    part = out_ref.shape[1] // (2 * count)
    place = 0
    for ref in refs[:-1]:
        for at in range(ref.shape[1] // (2 * part)):
            request = lax.rem(where_ref[2] + place, count)
            place += 1
            for swap in range(2):
                core = where_ref[1] if swap == 0 else 1 - where_ref[1]
                start = pl.multiple_of(core * (count * part) + request * part, 128)
                out_ref[:, pl.ds(start, part)] = ref[:, (2 * at + swap) * part : (2 * at + swap + 1) * part]


def weave(count, where, pieces):
    rows = pieces[0].shape[0]
    width = sum(p.shape[1] for p in pieces)
    shape = jax.ShapeDtypeStruct((rows, width), BF16)
    return small_call(functools.partial(weave_kernel, count), "weave", [shape], [where] + pieces, 4 * rows * width)[0]


def proj_kernel(wrows, part, blocks, visits, final, where_ref, ring_ref, *refs):
    total = None
    rows_refs = refs[:visits]
    width = rows_refs[0].shape[1] - 2 * part
    at = visits
    chips = ring_ref.shape[0] // 2
    position = ring_ref[where_ref[0] // 2]
    first_core = where_ref[1] == 0
    for offset in blocks:
        chip = ring_ref[chips + lax.rem(position + offset + chips, chips)]
        start = pl.multiple_of(chip * 2 * wrows, 128)
        columns = jnp.concatenate([r[:, pl.ds(start, 2 * wrows)] for r in rows_refs], axis=0)
        mine, other = refs[at][:wrows], refs[at + 1][:wrows]
        at += 2
        weight = jnp.concatenate([jnp.where(first_core, mine, other), jnp.where(first_core, other, mine)], axis=0)
        term = mm(columns, weight)
        total = term if total is None else total + term
    if final:
        total = total + refs[at][...]
        start = pl.multiple_of(width + where_ref[1] * part, 128)
        rows = rows_refs[0].shape[0]
        for i, out_ref in enumerate(refs[at + 1 :]):
            residual = rows_refs[i][:, pl.ds(start, part)].astype(F32)
            out_ref[...] = (residual + total[i * rows : (i + 1) * rows]).astype(BF16)
    else:
        refs[at][...] = total


def proj(wrows, blocks, where, ring, visits, weights, acc=None):
    final = acc is not None
    rows, part = visits[0].shape[0], weights[0].shape[1]
    operands = [where, ring] + visits + weights + ([acc] if final else [])
    count = len(visits)
    if final:
        outs = [jax.ShapeDtypeStruct((rows, part), BF16)] * count
    else:
        outs = [jax.ShapeDtypeStruct((rows * count, part), F32)]
    return pl.pallas_call(
        functools.partial(proj_kernel, wrows, part, blocks, count, final),
        out_shape=outs,
        in_specs=[smem()] * 2 + [vmem()] * (len(operands) - 2),
        out_specs=[vmem()] * len(outs),
        compiler_params=params(),
        cost_estimate=pl.CostEstimate(
            flops=8 * rows * count * part * wrows * len(blocks),
            bytes_accessed=4 * part * wrows * len(blocks) + 8 * rows * count * part,
            transcendentals=0,
        ),
        name="proj_final" if final else "proj_part",
    )(*operands)


def tables_kernel(wrows, slots, topk, rows, where_ref, *refs):
    pick_ref, put_ref, factor_ref = refs[-3:]
    both = 2 * rows
    expert_id = where_ref[0].astype(F32)
    row_of = lax.broadcasted_iota(jnp.int32, (both, both), 0)
    row_at = lax.broadcasted_iota(jnp.int32, (both, both), 1)
    slot_of = lax.broadcasted_iota(jnp.int32, (slots, both), 0).astype(F32)
    slot_at = lax.broadcasted_iota(jnp.int32, (both, slots), 1).astype(F32)
    for block in range(pick_ref.shape[0]):
        named = [refs[2 * block + i][wrows:].astype(F32) for i in range(2)]
        per_row = named[0].shape[1] // rows
        selected, factor = [], []
        for n in named:
            item = [n[i // per_row : i // per_row + 1, (i % per_row) * rows : (i % per_row + 1) * rows] for i in range(4 * topk)]
            hits = [item[k] == expert_id for k in range(topk)]
            values = [item[topk + k] + item[2 * topk + k] + item[3 * topk + k] for k in range(topk)]
            selected.append(sum(h.astype(F32) for h in hits))
            factor.append(sum(jnp.where(h, v, 0.0) for h, v in zip(hits, values)))
        selected = jnp.concatenate(selected, axis=1)
        factor = jnp.concatenate(factor, axis=1)
        spread = jnp.broadcast_to(selected, (both, both))
        before = jnp.sum(jnp.where(row_at < row_of, spread, 0.0), axis=1, keepdims=True)
        selected_down = jnp.sum(jnp.where(row_at == row_of, spread, 0.0), axis=1, keepdims=True)
        slot_down = jnp.where(selected_down > 0.0, before, -1.0)
        put_ref[block] = (slot_at == slot_down).astype(F32).astype(BF16)
        slot = jnp.sum(jnp.where(row_at == row_of, jnp.broadcast_to(slot_down, (both, both)), 0.0), axis=0, keepdims=True)
        taken = slot_of == slot
        pick_ref[block] = taken.astype(F32).astype(BF16)
        factor_ref[block] = jnp.sum(jnp.where(taken, factor, 0.0), axis=1, keepdims=True)


def tables(wrows, slots, topk, rows, where, blocks):
    chips = len(blocks) // 2
    both = 2 * rows
    return pl.pallas_call(
        functools.partial(tables_kernel, wrows, slots, topk, rows),
        out_shape=[
            jax.ShapeDtypeStruct((chips, slots, both), BF16),
            jax.ShapeDtypeStruct((chips, both, slots), BF16),
            jax.ShapeDtypeStruct((chips, slots, 1), F32),
        ],
        in_specs=[smem()] + [vmem()] * len(blocks),
        out_specs=[vmem()] * 3,
        compiler_params=params(),
        cost_estimate=pl.CostEstimate(flops=0, bytes_accessed=8 * chips * slots * both, transcendentals=0),
        name="tables",
    )(where, *blocks)


def expert_kernel(first, blocks, pieces, gain_ref, pick_ref, put_ref, factor_ref, gate_ref, up_ref, down_ref, *refs):
    slots, rows = pick_ref.shape[1:]
    own = rows // 2
    width = gain_ref.shape[1]
    hidden_units = gate_ref.shape[1]
    inputs = refs[: blocks * pieces]
    mine = refs[blocks * pieces : blocks * pieces + blocks]
    theirs, normed, hidden = refs[-3:]

    for b in range(blocks):
        block = jnp.concatenate([inputs[b * pieces + i][...] for i in range(pieces)], axis=0)
        taken = mm(pick_ref[first + b], block)
        scale = lax.rsqrt(jnp.sum(taken * taken, axis=1, keepdims=True) * (1.0 / width) + 1e-06)
        normed[b * slots : (b + 1) * slots, :] = (taken * scale * gain_ref[...]).astype(BF16)

    for start in range(0, hidden_units, TILE):
        columns = slice(start, min(start + TILE, hidden_units))
        gate_part = mm(normed[...], gate_ref[:, columns])
        up_part = mm(normed[...], up_ref[:, columns])
        hidden[:, columns] = (jax.nn.silu(gate_part) * up_part).astype(BF16)

    for start in range(0, width, TILE):
        columns = slice(start, start + TILE)
        result = mm(hidden[...], down_ref[:, columns])
        for b in range(blocks):
            weighted = (result[b * slots : (b + 1) * slots] * factor_ref[first + b]).astype(BF16)
            placed = mm(put_ref[first + b], weighted).astype(BF16)
            mine[b][:, columns] = placed[:own]
            theirs[b * own : (b + 1) * own, columns] = placed[own:]


def expert(first, blocks, tabs, gain, weights, inputs):
    slots, rows = tabs[0].shape[1:]
    width, hidden_units = weights[0].shape
    own = rows // 2
    m = blocks * slots
    weights = [pltpu.with_memory_space_constraint(w, pltpu.VMEM) for w in weights]
    out = pl.pallas_call(
        functools.partial(expert_kernel, first, blocks, len(inputs) // blocks),
        out_shape=[jax.ShapeDtypeStruct((own, width), BF16)] * blocks
        + [jax.ShapeDtypeStruct((blocks * own, width), BF16)],
        in_specs=[vmem()] * (7 + len(inputs)),
        out_specs=[vmem()] * (blocks + 1),
        scratch_shapes=[
            pltpu.VMEM((m, width), BF16),
            pltpu.VMEM((m, hidden_units), BF16),
        ],
        compiler_params=params(),
        cost_estimate=pl.CostEstimate(
            flops=12 * m * width * hidden_units,
            bytes_accessed=8 * blocks * rows * width,
            transcendentals=m * hidden_units,
        ),
        name="expert",
    )(gain, *tabs, *weights, *inputs)
    return out[:-1], out[-1]


def shared_kernel(count, gain_ref, gate_hbm, up_hbm, down_hbm, *refs):
    inputs, outs = refs[:count], refs[count : 2 * count]
    gate_ref, up_ref, down_ref, normed, hidden, sems = refs[2 * count :]
    units, width = gate_ref.shape
    rows = inputs[0].shape[0]
    tiles = [(start, min(256, units - start)) for start in range(0, units, 256)]
    copies = []
    for i, (start, size) in enumerate(tiles):
        span = pl.ds(start, size)
        for j, (source, target) in enumerate(((gate_hbm, gate_ref), (up_hbm, up_ref))):
            copies.append(pltpu.make_async_copy(source.at[span], target.at[span], sems.at[2 * i + j]))
    copies.append(pltpu.make_async_copy(down_hbm, down_ref, sems.at[2 * len(tiles)]))
    for copy in copies:
        copy.start()
    for i, ref in enumerate(inputs):
        x = ref[...].astype(F32)
        scale = lax.rsqrt(jnp.sum(x * x, axis=1, keepdims=True) * (1.0 / width) + 1e-06)
        normed[i * rows : (i + 1) * rows] = (x * scale * gain_ref[...]).astype(BF16)
    across = (((1,), (1,)), ((), ()))
    for i, (start, size) in enumerate(tiles):
        span = slice(start, start + size)
        copies[2 * i].wait()
        copies[2 * i + 1].wait()
        gate_part = lax.dot_general(normed[...], gate_ref[span], across, preferred_element_type=F32)
        up_part = lax.dot_general(normed[...], up_ref[span], across, preferred_element_type=F32)
        hidden[:, span] = (jax.nn.silu(gate_part) * up_part).astype(BF16)
    copies[-1].wait()
    for start in range(0, width, TILE):
        span = slice(start, start + TILE)
        result = mm(hidden[...], down_ref[:, span])
        for i, ref in enumerate(outs):
            ref[:, span] = result[i * rows : (i + 1) * rows].astype(ref.dtype)


def shared_expert(gain, weights, inputs):
    count = len(inputs)
    rows, width = inputs[0].shape
    units = weights[0].shape[0]
    weights = [pltpu.with_memory_space_constraint(w, pltpu.HBM) for w in weights]
    shapes = [jax.ShapeDtypeStruct((rows, width), F32)] + [jax.ShapeDtypeStruct((rows, width), BF16)] * (count - 1)
    return pl.pallas_call(
        functools.partial(shared_kernel, count),
        out_shape=shapes,
        in_specs=[vmem()] + [hbm()] * 3 + [vmem()] * count,
        out_specs=[vmem()] * count,
        scratch_shapes=[pltpu.VMEM((units, width), BF16)] * 3
        + [
            pltpu.VMEM((count * rows, width), BF16),
            pltpu.VMEM((count * rows, units), BF16),
            pltpu.SemaphoreType.DMA((2 * -(-units // 256) + 1,)),
        ],
        compiler_params=pltpu.CompilerParams(vmem_limit_bytes=24 * 1024 * 1024),
        cost_estimate=pl.CostEstimate(
            flops=12 * count * rows * width * units,
            bytes_accessed=6 * units * width + 4 * count * rows * width,
            transcendentals=count * rows * units,
        ),
        name="shared",
    )(gain, *weights, *inputs)


def base_kernel(*refs):
    total = refs[0][...]
    for ref in refs[1:-1]:
        total = total + ref[...].astype(F32)
    refs[-1][...] = total


def final_kernel(chunks, base_ref, *refs):
    out_ref = refs[-1]
    rows = refs[0].shape[0]
    for chunk in range(chunks):
        span = slice(chunk * rows, (chunk + 1) * rows)
        total = base_ref[span] + refs[chunk][...].astype(F32) + refs[chunks + chunk][...].astype(F32)
        out_ref[span] = total.astype(BF16)


def plain_call(kernel, name, shape, operands):
    return pl.pallas_call(
        kernel,
        out_shape=shape,
        in_specs=[vmem()] * len(operands),
        out_specs=vmem(),
        compiler_params=params(),
        cost_estimate=pl.CostEstimate(flops=0, bytes_accessed=8 * operands[0].size, transcendentals=0),
        name=name,
    )(*operands)


def add_kernel(*refs):
    total = refs[0][...].astype(F32)
    for ref in refs[1:-1]:
        total = total + ref[...].astype(F32)
    refs[-1][...] = total.astype(BF16)


def add(rows, *terms):
    width = terms[0][0].shape[1]

    def block(index):
        return pl.BlockSpec((rows, width), lambda i: (index, 0))

    return pl.pallas_call(
        add_kernel,
        grid=(1,),
        out_shape=jax.ShapeDtypeStruct((rows, width), BF16),
        in_specs=[block(index) for _, index in terms],
        out_specs=block(0),
        compiler_params=params(),
        cost_estimate=pl.CostEstimate(
            flops=rows * width * len(terms), bytes_accessed=2 * rows * width * (len(terms) + 1), transcendentals=0
        ),
        name="add",
    )(*[array for array, _ in terms])


def body(
    req_size,
    exp_size,
    attn_out,
    residual,
    out_weight,
    norm_gain,
    expert_ids,
    gate_weights,
    expert_gate,
    expert_up,
    expert_down,
    shared_gate,
    shared_up,
    shared_down,
):
    rows, width = attn_out.shape
    half = width // 2
    part = half // req_size
    topk = expert_ids.shape[1]
    wrows = out_weight.shape[0]
    capacity = min(rows, 3 * rows * topk // (2 * exp_size))
    slots = -(-2 * capacity // 16) * 16
    chips = exp_size // 2
    depth = chips // 2
    order = ring_order(chips)
    me = lax.axis_index("exp")
    request = lax.axis_index("req")
    here = jnp.stack([me, me % 2, lax.axis_index("req")]).astype(jnp.int32)
    ring = jnp.asarray([order.index(q) for q in range(chips)] + order, jnp.int32)

    steps = [(order[i], order[(i + 1) % chips]) for i in range(chips)]
    ahead = [(2 * a + c, 2 * b + c) for a, b in steps for c in range(2)]
    behind = [(b, a) for a, b in ahead]

    def to_ahead(x):
        return lax.ppermute(x, "exp", ahead)

    def to_behind(x):
        return lax.ppermute(x, "exp", behind)

    def to_core(x):
        return lax.ppermute(x, "exp", [(d, d ^ 1) for d in range(exp_size)])

    def to_request(x, shift, swap=0):
        pairs = [
            (i * exp_size + d, ((i + shift) % req_size) * exp_size + (d ^ swap))
            for i in range(req_size)
            for d in range(exp_size)
        ]
        return lax.ppermute(x, ("req", "exp"), pairs)

    weight_own, weight_sent = prepare(part, here, expert_ids.T, gate_weights.T, out_weight)
    weight_met = to_core(weight_sent)
    chains = [(weight_own, weight_own), (weight_met, weight_met)]
    arrived = [[weight_own, weight_met]]
    for _ in range(1, depth):
        chains = [(to_ahead(low), to_behind(high)) for low, high in chains]
        (low_own, high_own), (low_met, high_met) = chains
        arrived += [[low_own, low_met], [high_own, high_met]]

    weight_own, attn_out, residual = lax.optimization_barrier((weight_own, attn_out, residual))
    packed = pack(req_size, part, here, attn_out, residual)
    visits = [packed[0]] + [to_request(packed[shift], shift) for shift in range(1, req_size)]
    last = [to_ahead(arrived[-2][0]), to_behind(arrived[-1][1])]
    arrived[-2:], visits[1:] = lax.optimization_barrier((arrived[-2:], visits[1:]))
    visits += [to_core(v) for v in visits]

    early = [w for block in arrived[:-2] for w in block]
    late = last + [w for block in arrived[-2:] for w in block]
    whole = [w for block in arrived for w in block]
    places = [0] + [side * k for k in range(1, depth) for side in (-1, 1)]
    (acc,) = proj(wrows, places, here, ring, visits, whole)
    product = proj(wrows, [depth], here, ring, visits, last, acc)
    product, early = lax.optimization_barrier((product, early))
    tabs_early = tables(wrows, slots, topk, rows, here, early)
    tabs_late = tables(wrows, slots, topk, rows, here, late)

    got = {}
    for shift in reversed(range(req_size)):
        for swap in range(2):
            piece = product[swap * req_size + shift]
            if shift == 0:
                got[shift, swap] = piece if swap == 0 else to_core(piece)
            else:
                got[shift, swap] = to_request(piece, req_size - shift, swap)
    near = beside(here, [got[0, 0], got[0, 1]])
    far, tabs_early, tabs_late = lax.optimization_barrier(
        ([got[place, swap] for place in range(1, req_size) for swap in range(2)], tabs_early, tabs_late)
    )
    far = beside(here, far)
    gain = norm_gain.reshape(1, width)
    weights = [expert_gate[0], expert_up[0], expert_down[0]]

    lows, highs = [to_ahead(near)], [to_behind(near)]
    lows, highs, far = lax.optimization_barrier((lows, highs, far))
    lows.append(to_ahead(far))
    highs.append(to_behind(far))
    own_rows = weave(req_size, here, [near, far])
    results = {0: expert(0, 1, tabs_early, gain, weights, [own_rows, to_core(own_rows)])}
    lows, highs, results[0] = lax.optimization_barrier((lows, highs, results[0]))
    low, high = weave(req_size, here, lows), weave(req_size, here, highs)
    shared_rows = [own_rows]
    for shift in range(1, req_size):
        shared_rows.append(to_request(own_rows, shift))
    for k in range(1, depth):
        if k > 1:
            low, high, results[k - 1] = lax.optimization_barrier((low, high, results[k - 1]))
        if k == depth - 1:
            low, high, shared_rows = lax.optimization_barrier((low, high, shared_rows))
        first, tabs = (2 * k - 1, tabs_early) if k < depth - 1 else (1, tabs_late)
        results[k] = expert(first, 2, tabs, gain, weights, [low, to_core(low), high, to_core(high)])
        if k < depth - 1:
            low, high = to_ahead(low), to_behind(high)
        else:
            low, high = to_ahead(low[: rows // 2]), to_behind(high[rows // 2 :])
    low, high, results[depth - 1] = lax.optimization_barrier((low, high, results[depth - 1]))
    results[depth] = expert(0, 1, tabs_late, gain, weights, [low, high, to_core(low), to_core(high)])

    cut = rows // 2
    low, high = [None, None], [None, None]
    for k in range(depth - 1, 0, -1):
        (low_mine, high_mine), theirs = results[k]
        came = to_core(theirs)

        def send_low(chunk):
            terms = [(low_mine, chunk), (came, chunk)] + [(low[chunk], 0)] * (low[chunk] is not None)
            low[chunk] = to_behind(add(cut, *terms))

        def send_high(chunk):
            terms = [(high_mine, chunk), (came, 2 + chunk)] + [(high[chunk], 0)] * (high[chunk] is not None)
            high[chunk] = to_ahead(add(cut, *terms))

        if k == depth - 1:
            (mine,), theirs = results[depth]
            far = to_core(theirs)
            sums = add(cut, (mine, 1), (far, 1)), add(cut, (mine, 0), (far, 0))
            sums, shared_rows = lax.optimization_barrier((sums, shared_rows))
            shared = shared_expert(gain, [shared_gate.T, shared_up.T, shared_down.T], shared_rows)
            low[1], high[0] = to_behind(sums[0]), to_ahead(sums[1])
            came, shared = lax.optimization_barrier((came, shared))
            send_low(0)
            send_high(1)
            send_low(1)
            send_high(0)
            continue
        for chunk in range(2):
            send_low(chunk)
            send_high(1 - chunk)
    (mine,), theirs = results[0]
    backs = [to_request(shared[shift], req_size - shift) for shift in range(1, req_size)]
    terms = [shared[0], own_rows, mine, to_core(theirs)] + backs
    base = plain_call(base_kernel, "base", jax.ShapeDtypeStruct((rows, width), F32), terms)
    return plain_call(
        functools.partial(final_kernel, 2), "final", jax.ShapeDtypeStruct((rows, width), BF16), [base] + low + high
    )


def solution(mesh):
    return jax.shard_map(
        functools.partial(body, mesh.shape["req"], mesh.shape["exp"]),
        mesh=mesh,
        in_specs=(
            P(("req", "exp"), None),
            P(("req", "exp"), None),
            P("exp", None),
            P(),
            P(("req", "exp"), None),
            P(("req", "exp"), None),
            P("exp", None, None),
            P("exp", None, None),
            P("exp", None, None),
            P(None, "req"),
            P(None, "req"),
            P(None, "req"),
        ),
        out_specs=P(("req", "exp"), None),
        check_vma=False,
    )
```

```python
import functools

import jax
import jax.numpy as jnp
from jax import lax
from jax.experimental import pallas as pl
from jax.experimental.pallas import tpu as pltpu
from jax.sharding import PartitionSpec as P

F32 = jnp.float32
BF16 = jnp.bfloat16
VMEM_BYTES = 12 * 1024 * 1024
TILE = 512
TABLE_ROWS = 16


def ring_order(chips):
    slow = 4
    fast = chips // slow
    order = [a * fast for a in range(slow)]
    for turn, a in enumerate(reversed(range(slow))):
        inner = range(1, fast) if turn % 2 == 0 else range(fast - 1, 0, -1)
        order += [a * fast + b for b in inner]
    return order


def mm(a, b):
    return jnp.dot(a, b, preferred_element_type=F32)


def vmem():
    return pl.BlockSpec(memory_space=pltpu.VMEM)


def smem():
    return pl.BlockSpec(memory_space=pltpu.SMEM)


def hbm():
    return pl.BlockSpec(memory_space=pl.ANY)


def params():
    return pltpu.CompilerParams(vmem_limit_bytes=VMEM_BYTES)


def prepare_kernel(count, part, where_ref, ids_hbm, factors_hbm, weight_hbm, attn_hbm, residual_hbm, own_ref, sent_ref, *refs):
    packs = refs[:count]
    ids_ref, factors_ref, sems = refs[count:]
    wrows, width = weight_hbm.shape
    topk, rows = ids_ref.shape
    core, request = where_ref[1], where_ref[2]
    moves = [(ids_hbm, ids_ref), (factors_hbm, factors_ref)]
    for ref, which in ((own_ref, core), (sent_ref, 1 - core)):
        start = pl.multiple_of(which * (width // 2) + request * part, 128)
        moves.append((weight_hbm.at[:, pl.ds(start, part)], ref.at[:wrows]))
    for shift, ref in enumerate(packs):
        moves.append((attn_hbm, ref.at[:, :width]))
        other = lax.rem(request + shift, count)
        for half in range(2):
            start = pl.multiple_of(half * (width // 2) + other * part, 128)
            target = ref.at[:, width + half * part : width + (half + 1) * part]
            moves.append((residual_hbm.at[:, pl.ds(start, part)], target))
    copies = [pltpu.make_async_copy(source, target, sems.at[i]) for i, (source, target) in enumerate(moves)]
    for copy in copies:
        copy.start()
    for copy in copies[:2]:
        copy.wait()
    per_row = part // rows
    factors = factors_ref[...]
    big = factors.astype(BF16).astype(F32)
    middle = (factors - big).astype(BF16).astype(F32)
    named = (ids_ref[...].astype(F32), big, middle, factors - big - middle)
    items = [kind[k : k + 1] for kind in named for k in range(topk)]
    items += [jnp.zeros((1, rows), F32)] * (-len(items) % per_row)
    lines = [jnp.concatenate(items[i : i + per_row], axis=1) for i in range(0, len(items), per_row)]
    lines.append(jnp.zeros((TABLE_ROWS - len(lines), part), F32))
    table = jnp.concatenate(lines, axis=0).astype(BF16)
    own_ref[wrows:] = table
    sent_ref[wrows:] = table
    for copy in copies[2:]:
        copy.wait()


def prepare(count, part, where, ids, factors, weight, attn, residual):
    rows, width = attn.shape
    shape = jax.ShapeDtypeStruct((weight.shape[0] + TABLE_ROWS, part), BF16)
    packed = jax.ShapeDtypeStruct((rows, width + 2 * part), BF16)
    arrays = [pltpu.with_memory_space_constraint(x, pltpu.HBM) for x in (ids, factors, weight, attn, residual)]
    out = pl.pallas_call(
        functools.partial(prepare_kernel, count, part),
        out_shape=[shape] * 2 + [packed] * count,
        in_specs=[smem()] + [hbm()] * 5,
        out_specs=[vmem()] * (2 + count),
        scratch_shapes=[
            pltpu.VMEM(ids.shape, ids.dtype),
            pltpu.VMEM(factors.shape, factors.dtype),
            pltpu.SemaphoreType.DMA((4 + 3 * count,)),
        ],
        compiler_params=params(),
        cost_estimate=pl.CostEstimate(flops=0, bytes_accessed=8 * attn.size, transcendentals=0),
        name="prepare",
    )(where, *arrays)
    return out[0], out[1], out[2:]


def small_call(kernel, name, shapes, operands, moved):
    return pl.pallas_call(
        kernel,
        out_shape=shapes,
        in_specs=[smem()] + [vmem()] * (len(operands) - 1),
        out_specs=[vmem()] * len(shapes),
        compiler_params=params(),
        cost_estimate=pl.CostEstimate(flops=0, bytes_accessed=moved, transcendentals=0),
        name=name,
    )(*operands)


def beside_kernel(where_ref, *refs):
    part = refs[0].shape[1]
    for i, ref in enumerate(refs[:-1]):
        refs[-1][:, i * part : (i + 1) * part] = ref[...]


def beside(where, pieces):
    rows, part = pieces[0].shape
    shape = jax.ShapeDtypeStruct((rows, len(pieces) * part), BF16)
    return small_call(beside_kernel, "beside", [shape], [where] + pieces, 4 * rows * part * len(pieces))[0]


def weave_kernel(count, where_ref, *refs):
    out_ref = refs[-1]
    part = out_ref.shape[1] // (2 * count)
    place = 0
    for ref in refs[:-1]:
        for at in range(ref.shape[1] // (2 * part)):
            request = lax.rem(where_ref[2] + place, count)
            place += 1
            for swap in range(2):
                core = where_ref[1] if swap == 0 else 1 - where_ref[1]
                start = pl.multiple_of(core * (count * part) + request * part, 128)
                out_ref[:, pl.ds(start, part)] = ref[:, (2 * at + swap) * part : (2 * at + swap + 1) * part]


def weave(count, where, pieces):
    rows = pieces[0].shape[0]
    width = sum(p.shape[1] for p in pieces)
    shape = jax.ShapeDtypeStruct((rows, width), BF16)
    return small_call(functools.partial(weave_kernel, count), "weave", [shape], [where] + pieces, 4 * rows * width)[0]


def proj_kernel(wrows, part, blocks, visits, final, where_ref, ring_ref, *refs):
    total = None
    rows_refs = refs[:visits]
    width = rows_refs[0].shape[1] - 2 * part
    at = visits
    chips = ring_ref.shape[0] // 2
    position = ring_ref[where_ref[0] // 2]
    first_core = where_ref[1] == 0
    for offset in blocks:
        chip = ring_ref[chips + lax.rem(position + offset + chips, chips)]
        start = pl.multiple_of(chip * 2 * wrows, 128)
        columns = jnp.concatenate([r[:, pl.ds(start, 2 * wrows)] for r in rows_refs], axis=0)
        mine, other = refs[at][:wrows], refs[at + 1][:wrows]
        at += 2
        weight = jnp.concatenate([jnp.where(first_core, mine, other), jnp.where(first_core, other, mine)], axis=0)
        term = mm(columns, weight)
        total = term if total is None else total + term
    if final:
        total = total + refs[at][...]
        start = pl.multiple_of(width + where_ref[1] * part, 128)
        rows = rows_refs[0].shape[0]
        for i, out_ref in enumerate(refs[at + 1 :]):
            residual = rows_refs[i][:, pl.ds(start, part)].astype(F32)
            out_ref[...] = (residual + total[i * rows : (i + 1) * rows]).astype(BF16)
    else:
        refs[at][...] = total


def proj(wrows, blocks, where, ring, visits, weights, acc=None):
    final = acc is not None
    rows, part = visits[0].shape[0], weights[0].shape[1]
    operands = [where, ring] + visits + weights + ([acc] if final else [])
    count = len(visits)
    if final:
        outs = [jax.ShapeDtypeStruct((rows, part), BF16)] * count
    else:
        outs = [jax.ShapeDtypeStruct((rows * count, part), F32)]
    return pl.pallas_call(
        functools.partial(proj_kernel, wrows, part, blocks, count, final),
        out_shape=outs,
        in_specs=[smem()] * 2 + [vmem()] * (len(operands) - 2),
        out_specs=[vmem()] * len(outs),
        compiler_params=params(),
        cost_estimate=pl.CostEstimate(
            flops=8 * rows * count * part * wrows * len(blocks),
            bytes_accessed=4 * part * wrows * len(blocks) + 8 * rows * count * part,
            transcendentals=0,
        ),
        name="proj_final" if final else "proj_part",
    )(*operands)


def tables_kernel(wrows, slots, topk, rows, where_ref, *refs):
    pick_ref, put_ref, factor_ref = refs[-3:]
    both = 2 * rows
    expert_id = where_ref[0].astype(F32)
    row_of = lax.broadcasted_iota(jnp.int32, (both, both), 0)
    row_at = lax.broadcasted_iota(jnp.int32, (both, both), 1)
    slot_of = lax.broadcasted_iota(jnp.int32, (slots, both), 0).astype(F32)
    slot_at = lax.broadcasted_iota(jnp.int32, (both, slots), 1).astype(F32)
    for block in range(pick_ref.shape[0]):
        named = [refs[2 * block + i][wrows:].astype(F32) for i in range(2)]
        per_row = named[0].shape[1] // rows
        selected, factor = [], []
        for n in named:
            item = [n[i // per_row : i // per_row + 1, (i % per_row) * rows : (i % per_row + 1) * rows] for i in range(4 * topk)]
            hits = [item[k] == expert_id for k in range(topk)]
            values = [item[topk + k] + item[2 * topk + k] + item[3 * topk + k] for k in range(topk)]
            selected.append(sum(h.astype(F32) for h in hits))
            factor.append(sum(jnp.where(h, v, 0.0) for h, v in zip(hits, values)))
        selected = jnp.concatenate(selected, axis=1)
        factor = jnp.concatenate(factor, axis=1)
        spread = jnp.broadcast_to(selected, (both, both))
        before = jnp.sum(jnp.where(row_at < row_of, spread, 0.0), axis=1, keepdims=True)
        selected_down = jnp.sum(jnp.where(row_at == row_of, spread, 0.0), axis=1, keepdims=True)
        slot_down = jnp.where(selected_down > 0.0, before, -1.0)
        put_ref[block] = (slot_at == slot_down).astype(F32).astype(BF16)
        slot = jnp.sum(jnp.where(row_at == row_of, jnp.broadcast_to(slot_down, (both, both)), 0.0), axis=0, keepdims=True)
        taken = slot_of == slot
        pick_ref[block] = taken.astype(F32).astype(BF16)
        factor_ref[block] = jnp.sum(jnp.where(taken, factor, 0.0), axis=1, keepdims=True)


def tables(wrows, slots, topk, rows, where, blocks):
    chips = len(blocks) // 2
    both = 2 * rows
    return pl.pallas_call(
        functools.partial(tables_kernel, wrows, slots, topk, rows),
        out_shape=[
            jax.ShapeDtypeStruct((chips, slots, both), BF16),
            jax.ShapeDtypeStruct((chips, both, slots), BF16),
            jax.ShapeDtypeStruct((chips, slots, 1), F32),
        ],
        in_specs=[smem()] + [vmem()] * len(blocks),
        out_specs=[vmem()] * 3,
        compiler_params=params(),
        cost_estimate=pl.CostEstimate(flops=0, bytes_accessed=8 * chips * slots * both, transcendentals=0),
        name="tables",
    )(where, *blocks)


def expert_kernel(first, blocks, pieces, gain_ref, pick_ref, put_ref, factor_ref, gate_ref, up_ref, down_ref, *refs):
    slots, rows = pick_ref.shape[1:]
    own = rows // 2
    width = gain_ref.shape[1]
    hidden_units = gate_ref.shape[1]
    inputs = refs[: blocks * pieces]
    mine = refs[blocks * pieces : blocks * pieces + blocks]
    theirs, normed, hidden = refs[-3:]

    for b in range(blocks):
        block = jnp.concatenate([inputs[b * pieces + i][...] for i in range(pieces)], axis=0)
        taken = mm(pick_ref[first + b], block)
        scale = lax.rsqrt(jnp.sum(taken * taken, axis=1, keepdims=True) * (1.0 / width) + 1e-06)
        normed[b * slots : (b + 1) * slots, :] = (taken * scale * gain_ref[...]).astype(BF16)

    for start in range(0, hidden_units, TILE):
        columns = slice(start, min(start + TILE, hidden_units))
        gate_part = mm(normed[...], gate_ref[:, columns])
        up_part = mm(normed[...], up_ref[:, columns])
        hidden[:, columns] = (jax.nn.silu(gate_part) * up_part).astype(BF16)

    for start in range(0, width, TILE):
        columns = slice(start, start + TILE)
        result = mm(hidden[...], down_ref[:, columns])
        for b in range(blocks):
            weighted = (result[b * slots : (b + 1) * slots] * factor_ref[first + b]).astype(BF16)
            placed = mm(put_ref[first + b], weighted).astype(BF16)
            mine[b][:, columns] = placed[:own]
            theirs[b * own : (b + 1) * own, columns] = placed[own:]


def expert(first, blocks, tabs, gain, weights, inputs):
    slots, rows = tabs[0].shape[1:]
    width, hidden_units = weights[0].shape
    own = rows // 2
    m = blocks * slots
    weights = [pltpu.with_memory_space_constraint(w, pltpu.VMEM) for w in weights]
    out = pl.pallas_call(
        functools.partial(expert_kernel, first, blocks, len(inputs) // blocks),
        out_shape=[jax.ShapeDtypeStruct((own, width), BF16)] * blocks
        + [jax.ShapeDtypeStruct((blocks * own, width), BF16)],
        in_specs=[vmem()] * (7 + len(inputs)),
        out_specs=[vmem()] * (blocks + 1),
        scratch_shapes=[
            pltpu.VMEM((m, width), BF16),
            pltpu.VMEM((m, hidden_units), BF16),
        ],
        compiler_params=params(),
        cost_estimate=pl.CostEstimate(
            flops=2 * m * width * hidden_units,
            bytes_accessed=8 * blocks * rows * width,
            transcendentals=m * hidden_units,
        ),
        name="expert",
    )(gain, *tabs, *weights, *inputs)
    return out[:-1], out[-1]


def shared_kernel(count, gain_ref, gate_hbm, up_hbm, down_hbm, *refs):
    inputs, outs = refs[:count], refs[count + 1 : 2 * count + 1]
    gate_ref, up_ref, down_ref, normed, hidden, sems = refs[2 * count + 1 :]
    units, width = gate_ref.shape
    rows = inputs[0].shape[0]
    tiles = [(start, min(256, units - start)) for start in range(0, units, 256)]
    copies = []
    for i, (start, size) in enumerate(tiles):
        span = pl.ds(start, size)
        for j, (source, target) in enumerate(((gate_hbm, gate_ref), (up_hbm, up_ref))):
            copies.append(pltpu.make_async_copy(source.at[span], target.at[span], sems.at[2 * i + j]))
    copies.append(pltpu.make_async_copy(down_hbm, down_ref, sems.at[2 * len(tiles)]))
    for copy in copies:
        copy.start()
    for i, ref in enumerate(inputs):
        x = ref[...].astype(F32)
        scale = lax.rsqrt(jnp.sum(x * x, axis=1, keepdims=True) * (1.0 / width) + 1e-06)
        normed[i * rows : (i + 1) * rows] = (x * scale * gain_ref[...]).astype(BF16)
    across = (((1,), (1,)), ((), ()))
    for i, (start, size) in enumerate(tiles):
        span = slice(start, start + size)
        copies[2 * i].wait()
        copies[2 * i + 1].wait()
        gate_part = lax.dot_general(normed[...], gate_ref[span], across, preferred_element_type=F32)
        up_part = lax.dot_general(normed[...], up_ref[span], across, preferred_element_type=F32)
        hidden[:, span] = (jax.nn.silu(gate_part) * up_part).astype(BF16)
    copies[-1].wait()
    for start in range(0, width, TILE):
        span = slice(start, start + TILE)
        result = mm(hidden[...], down_ref[:, span])
        for i, ref in enumerate(outs):
            ref[:, span] = result[i * rows : (i + 1) * rows].astype(ref.dtype)


def shared_expert(gain, weights, inputs, after):
    count = len(inputs)
    rows, width = inputs[0].shape
    units = weights[0].shape[0]
    weights = [pltpu.with_memory_space_constraint(w, pltpu.HBM) for w in weights]
    shapes = [jax.ShapeDtypeStruct((rows, width), F32)] + [jax.ShapeDtypeStruct((rows, width), BF16)] * (count - 1)
    return pl.pallas_call(
        functools.partial(shared_kernel, count),
        out_shape=shapes,
        in_specs=[vmem()] + [hbm()] * 3 + [vmem()] * count + [hbm()],
        out_specs=[vmem()] * count,
        scratch_shapes=[pltpu.VMEM((units, width), BF16)] * 3
        + [
            pltpu.VMEM((count * rows, width), BF16),
            pltpu.VMEM((count * rows, units), BF16),
            pltpu.SemaphoreType.DMA((2 * -(-units // 256) + 1,)),
        ],
        compiler_params=pltpu.CompilerParams(vmem_limit_bytes=24 * 1024 * 1024),
        cost_estimate=pl.CostEstimate(
            flops=12 * count * rows * width * units,
            bytes_accessed=6 * units * width + 4 * count * rows * width,
            transcendentals=count * rows * units,
        ),
        name="shared",
    )(gain, *weights, *inputs, after)


def base_kernel(*refs):
    total = refs[0][...]
    for ref in refs[1:-1]:
        total = total + ref[...].astype(F32)
    refs[-1][...] = total


def final_kernel(chunks, base_ref, *refs):
    out_ref = refs[-1]
    rows = refs[0].shape[0]
    for chunk in range(chunks):
        span = slice(chunk * rows, (chunk + 1) * rows)
        total = base_ref[span] + refs[chunk][...].astype(F32) + refs[chunks + chunk][...].astype(F32)
        out_ref[span] = total.astype(BF16)


def plain_call(kernel, name, shape, operands):
    return pl.pallas_call(
        kernel,
        out_shape=shape,
        in_specs=[vmem()] * len(operands),
        out_specs=vmem(),
        compiler_params=params(),
        cost_estimate=pl.CostEstimate(flops=0, bytes_accessed=8 * operands[0].size, transcendentals=0),
        name=name,
    )(*operands)


def add_kernel(count, *refs):
    total = refs[0][...].astype(F32)
    for ref in refs[1:count]:
        total = total + ref[...].astype(F32)
    refs[-1][...] = total.astype(BF16)


def add(rows, after, *terms):
    width = terms[0][0].shape[1]

    def block(index):
        return pl.BlockSpec((rows, width), lambda i: (index, 0))

    return pl.pallas_call(
        functools.partial(add_kernel, len(terms)),
        grid=(1,),
        out_shape=jax.ShapeDtypeStruct((rows, width), BF16),
        in_specs=[block(index) for _, index in terms] + [hbm()] * len(after),
        out_specs=block(0),
        compiler_params=params(),
        cost_estimate=pl.CostEstimate(
            flops=rows * width * len(terms), bytes_accessed=2 * rows * width * (len(terms) + 1), transcendentals=0
        ),
        name="add",
    )(*[array for array, _ in terms], *after)


def body(
    req_size,
    exp_size,
    attn_out,
    residual,
    out_weight,
    norm_gain,
    expert_ids,
    gate_weights,
    expert_gate,
    expert_up,
    expert_down,
    shared_gate,
    shared_up,
    shared_down,
):
    rows, width = attn_out.shape
    half = width // 2
    part = half // req_size
    topk = expert_ids.shape[1]
    wrows = out_weight.shape[0]
    capacity = min(rows, 3 * rows * topk // (2 * exp_size))
    slots = -(-2 * capacity // 16) * 16
    chips = exp_size // 2
    depth = chips // 2
    order = ring_order(chips)
    me = lax.axis_index("exp")
    request = lax.axis_index("req")
    here = jnp.stack([me, me % 2, lax.axis_index("req")]).astype(jnp.int32)
    ring = jnp.asarray([order.index(q) for q in range(chips)] + order, jnp.int32)

    steps = [(order[i], order[(i + 1) % chips]) for i in range(chips)]
    ahead = [(2 * a + c, 2 * b + c) for a, b in steps for c in range(2)]
    behind = [(b, a) for a, b in ahead]

    def to_ahead(x):
        return lax.ppermute(x, "exp", ahead)

    def to_behind(x):
        return lax.ppermute(x, "exp", behind)

    def to_core(x):
        return lax.ppermute(x, "exp", [(d, d ^ 1) for d in range(exp_size)])

    def to_request(x, shift, swap=0):
        pairs = [
            (i * exp_size + d, ((i + shift) % req_size) * exp_size + (d ^ swap))
            for i in range(req_size)
            for d in range(exp_size)
        ]
        return lax.ppermute(x, ("req", "exp"), pairs)

    weight_own, weight_sent, packed = prepare(
        req_size, part, here, expert_ids.T, gate_weights.T, out_weight, attn_out, residual
    )
    weight_met = to_core(weight_sent)
    chains = [(weight_own, weight_own), (weight_met, weight_met)]
    arrived = [[weight_own, weight_met]]
    for _ in range(1, depth):
        chains = [(to_ahead(low), to_behind(high)) for low, high in chains]
        (low_own, high_own), (low_met, high_met) = chains
        arrived += [[low_own, low_met], [high_own, high_met]]

    visits = [packed[0]] + [to_request(packed[shift], shift) for shift in range(1, req_size)]
    last = [to_ahead(arrived[-2][0]), to_behind(arrived[-1][1])]
    arrived[-2:], visits[1:] = lax.optimization_barrier((arrived[-2:], visits[1:]))
    visits += [to_core(v) for v in visits]

    early = [w for block in arrived[:-2] for w in block]
    late = last + [w for block in arrived[-2:] for w in block]
    whole = [w for block in arrived for w in block]
    places = [0] + [side * k for k in range(1, depth) for side in (-1, 1)]
    (acc,) = proj(wrows, places, here, ring, visits, whole)
    product = proj(wrows, [depth], here, ring, visits, last, acc)
    product, early = lax.optimization_barrier((product, early))
    tabs_early = tables(wrows, slots, topk, rows, here, early)
    tabs_late = tables(wrows, slots, topk, rows, here, late)

    got = {}
    for shift in reversed(range(req_size)):
        for swap in range(2):
            piece = product[swap * req_size + shift]
            if shift == 0:
                got[shift, swap] = piece if swap == 0 else to_core(piece)
            else:
                got[shift, swap] = to_request(piece, req_size - shift, swap)
    near = beside(here, [got[0, 0], got[0, 1]])
    far, tabs_early, tabs_late = lax.optimization_barrier(
        ([got[place, swap] for place in range(1, req_size) for swap in range(2)], tabs_early, tabs_late)
    )
    far = beside(here, far)
    gain = norm_gain.reshape(1, width)
    weights = [expert_gate[0], expert_up[0], expert_down[0]]

    lows, highs = [to_ahead(near)], [to_behind(near)]
    lows, highs, far = lax.optimization_barrier((lows, highs, far))
    lows.append(to_ahead(far))
    highs.append(to_behind(far))
    own_rows = weave(req_size, here, [near, far])
    results = {0: expert(0, 1, tabs_early, gain, weights, [own_rows, to_core(own_rows)])}
    lows, highs, results[0] = lax.optimization_barrier((lows, highs, results[0]))
    low, high = weave(req_size, here, lows), weave(req_size, here, highs)
    came = {}
    theirs = results[0][1]
    for k in range(1, depth):
        if k > 1:
            low, high, results[k - 1], came[k - 2] = lax.optimization_barrier(
                (low, high, results[k - 1], came[k - 2])
            )
            theirs = results[k - 1][1]
        if k == min(2, depth - 1):
            low, high, shared_rows = lax.optimization_barrier((low, high, shared_rows))
        others = to_core(low), to_core(high)
        came[k - 1] = to_core(theirs)
        if k == 1:
            others, own_rows = lax.optimization_barrier((others, own_rows))
            shared_rows = [own_rows]
            for shift in range(1, req_size):
                shared_rows.append(to_request(own_rows, shift))
        first, tabs = (2 * k - 1, tabs_early) if k < depth - 1 else (1, tabs_late)
        results[k] = expert(first, 2, tabs, gain, weights, [low, others[0], high, others[1]])
        if k < depth - 1:
            low, high = to_ahead(low), to_behind(high)
        else:
            low, high = to_ahead(low[: rows // 2]), to_behind(high[rows // 2 :])
    low, high, results[depth - 1], came[depth - 2] = lax.optimization_barrier(
        (low, high, results[depth - 1], came[depth - 2])
    )
    results[depth] = expert(0, 1, tabs_late, gain, weights, [low, high, to_core(low), to_core(high)])

    cut = rows // 2
    came[depth - 1], came[depth] = to_core(results[depth - 1][1]), to_core(results[depth][1])

    def step(after, k, low_chunk, low, high):
        low_mine, high_mine = results[k][0]
        low_terms = [(low_mine, low_chunk), (came[k], low_chunk)] + [(x, 0) for x in low]
        high_terms = [(high_mine, 1 - low_chunk), (came[k], 3 - low_chunk)] + [(x, 0) for x in high]
        low_sum = add(cut, after, *low_terms)
        high_sum = add(cut, [low_sum], *high_terms)
        return [high_sum], [to_behind(low_sum)], [to_ahead(high_sum)]

    (mine,), _ = results[depth]
    low_sum = add(cut, [], (mine, 1), (came[depth], 1))
    high_sum = add(cut, [low_sum], (mine, 0), (came[depth], 0))
    first = [to_behind(low_sum)], [to_ahead(high_sum)]
    second = [], []
    after = [high_sum]
    for k in range(depth - 1, 0, -1):
        if k == 1:
            (mine,), _ = results[0]
            backs = [to_request(shared[shift], req_size - shift) for shift in range(1, req_size)]
            terms = [shared[0], own_rows, mine, came[0]] + backs
            base = plain_call(base_kernel, "base", jax.ShapeDtypeStruct((rows, width), F32), terms)
            after = after + [base]
        after, *second = step(after, k, 0, *second)
        if k == depth - 1:
            shared = shared_expert(gain, [shared_gate.T, shared_up.T, shared_down.T], shared_rows, after[0])
            after = [shared[0]]
        after, *first = step(after, k, 1, *first)
    low, high = [second[0][0], first[0][0]], [first[1][0], second[1][0]]
    return plain_call(
        functools.partial(final_kernel, 2), "final", jax.ShapeDtypeStruct((rows, width), BF16), [base] + low + high
    )


def solution(mesh):
    return jax.shard_map(
        functools.partial(body, mesh.shape["req"], mesh.shape["exp"]),
        mesh=mesh,
        in_specs=(
            P(("req", "exp"), None),
            P(("req", "exp"), None),
            P("exp", None),
            P(),
            P(("req", "exp"), None),
            P(("req", "exp"), None),
            P("exp", None, None),
            P("exp", None, None),
            P("exp", None, None),
            P(None, "req"),
            P(None, "req"),
            P(None, "req"),
        ),
        out_specs=P(("req", "exp"), None),
        check_vma=False,
    )
```

```python
import functools

import jax
import jax.numpy as jnp
from jax import lax
from jax.experimental import pallas as pl
from jax.experimental.pallas import tpu as pltpu
from jax.sharding import PartitionSpec as P

F32 = jnp.float32
BF16 = jnp.bfloat16
VMEM_BYTES = 12 * 1024 * 1024
TILE = 512
TABLE_ROWS = 16


def ring_order(chips):
    slow = 4
    fast = chips // slow
    order = [a * fast for a in range(slow)]
    for turn, a in enumerate(reversed(range(slow))):
        inner = range(1, fast) if turn % 2 == 0 else range(fast - 1, 0, -1)
        order += [a * fast + b for b in inner]
    return order


def mm(a, b):
    return jnp.dot(a, b, preferred_element_type=F32)


def vmem():
    return pl.BlockSpec(memory_space=pltpu.VMEM)


def smem():
    return pl.BlockSpec(memory_space=pltpu.SMEM)


def hbm():
    return pl.BlockSpec(memory_space=pl.ANY)


def params():
    return pltpu.CompilerParams(vmem_limit_bytes=VMEM_BYTES)


def prepare_kernel(count, part, where_ref, ids_hbm, factors_hbm, weight_hbm, attn_hbm, residual_hbm, own_ref, sent_ref, *refs):
    packs = refs[:count]
    ids_ref, factors_ref, sems = refs[count:]
    wrows, width = weight_hbm.shape
    topk, rows = ids_ref.shape
    core, request = where_ref[1], where_ref[2]
    moves = [(ids_hbm, ids_ref), (factors_hbm, factors_ref)]
    for ref, which in ((own_ref, core), (sent_ref, 1 - core)):
        start = pl.multiple_of(which * (width // 2) + request * part, 128)
        moves.append((weight_hbm.at[:, pl.ds(start, part)], ref.at[:wrows]))
    for shift, ref in enumerate(packs):
        moves.append((attn_hbm, ref.at[:, :width]))
        other = lax.rem(request + shift, count)
        for half in range(2):
            start = pl.multiple_of(half * (width // 2) + other * part, 128)
            target = ref.at[:, width + half * part : width + (half + 1) * part]
            moves.append((residual_hbm.at[:, pl.ds(start, part)], target))
    copies = [pltpu.make_async_copy(source, target, sems.at[i]) for i, (source, target) in enumerate(moves)]
    for copy in copies:
        copy.start()
    for copy in copies[:2]:
        copy.wait()
    per_row = part // rows
    factors = factors_ref[...]
    big = factors.astype(BF16).astype(F32)
    middle = (factors - big).astype(BF16).astype(F32)
    named = (ids_ref[...].astype(F32), big, middle, factors - big - middle)
    items = [kind[k : k + 1] for kind in named for k in range(topk)]
    items += [jnp.zeros((1, rows), F32)] * (-len(items) % per_row)
    lines = [jnp.concatenate(items[i : i + per_row], axis=1) for i in range(0, len(items), per_row)]
    lines.append(jnp.zeros((TABLE_ROWS - len(lines), part), F32))
    table = jnp.concatenate(lines, axis=0).astype(BF16)
    own_ref[wrows:] = table
    sent_ref[wrows:] = table
    for copy in copies[2:]:
        copy.wait()


def prepare(count, part, where, ids, factors, weight, attn, residual):
    rows, width = attn.shape
    shape = jax.ShapeDtypeStruct((weight.shape[0] + TABLE_ROWS, part), BF16)
    packed = jax.ShapeDtypeStruct((rows, width + 2 * part), BF16)
    arrays = [pltpu.with_memory_space_constraint(x, pltpu.HBM) for x in (ids, factors, weight, attn, residual)]
    out = pl.pallas_call(
        functools.partial(prepare_kernel, count, part),
        out_shape=[shape] * 2 + [packed] * count,
        in_specs=[smem()] + [hbm()] * 5,
        out_specs=[vmem()] * (2 + count),
        scratch_shapes=[
            pltpu.VMEM(ids.shape, ids.dtype),
            pltpu.VMEM(factors.shape, factors.dtype),
            pltpu.SemaphoreType.DMA((4 + 3 * count,)),
        ],
        compiler_params=params(),
        cost_estimate=pl.CostEstimate(flops=0, bytes_accessed=8 * attn.size, transcendentals=0),
        name="prepare",
    )(where, *arrays)
    return out[0], out[1], out[2:]


def small_call(kernel, name, shapes, operands, moved):
    return pl.pallas_call(
        kernel,
        out_shape=shapes,
        in_specs=[smem()] + [vmem()] * (len(operands) - 1),
        out_specs=[vmem()] * len(shapes),
        compiler_params=params(),
        cost_estimate=pl.CostEstimate(flops=0, bytes_accessed=moved, transcendentals=0),
        name=name,
    )(*operands)


def beside_kernel(where_ref, *refs):
    part = refs[0].shape[1]
    for i, ref in enumerate(refs[:-1]):
        refs[-1][:, i * part : (i + 1) * part] = ref[...]


def beside(where, pieces):
    rows, part = pieces[0].shape
    shape = jax.ShapeDtypeStruct((rows, len(pieces) * part), BF16)
    return small_call(beside_kernel, "beside", [shape], [where] + pieces, 4 * rows * part * len(pieces))[0]


def weave_kernel(count, where_ref, *refs):
    out_ref = refs[-1]
    part = out_ref.shape[1] // (2 * count)
    place = 0
    for ref in refs[:-1]:
        for at in range(ref.shape[1] // (2 * part)):
            request = lax.rem(where_ref[2] + place, count)
            place += 1
            for swap in range(2):
                core = where_ref[1] if swap == 0 else 1 - where_ref[1]
                start = pl.multiple_of(core * (count * part) + request * part, 128)
                out_ref[:, pl.ds(start, part)] = ref[:, (2 * at + swap) * part : (2 * at + swap + 1) * part]


def weave(count, where, pieces):
    rows = pieces[0].shape[0]
    width = sum(p.shape[1] for p in pieces)
    shape = jax.ShapeDtypeStruct((rows, width), BF16)
    return small_call(functools.partial(weave_kernel, count), "weave", [shape], [where] + pieces, 4 * rows * width)[0]


def proj_kernel(wrows, part, blocks, visits, final, where_ref, ring_ref, *refs):
    total = None
    rows_refs = refs[:visits]
    width = rows_refs[0].shape[1] - 2 * part
    at = visits
    chips = ring_ref.shape[0] // 2
    position = ring_ref[where_ref[0] // 2]
    first_core = where_ref[1] == 0
    for offset in blocks:
        chip = ring_ref[chips + lax.rem(position + offset + chips, chips)]
        start = pl.multiple_of(chip * 2 * wrows, 128)
        columns = jnp.concatenate([r[:, pl.ds(start, 2 * wrows)] for r in rows_refs], axis=0)
        mine, other = refs[at][:wrows], refs[at + 1][:wrows]
        at += 2
        weight = jnp.concatenate([jnp.where(first_core, mine, other), jnp.where(first_core, other, mine)], axis=0)
        term = mm(columns, weight)
        total = term if total is None else total + term
    if final:
        total = total + refs[at][...]
        start = pl.multiple_of(width + where_ref[1] * part, 128)
        rows = rows_refs[0].shape[0]
        for i, out_ref in enumerate(refs[at + 1 :]):
            residual = rows_refs[i][:, pl.ds(start, part)].astype(F32)
            out_ref[...] = (residual + total[i * rows : (i + 1) * rows]).astype(BF16)
    else:
        refs[at][...] = total


def proj(wrows, blocks, where, ring, visits, weights, acc=None):
    final = acc is not None
    rows, part = visits[0].shape[0], weights[0].shape[1]
    operands = [where, ring] + visits + weights + ([acc] if final else [])
    count = len(visits)
    if final:
        outs = [jax.ShapeDtypeStruct((rows, part), BF16)] * count
    else:
        outs = [jax.ShapeDtypeStruct((rows * count, part), F32)]
    return pl.pallas_call(
        functools.partial(proj_kernel, wrows, part, blocks, count, final),
        out_shape=outs,
        in_specs=[smem()] * 2 + [vmem()] * (len(operands) - 2),
        out_specs=[vmem()] * len(outs),
        compiler_params=params(),
        cost_estimate=pl.CostEstimate(
            flops=8 * rows * count * part * wrows * len(blocks),
            bytes_accessed=4 * part * wrows * len(blocks) + 8 * rows * count * part,
            transcendentals=0,
        ),
        name="proj_final" if final else "proj_part",
    )(*operands)


def tables_kernel(wrows, slots, topk, rows, where_ref, *refs):
    pick_ref, put_ref, factor_ref = refs[-3:]
    both = 2 * rows
    expert_id = where_ref[0].astype(F32)
    row_of = lax.broadcasted_iota(jnp.int32, (both, both), 0)
    row_at = lax.broadcasted_iota(jnp.int32, (both, both), 1)
    slot_of = lax.broadcasted_iota(jnp.int32, (slots, both), 0).astype(F32)
    slot_at = lax.broadcasted_iota(jnp.int32, (both, slots), 1).astype(F32)
    for block in range(pick_ref.shape[0]):
        named = [refs[2 * block + i][wrows:].astype(F32) for i in range(2)]
        per_row = named[0].shape[1] // rows
        selected, factor = [], []
        for n in named:
            item = [n[i // per_row : i // per_row + 1, (i % per_row) * rows : (i % per_row + 1) * rows] for i in range(4 * topk)]
            hits = [item[k] == expert_id for k in range(topk)]
            values = [item[topk + k] + item[2 * topk + k] + item[3 * topk + k] for k in range(topk)]
            selected.append(sum(h.astype(F32) for h in hits))
            factor.append(sum(jnp.where(h, v, 0.0) for h, v in zip(hits, values)))
        selected = jnp.concatenate(selected, axis=1)
        factor = jnp.concatenate(factor, axis=1)
        spread = jnp.broadcast_to(selected, (both, both))
        before = jnp.sum(jnp.where(row_at < row_of, spread, 0.0), axis=1, keepdims=True)
        selected_down = jnp.sum(jnp.where(row_at == row_of, spread, 0.0), axis=1, keepdims=True)
        slot_down = jnp.where(selected_down > 0.0, before, -1.0)
        put_ref[block] = (slot_at == slot_down).astype(F32).astype(BF16)
        slot = jnp.sum(jnp.where(row_at == row_of, jnp.broadcast_to(slot_down, (both, both)), 0.0), axis=0, keepdims=True)
        taken = slot_of == slot
        pick_ref[block] = taken.astype(F32).astype(BF16)
        factor_ref[block] = jnp.sum(jnp.where(taken, factor, 0.0), axis=1, keepdims=True)


def tables(wrows, slots, topk, rows, where, blocks):
    chips = len(blocks) // 2
    both = 2 * rows
    return pl.pallas_call(
        functools.partial(tables_kernel, wrows, slots, topk, rows),
        out_shape=[
            jax.ShapeDtypeStruct((chips, slots, both), BF16),
            jax.ShapeDtypeStruct((chips, both, slots), BF16),
            jax.ShapeDtypeStruct((chips, slots, 1), F32),
        ],
        in_specs=[smem()] + [vmem()] * len(blocks),
        out_specs=[vmem()] * 3,
        compiler_params=params(),
        cost_estimate=pl.CostEstimate(flops=0, bytes_accessed=8 * chips * slots * both, transcendentals=0),
        name="tables",
    )(where, *blocks)


def expert_kernel(first, blocks, pieces, gain_ref, pick_ref, put_ref, factor_ref, gate_ref, up_ref, down_ref, *refs):
    slots, rows = pick_ref.shape[1:]
    own = rows // 2
    width = gain_ref.shape[1]
    hidden_units = gate_ref.shape[1]
    inputs = refs[: blocks * pieces]
    mine = refs[blocks * pieces : blocks * pieces + blocks]
    theirs, normed, hidden = refs[-3:]

    for b in range(blocks):
        block = jnp.concatenate([inputs[b * pieces + i][...] for i in range(pieces)], axis=0)
        taken = mm(pick_ref[first + b], block)
        scale = lax.rsqrt(jnp.sum(taken * taken, axis=1, keepdims=True) * (1.0 / width) + 1e-06)
        normed[b * slots : (b + 1) * slots, :] = (taken * scale * gain_ref[...]).astype(BF16)

    for start in range(0, hidden_units, TILE):
        columns = slice(start, min(start + TILE, hidden_units))
        gate_part = mm(normed[...], gate_ref[:, columns])
        up_part = mm(normed[...], up_ref[:, columns])
        hidden[:, columns] = (jax.nn.silu(gate_part) * up_part).astype(BF16)

    for start in range(0, width, TILE):
        columns = slice(start, start + TILE)
        result = mm(hidden[...], down_ref[:, columns])
        for b in range(blocks):
            weighted = (result[b * slots : (b + 1) * slots] * factor_ref[first + b]).astype(BF16)
            placed = mm(put_ref[first + b], weighted).astype(BF16)
            mine[b][:, columns] = placed[:own]
            theirs[b * own : (b + 1) * own, columns] = placed[own:]


def expert(first, blocks, tabs, gain, weights, inputs):
    slots, rows = tabs[0].shape[1:]
    width, hidden_units = weights[0].shape
    own = rows // 2
    m = blocks * slots
    weights = [pltpu.with_memory_space_constraint(w, pltpu.VMEM) for w in weights]
    out = pl.pallas_call(
        functools.partial(expert_kernel, first, blocks, len(inputs) // blocks),
        out_shape=[jax.ShapeDtypeStruct((own, width), BF16)] * blocks
        + [jax.ShapeDtypeStruct((blocks * own, width), BF16)],
        in_specs=[vmem()] * (7 + len(inputs)),
        out_specs=[vmem()] * (blocks + 1),
        scratch_shapes=[
            pltpu.VMEM((m, width), BF16),
            pltpu.VMEM((m, hidden_units), BF16),
        ],
        compiler_params=params(),
        cost_estimate=pl.CostEstimate(
            flops=2 * m * width * hidden_units,
            bytes_accessed=8 * blocks * rows * width,
            transcendentals=m * hidden_units,
        ),
        name="expert",
    )(gain, *tabs, *weights, *inputs)
    return out[:-1], out[-1]


def shared_kernel(count, gain_ref, gate_hbm, up_hbm, down_hbm, *refs):
    inputs, outs = refs[:count], refs[count + 1 : 2 * count + 1]
    gate_ref, up_ref, down_ref, normed, hidden, sems = refs[2 * count + 1 :]
    units, width = gate_ref.shape
    rows = inputs[0].shape[0]
    tiles = [(start, min(256, units - start)) for start in range(0, units, 256)]
    copies = []
    for i, (start, size) in enumerate(tiles):
        span = pl.ds(start, size)
        for j, (source, target) in enumerate(((gate_hbm, gate_ref), (up_hbm, up_ref))):
            copies.append(pltpu.make_async_copy(source.at[span], target.at[span], sems.at[2 * i + j]))
    copies.append(pltpu.make_async_copy(down_hbm, down_ref, sems.at[2 * len(tiles)]))
    for copy in copies:
        copy.start()
    for i, ref in enumerate(inputs):
        x = ref[...].astype(F32)
        scale = lax.rsqrt(jnp.sum(x * x, axis=1, keepdims=True) * (1.0 / width) + 1e-06)
        normed[i * rows : (i + 1) * rows] = (x * scale * gain_ref[...]).astype(BF16)
    across = (((1,), (1,)), ((), ()))
    for i, (start, size) in enumerate(tiles):
        span = slice(start, start + size)
        copies[2 * i].wait()
        copies[2 * i + 1].wait()
        gate_part = lax.dot_general(normed[...], gate_ref[span], across, preferred_element_type=F32)
        up_part = lax.dot_general(normed[...], up_ref[span], across, preferred_element_type=F32)
        hidden[:, span] = (jax.nn.silu(gate_part) * up_part).astype(BF16)
    copies[-1].wait()
    for start in range(0, width, TILE):
        span = slice(start, start + TILE)
        result = mm(hidden[...], down_ref[:, span])
        for i, ref in enumerate(outs):
            ref[:, span] = result[i * rows : (i + 1) * rows].astype(ref.dtype)


def shared_expert(gain, weights, inputs, after):
    count = len(inputs)
    rows, width = inputs[0].shape
    units = weights[0].shape[0]
    weights = [pltpu.with_memory_space_constraint(w, pltpu.HBM) for w in weights]
    shapes = [jax.ShapeDtypeStruct((rows, width), F32)] + [jax.ShapeDtypeStruct((rows, width), BF16)] * (count - 1)
    return pl.pallas_call(
        functools.partial(shared_kernel, count),
        out_shape=shapes,
        in_specs=[vmem()] + [hbm()] * 3 + [vmem()] * count + [hbm()],
        out_specs=[vmem()] * count,
        scratch_shapes=[pltpu.VMEM((units, width), BF16)] * 3
        + [
            pltpu.VMEM((count * rows, width), BF16),
            pltpu.VMEM((count * rows, units), BF16),
            pltpu.SemaphoreType.DMA((2 * -(-units // 256) + 1,)),
        ],
        compiler_params=pltpu.CompilerParams(vmem_limit_bytes=24 * 1024 * 1024),
        cost_estimate=pl.CostEstimate(
            flops=12 * count * rows * width * units,
            bytes_accessed=6 * units * width + 4 * count * rows * width,
            transcendentals=count * rows * units,
        ),
        name="shared",
    )(gain, *weights, *inputs, after)


def base_kernel(*refs):
    total = refs[0][...]
    for ref in refs[1:-1]:
        total = total + ref[...].astype(F32)
    refs[-1][...] = total


def half_sum_kernel(base_ref, top_ref, bottom_ref, out_ref):
    rows = top_ref.shape[0]
    for span, ref in ((slice(0, rows), top_ref), (slice(rows, 2 * rows), bottom_ref)):
        out_ref[span] = (base_ref[span] + ref[...].astype(F32)).astype(out_ref.dtype)


def plain_call(kernel, name, shape, operands):
    return pl.pallas_call(
        kernel,
        out_shape=shape,
        in_specs=[vmem()] * len(operands),
        out_specs=vmem(),
        compiler_params=params(),
        cost_estimate=pl.CostEstimate(flops=0, bytes_accessed=8 * operands[0].size, transcendentals=0),
        name=name,
    )(*operands)


def add_kernel(count, *refs):
    total = refs[0][...].astype(F32)
    for ref in refs[1:count]:
        total = total + ref[...].astype(F32)
    refs[-1][...] = total.astype(BF16)


def add(rows, after, *terms):
    width = terms[0][0].shape[1]

    def block(index):
        return pl.BlockSpec((rows, width), lambda i: (index, 0))

    return pl.pallas_call(
        functools.partial(add_kernel, len(terms)),
        grid=(1,),
        out_shape=jax.ShapeDtypeStruct((rows, width), BF16),
        in_specs=[block(index) for _, index in terms] + [hbm()] * len(after),
        out_specs=block(0),
        compiler_params=params(),
        cost_estimate=pl.CostEstimate(
            flops=rows * width * len(terms), bytes_accessed=2 * rows * width * (len(terms) + 1), transcendentals=0
        ),
        name="add",
    )(*[array for array, _ in terms], *after)


def body(
    req_size,
    exp_size,
    attn_out,
    residual,
    out_weight,
    norm_gain,
    expert_ids,
    gate_weights,
    expert_gate,
    expert_up,
    expert_down,
    shared_gate,
    shared_up,
    shared_down,
):
    rows, width = attn_out.shape
    half = width // 2
    part = half // req_size
    topk = expert_ids.shape[1]
    wrows = out_weight.shape[0]
    capacity = min(rows, 3 * rows * topk // (2 * exp_size))
    slots = -(-2 * capacity // 16) * 16
    chips = exp_size // 2
    depth = chips // 2
    order = ring_order(chips)
    me = lax.axis_index("exp")
    request = lax.axis_index("req")
    here = jnp.stack([me, me % 2, lax.axis_index("req")]).astype(jnp.int32)
    ring = jnp.asarray([order.index(q) for q in range(chips)] + order, jnp.int32)

    steps = [(order[i], order[(i + 1) % chips]) for i in range(chips)]
    ahead = [(2 * a + c, 2 * b + c) for a, b in steps for c in range(2)]
    behind = [(b, a) for a, b in ahead]

    def to_ahead(x):
        return lax.ppermute(x, "exp", ahead)

    def to_behind(x):
        return lax.ppermute(x, "exp", behind)

    def to_core(x):
        return lax.ppermute(x, "exp", [(d, d ^ 1) for d in range(exp_size)])

    def to_request(x, shift, swap=0):
        pairs = [
            (i * exp_size + d, ((i + shift) % req_size) * exp_size + (d ^ swap))
            for i in range(req_size)
            for d in range(exp_size)
        ]
        return lax.ppermute(x, ("req", "exp"), pairs)

    weight_own, weight_sent, packed = prepare(
        req_size, part, here, expert_ids.T, gate_weights.T, out_weight, attn_out, residual
    )
    weight_met = to_core(weight_sent)
    chains = [(weight_own, weight_own), (weight_met, weight_met)]
    arrived = [[weight_own, weight_met]]
    for _ in range(1, depth):
        chains = [(to_ahead(low), to_behind(high)) for low, high in chains]
        (low_own, high_own), (low_met, high_met) = chains
        arrived += [[low_own, low_met], [high_own, high_met]]

    visits = [packed[0]] + [to_request(packed[shift], shift) for shift in range(1, req_size)]
    last = [to_ahead(arrived[-2][0]), to_behind(arrived[-1][1])]
    arrived[-2:], visits[1:] = lax.optimization_barrier((arrived[-2:], visits[1:]))
    visits += [to_core(v) for v in visits]

    early = [w for block in arrived[:-2] for w in block]
    late = last + [w for block in arrived[-2:] for w in block]
    whole = [w for block in arrived for w in block]
    places = [0] + [side * k for k in range(1, depth) for side in (-1, 1)]
    (acc,) = proj(wrows, places, here, ring, visits, whole)
    product = proj(wrows, [depth], here, ring, visits, last, acc)
    product, early = lax.optimization_barrier((product, early))
    tabs_early = tables(wrows, slots, topk, rows, here, early)
    tabs_late = tables(wrows, slots, topk, rows, here, late)

    got = {}
    for shift in reversed(range(req_size)):
        for swap in range(2):
            piece = product[swap * req_size + shift]
            if shift == 0:
                got[shift, swap] = piece if swap == 0 else to_core(piece)
            else:
                got[shift, swap] = to_request(piece, req_size - shift, swap)
    near = beside(here, [got[0, 0], got[0, 1]])
    far, tabs_early, tabs_late = lax.optimization_barrier(
        ([got[place, swap] for place in range(1, req_size) for swap in range(2)], tabs_early, tabs_late)
    )
    far = beside(here, far)
    gain = norm_gain.reshape(1, width)
    weights = [expert_gate[0], expert_up[0], expert_down[0]]

    lows, highs = [to_ahead(near)], [to_behind(near)]
    lows, highs, far = lax.optimization_barrier((lows, highs, far))
    lows.append(to_ahead(far))
    highs.append(to_behind(far))
    own_rows = weave(req_size, here, [near, far])
    results = {0: expert(0, 1, tabs_early, gain, weights, [own_rows, to_core(own_rows)])}
    lows, highs, results[0] = lax.optimization_barrier((lows, highs, results[0]))
    low, high = weave(req_size, here, lows), weave(req_size, here, highs)
    came = {}
    theirs = results[0][1]
    for k in range(1, depth):
        if k > 1:
            low, high, results[k - 1] = lax.optimization_barrier((low, high, results[k - 1]))
            if k == 2:
                low, high, came[0] = lax.optimization_barrier((low, high, came[0]))
            theirs = results[k - 1][1]
        if k == depth - 1:
            low, high, shared_rows = lax.optimization_barrier((low, high, shared_rows))
        others = to_core(low), to_core(high)
        if k == depth - 1:
            others, theirs = lax.optimization_barrier((others, theirs))
        came[k - 1] = to_core(theirs)
        if k == 1:
            shared_rows = [own_rows]
            for shift in range(1, req_size):
                shared_rows.append(to_request(own_rows, shift))
        first, tabs = (2 * k - 1, tabs_early) if k < depth - 1 else (1, tabs_late)
        results[k] = expert(first, 2, tabs, gain, weights, [low, others[0], high, others[1]])
        if k < depth - 1:
            low, high = to_ahead(low), to_behind(high)
        else:
            low, high = to_ahead(low[: rows // 2]), to_behind(high[rows // 2 :])
    low, high, results[depth - 1], came[1] = lax.optimization_barrier((low, high, results[depth - 1], came[1]))
    results[depth] = expert(0, 1, tabs_late, gain, weights, [low, high, to_core(low), to_core(high)])

    cut = rows // 2
    came, results[depth] = lax.optimization_barrier((came, results[depth]))
    came[depth - 1], came[depth] = to_core(results[depth - 1][1]), to_core(results[depth][1])

    def step(after, k, low_chunk, low, high):
        low_mine, high_mine = results[k][0]
        low_terms = [(low_mine, low_chunk), (came[k], low_chunk)] + [(x, 0) for x in low]
        high_terms = [(high_mine, 1 - low_chunk), (came[k], 3 - low_chunk)] + [(x, 0) for x in high]
        low_sum = add(cut, after, *low_terms)
        high_sum = add(cut, [low_sum], *high_terms)
        return [high_sum], [to_behind(low_sum)], [to_ahead(high_sum)]

    (mine,), _ = results[depth]
    low_sum = add(cut, [], (mine, 1), (came[depth], 1))
    high_sum = add(cut, [low_sum], (mine, 0), (came[depth], 0))
    first = [to_behind(low_sum)], [to_ahead(high_sum)]
    second = [], []
    after = [high_sum]
    for k in range(depth - 1, 0, -1):
        if k == 1:
            (mine,), _ = results[0]
            backs = [to_request(shared[shift], req_size - shift) for shift in range(1, req_size)]
            terms = [shared[0], own_rows, mine, came[0]] + backs
            base = plain_call(base_kernel, "base", jax.ShapeDtypeStruct((rows, width), F32), terms)
            after = after + [base]
        after, *second = step(after, k, 0, *second)
        if k == depth - 1:
            shared = shared_expert(gain, [shared_gate.T, shared_up.T, shared_down.T], shared_rows, after[0])
            after = [shared[0]]
        after, *first = step(after, k, 1, *first)
    shape = base.shape
    part_sum = plain_call(
        half_sum_kernel, "part_sum", jax.ShapeDtypeStruct(shape, F32), [base, second[0][0], second[1][0]]
    )
    return plain_call(
        half_sum_kernel, "final", jax.ShapeDtypeStruct(shape, BF16), [part_sum, first[1][0], first[0][0]]
    )


def solution(mesh):
    return jax.shard_map(
        functools.partial(body, mesh.shape["req"], mesh.shape["exp"]),
        mesh=mesh,
        in_specs=(
            P(("req", "exp"), None),
            P(("req", "exp"), None),
            P("exp", None),
            P(),
            P(("req", "exp"), None),
            P(("req", "exp"), None),
            P("exp", None, None),
            P("exp", None, None),
            P("exp", None, None),
            P(None, "req"),
            P(None, "req"),
            P(None, "req"),
        ),
        out_specs=P(("req", "exp"), None),
        check_vma=False,
    )
```

```python
import functools

import jax
import jax.numpy as jnp
from jax import lax
from jax.experimental import pallas as pl
from jax.experimental.pallas import tpu as pltpu
from jax.sharding import PartitionSpec as P

F32 = jnp.float32
BF16 = jnp.bfloat16
VMEM_BYTES = 12 * 1024 * 1024
TILE = 512
TABLE_ROWS = 16


def ring_order(chips):
    slow = 4
    fast = chips // slow
    order = [a * fast for a in range(slow)]
    for turn, a in enumerate(reversed(range(slow))):
        inner = range(1, fast) if turn % 2 == 0 else range(fast - 1, 0, -1)
        order += [a * fast + b for b in inner]
    return order


def mm(a, b):
    return jnp.dot(a, b, preferred_element_type=F32)


def vmem():
    return pl.BlockSpec(memory_space=pltpu.VMEM)


def smem():
    return pl.BlockSpec(memory_space=pltpu.SMEM)


def hbm():
    return pl.BlockSpec(memory_space=pl.ANY)


def params():
    return pltpu.CompilerParams(vmem_limit_bytes=VMEM_BYTES)


def prepare_kernel(count, part, where_ref, ids_hbm, factors_hbm, weight_hbm, attn_hbm, residual_hbm, own_ref, sent_ref, *refs):
    packs = refs[:count]
    ids_ref, factors_ref, sems = refs[count:]
    wrows, width = weight_hbm.shape
    topk, rows = ids_ref.shape
    core, request = where_ref[1], where_ref[2]
    moves = [(ids_hbm, ids_ref), (factors_hbm, factors_ref)]
    for ref, which in ((own_ref, core), (sent_ref, 1 - core)):
        start = pl.multiple_of(which * (width // 2) + request * part, 128)
        moves.append((weight_hbm.at[:, pl.ds(start, part)], ref.at[:wrows]))
    for shift, ref in enumerate(packs):
        moves.append((attn_hbm, ref.at[:, :width]))
        other = lax.rem(request + shift, count)
        for half in range(2):
            start = pl.multiple_of(half * (width // 2) + other * part, 128)
            target = ref.at[:, width + half * part : width + (half + 1) * part]
            moves.append((residual_hbm.at[:, pl.ds(start, part)], target))
    copies = [pltpu.make_async_copy(source, target, sems.at[i]) for i, (source, target) in enumerate(moves)]
    for copy in copies:
        copy.start()
    for copy in copies[:2]:
        copy.wait()
    per_row = part // rows
    factors = factors_ref[...]
    big = factors.astype(BF16).astype(F32)
    middle = (factors - big).astype(BF16).astype(F32)
    named = (ids_ref[...].astype(F32), big, middle, factors - big - middle)
    items = [kind[k : k + 1] for kind in named for k in range(topk)]
    items += [jnp.zeros((1, rows), F32)] * (-len(items) % per_row)
    lines = [jnp.concatenate(items[i : i + per_row], axis=1) for i in range(0, len(items), per_row)]
    lines.append(jnp.zeros((TABLE_ROWS - len(lines), part), F32))
    table = jnp.concatenate(lines, axis=0).astype(BF16)
    own_ref[wrows:] = table
    sent_ref[wrows:] = table
    for copy in copies[2:]:
        copy.wait()


def prepare(count, part, where, ids, factors, weight, attn, residual):
    rows, width = attn.shape
    shape = jax.ShapeDtypeStruct((weight.shape[0] + TABLE_ROWS, part), BF16)
    packed = jax.ShapeDtypeStruct((rows, width + 2 * part), BF16)
    arrays = [pltpu.with_memory_space_constraint(x, pltpu.HBM) for x in (ids, factors, weight, attn, residual)]
    out = pl.pallas_call(
        functools.partial(prepare_kernel, count, part),
        out_shape=[shape] * 2 + [packed] * count,
        in_specs=[smem()] + [hbm()] * 5,
        out_specs=[vmem()] * (2 + count),
        scratch_shapes=[
            pltpu.VMEM(ids.shape, ids.dtype),
            pltpu.VMEM(factors.shape, factors.dtype),
            pltpu.SemaphoreType.DMA((4 + 3 * count,)),
        ],
        compiler_params=params(),
        cost_estimate=pl.CostEstimate(flops=0, bytes_accessed=8 * attn.size, transcendentals=0),
        name="prepare",
    )(where, *arrays)
    return out[0], out[1], out[2:]


def small_call(kernel, name, shapes, operands, moved):
    return pl.pallas_call(
        kernel,
        out_shape=shapes,
        in_specs=[smem()] + [vmem()] * (len(operands) - 1),
        out_specs=[vmem()] * len(shapes),
        compiler_params=params(),
        cost_estimate=pl.CostEstimate(flops=0, bytes_accessed=moved, transcendentals=0),
        name=name,
    )(*operands)


def beside_kernel(where_ref, *refs):
    part = refs[0].shape[1]
    for i, ref in enumerate(refs[:-1]):
        refs[-1][:, i * part : (i + 1) * part] = ref[...]


def beside(where, pieces):
    rows, part = pieces[0].shape
    shape = jax.ShapeDtypeStruct((rows, len(pieces) * part), BF16)
    return small_call(beside_kernel, "beside", [shape], [where] + pieces, 4 * rows * part * len(pieces))[0]


def weave_kernel(count, where_ref, *refs):
    out_ref = refs[-1]
    part = out_ref.shape[1] // (2 * count)
    place = 0
    for ref in refs[:-1]:
        for at in range(ref.shape[1] // (2 * part)):
            request = lax.rem(where_ref[2] + place, count)
            place += 1
            for swap in range(2):
                core = where_ref[1] if swap == 0 else 1 - where_ref[1]
                start = pl.multiple_of(core * (count * part) + request * part, 128)
                out_ref[:, pl.ds(start, part)] = ref[:, (2 * at + swap) * part : (2 * at + swap + 1) * part]


def weave(count, where, pieces):
    rows = pieces[0].shape[0]
    width = sum(p.shape[1] for p in pieces)
    shape = jax.ShapeDtypeStruct((rows, width), BF16)
    return small_call(functools.partial(weave_kernel, count), "weave", [shape], [where] + pieces, 4 * rows * width)[0]


def proj_kernel(wrows, part, blocks, visits, final, where_ref, ring_ref, *refs):
    total = None
    rows_refs = refs[:visits]
    width = rows_refs[0].shape[1] - 2 * part
    at = visits
    chips = ring_ref.shape[0] // 2
    position = ring_ref[where_ref[0] // 2]
    first_core = where_ref[1] == 0
    for offset in blocks:
        chip = ring_ref[chips + lax.rem(position + offset + chips, chips)]
        start = pl.multiple_of(chip * 2 * wrows, 128)
        columns = jnp.concatenate([r[:, pl.ds(start, 2 * wrows)] for r in rows_refs], axis=0)
        mine, other = refs[at][:wrows], refs[at + 1][:wrows]
        at += 2
        weight = jnp.concatenate([jnp.where(first_core, mine, other), jnp.where(first_core, other, mine)], axis=0)
        term = mm(columns, weight)
        total = term if total is None else total + term
    if final:
        total = total + refs[at][...]
        start = pl.multiple_of(width + where_ref[1] * part, 128)
        rows = rows_refs[0].shape[0]
        for i, out_ref in enumerate(refs[at + 1 :]):
            residual = rows_refs[i][:, pl.ds(start, part)].astype(F32)
            out_ref[...] = (residual + total[i * rows : (i + 1) * rows]).astype(BF16)
    else:
        refs[at][...] = total


def proj(wrows, blocks, where, ring, visits, weights, acc=None):
    final = acc is not None
    rows, part = visits[0].shape[0], weights[0].shape[1]
    operands = [where, ring] + visits + weights + ([acc] if final else [])
    count = len(visits)
    if final:
        outs = [jax.ShapeDtypeStruct((rows, part), BF16)] * count
    else:
        outs = [jax.ShapeDtypeStruct((rows * count, part), F32)]
    return pl.pallas_call(
        functools.partial(proj_kernel, wrows, part, blocks, count, final),
        out_shape=outs,
        in_specs=[smem()] * 2 + [vmem()] * (len(operands) - 2),
        out_specs=[vmem()] * len(outs),
        compiler_params=params(),
        cost_estimate=pl.CostEstimate(
            flops=8 * rows * count * part * wrows * len(blocks),
            bytes_accessed=4 * part * wrows * len(blocks) + 8 * rows * count * part,
            transcendentals=0,
        ),
        name="proj_final" if final else "proj_part",
    )(*operands)


def tables_kernel(wrows, slots, topk, rows, where_ref, *refs):
    pick_ref, put_ref, factor_ref = refs[-3:]
    both = 2 * rows
    expert_id = where_ref[0].astype(F32)
    row_of = lax.broadcasted_iota(jnp.int32, (both, both), 0)
    row_at = lax.broadcasted_iota(jnp.int32, (both, both), 1)
    slot_of = lax.broadcasted_iota(jnp.int32, (slots, both), 0).astype(F32)
    slot_at = lax.broadcasted_iota(jnp.int32, (both, slots), 1).astype(F32)
    for block in range(pick_ref.shape[0]):
        named = [refs[2 * block + i][wrows:].astype(F32) for i in range(2)]
        per_row = named[0].shape[1] // rows
        selected, factor = [], []
        for n in named:
            item = [n[i // per_row : i // per_row + 1, (i % per_row) * rows : (i % per_row + 1) * rows] for i in range(4 * topk)]
            hits = [item[k] == expert_id for k in range(topk)]
            values = [item[topk + k] + item[2 * topk + k] + item[3 * topk + k] for k in range(topk)]
            selected.append(sum(h.astype(F32) for h in hits))
            factor.append(sum(jnp.where(h, v, 0.0) for h, v in zip(hits, values)))
        selected = jnp.concatenate(selected, axis=1)
        factor = jnp.concatenate(factor, axis=1)
        spread = jnp.broadcast_to(selected, (both, both))
        before = jnp.sum(jnp.where(row_at < row_of, spread, 0.0), axis=1, keepdims=True)
        selected_down = jnp.sum(jnp.where(row_at == row_of, spread, 0.0), axis=1, keepdims=True)
        slot_down = jnp.where(selected_down > 0.0, before, -1.0)
        put_ref[block] = (slot_at == slot_down).astype(F32).astype(BF16)
        slot = jnp.sum(jnp.where(row_at == row_of, jnp.broadcast_to(slot_down, (both, both)), 0.0), axis=0, keepdims=True)
        taken = slot_of == slot
        pick_ref[block] = taken.astype(F32).astype(BF16)
        factor_ref[block] = jnp.sum(jnp.where(taken, factor, 0.0), axis=1, keepdims=True)


def tables(wrows, slots, topk, rows, where, blocks):
    chips = len(blocks) // 2
    both = 2 * rows
    return pl.pallas_call(
        functools.partial(tables_kernel, wrows, slots, topk, rows),
        out_shape=[
            jax.ShapeDtypeStruct((chips, slots, both), BF16),
            jax.ShapeDtypeStruct((chips, both, slots), BF16),
            jax.ShapeDtypeStruct((chips, slots, 1), F32),
        ],
        in_specs=[smem()] + [vmem()] * len(blocks),
        out_specs=[vmem()] * 3,
        compiler_params=params(),
        cost_estimate=pl.CostEstimate(flops=0, bytes_accessed=8 * chips * slots * both, transcendentals=0),
        name="tables",
    )(where, *blocks)


def expert_kernel(first, blocks, pieces, gain_ref, pick_ref, put_ref, factor_ref, gate_ref, up_ref, down_ref, *refs):
    slots, rows = pick_ref.shape[1:]
    own = rows // 2
    width = gain_ref.shape[1]
    hidden_units = gate_ref.shape[1]
    inputs = refs[: blocks * pieces]
    mine = refs[blocks * pieces : blocks * pieces + blocks]
    theirs, normed, hidden = refs[-3:]

    for b in range(blocks):
        block = jnp.concatenate([inputs[b * pieces + i][...] for i in range(pieces)], axis=0)
        taken = mm(pick_ref[first + b], block)
        scale = lax.rsqrt(jnp.sum(taken * taken, axis=1, keepdims=True) * (1.0 / width) + 1e-06)
        normed[b * slots : (b + 1) * slots, :] = (taken * scale * gain_ref[...]).astype(BF16)

    for start in range(0, hidden_units, TILE):
        columns = slice(start, min(start + TILE, hidden_units))
        gate_part = mm(normed[...], gate_ref[:, columns])
        up_part = mm(normed[...], up_ref[:, columns])
        hidden[:, columns] = (jax.nn.silu(gate_part) * up_part).astype(BF16)

    for start in range(0, width, TILE):
        columns = slice(start, start + TILE)
        result = mm(hidden[...], down_ref[:, columns])
        for b in range(blocks):
            weighted = (result[b * slots : (b + 1) * slots] * factor_ref[first + b]).astype(BF16)
            placed = mm(put_ref[first + b], weighted).astype(BF16)
            mine[b][:, columns] = placed[:own]
            theirs[b * own : (b + 1) * own, columns] = placed[own:]


def expert(first, blocks, tabs, gain, weights, inputs):
    slots, rows = tabs[0].shape[1:]
    width, hidden_units = weights[0].shape
    own = rows // 2
    m = blocks * slots
    weights = [pltpu.with_memory_space_constraint(w, pltpu.VMEM) for w in weights]
    out = pl.pallas_call(
        functools.partial(expert_kernel, first, blocks, len(inputs) // blocks),
        out_shape=[jax.ShapeDtypeStruct((own, width), BF16)] * blocks
        + [jax.ShapeDtypeStruct((blocks * own, width), BF16)],
        in_specs=[vmem()] * (7 + len(inputs)),
        out_specs=[vmem()] * (blocks + 1),
        scratch_shapes=[
            pltpu.VMEM((m, width), BF16),
            pltpu.VMEM((m, hidden_units), BF16),
        ],
        compiler_params=params(),
        cost_estimate=pl.CostEstimate(
            flops=2 * m * width * hidden_units,
            bytes_accessed=8 * blocks * rows * width,
            transcendentals=m * hidden_units,
        ),
        name="expert",
    )(gain, *tabs, *weights, *inputs)
    return out[:-1], out[-1]


def shared_kernel(count, gain_ref, gate_hbm, up_hbm, down_hbm, *refs):
    inputs, outs = refs[:count], refs[count + 1 : 2 * count + 1]
    gate_ref, up_ref, down_ref, normed, hidden, sems = refs[2 * count + 1 :]
    units, width = gate_ref.shape
    rows = inputs[0].shape[0]
    tiles = [(start, min(256, units - start)) for start in range(0, units, 256)]
    copies = []
    for i, (start, size) in enumerate(tiles):
        span = pl.ds(start, size)
        for j, (source, target) in enumerate(((gate_hbm, gate_ref), (up_hbm, up_ref))):
            copies.append(pltpu.make_async_copy(source.at[span], target.at[span], sems.at[2 * i + j]))
    copies.append(pltpu.make_async_copy(down_hbm, down_ref, sems.at[2 * len(tiles)]))
    for copy in copies:
        copy.start()
    for i, ref in enumerate(inputs):
        x = ref[...].astype(F32)
        scale = lax.rsqrt(jnp.sum(x * x, axis=1, keepdims=True) * (1.0 / width) + 1e-06)
        normed[i * rows : (i + 1) * rows] = (x * scale * gain_ref[...]).astype(BF16)
    across = (((1,), (1,)), ((), ()))
    for i, (start, size) in enumerate(tiles):
        span = slice(start, start + size)
        copies[2 * i].wait()
        copies[2 * i + 1].wait()
        gate_part = lax.dot_general(normed[...], gate_ref[span], across, preferred_element_type=F32)
        up_part = lax.dot_general(normed[...], up_ref[span], across, preferred_element_type=F32)
        hidden[:, span] = (jax.nn.silu(gate_part) * up_part).astype(BF16)
    copies[-1].wait()
    for start in range(0, width, TILE):
        span = slice(start, start + TILE)
        result = mm(hidden[...], down_ref[:, span])
        for i, ref in enumerate(outs):
            ref[:, span] = result[i * rows : (i + 1) * rows].astype(ref.dtype)


def shared_expert(gain, weights, inputs, after):
    count = len(inputs)
    rows, width = inputs[0].shape
    units = weights[0].shape[0]
    weights = [pltpu.with_memory_space_constraint(w, pltpu.HBM) for w in weights]
    shapes = [jax.ShapeDtypeStruct((rows, width), F32)] + [jax.ShapeDtypeStruct((rows, width), BF16)] * (count - 1)
    return pl.pallas_call(
        functools.partial(shared_kernel, count),
        out_shape=shapes,
        in_specs=[vmem()] + [hbm()] * 3 + [vmem()] * count + [hbm()],
        out_specs=[vmem()] * count,
        scratch_shapes=[pltpu.VMEM((units, width), BF16)] * 3
        + [
            pltpu.VMEM((count * rows, width), BF16),
            pltpu.VMEM((count * rows, units), BF16),
            pltpu.SemaphoreType.DMA((2 * -(-units // 256) + 1,)),
        ],
        compiler_params=pltpu.CompilerParams(vmem_limit_bytes=24 * 1024 * 1024),
        cost_estimate=pl.CostEstimate(
            flops=12 * count * rows * width * units,
            bytes_accessed=6 * units * width + 4 * count * rows * width,
            transcendentals=count * rows * units,
        ),
        name="shared",
    )(gain, *weights, *inputs, after)


def base_kernel(*refs):
    total = refs[0][...]
    for ref in refs[1:-1]:
        total = total + ref[...].astype(F32)
    refs[-1][...] = total


def half_sum_kernel(base_ref, top_ref, bottom_ref, out_ref):
    rows = top_ref.shape[0]
    for span, ref in ((slice(0, rows), top_ref), (slice(rows, 2 * rows), bottom_ref)):
        out_ref[span] = (base_ref[span] + ref[...].astype(F32)).astype(out_ref.dtype)


def plain_call(kernel, name, shape, operands):
    return pl.pallas_call(
        kernel,
        out_shape=shape,
        in_specs=[vmem()] * len(operands),
        out_specs=vmem(),
        compiler_params=params(),
        cost_estimate=pl.CostEstimate(flops=0, bytes_accessed=8 * operands[0].size, transcendentals=0),
        name=name,
    )(*operands)


def add_kernel(count, *refs):
    total = refs[0][...].astype(F32)
    for ref in refs[1:count]:
        total = total + ref[...].astype(F32)
    refs[-1][...] = total.astype(BF16)


def add(rows, after, *terms):
    width = terms[0][0].shape[1]

    def block(index):
        return pl.BlockSpec((rows, width), lambda i: (index, 0))

    return pl.pallas_call(
        functools.partial(add_kernel, len(terms)),
        grid=(1,),
        out_shape=jax.ShapeDtypeStruct((rows, width), BF16),
        in_specs=[block(index) for _, index in terms] + [hbm()] * len(after),
        out_specs=block(0),
        compiler_params=params(),
        cost_estimate=pl.CostEstimate(
            flops=rows * width * len(terms), bytes_accessed=2 * rows * width * (len(terms) + 1), transcendentals=0
        ),
        name="add",
    )(*[array for array, _ in terms], *after)


def body(
    req_size,
    exp_size,
    attn_out,
    residual,
    out_weight,
    norm_gain,
    expert_ids,
    gate_weights,
    expert_gate,
    expert_up,
    expert_down,
    shared_gate,
    shared_up,
    shared_down,
):
    rows, width = attn_out.shape
    half = width // 2
    part = half // req_size
    topk = expert_ids.shape[1]
    wrows = out_weight.shape[0]
    capacity = min(rows, 3 * rows * topk // (2 * exp_size))
    slots = -(-2 * capacity // 16) * 16
    chips = exp_size // 2
    depth = chips // 2
    order = ring_order(chips)
    me = lax.axis_index("exp")
    request = lax.axis_index("req")
    here = jnp.stack([me, me % 2, lax.axis_index("req")]).astype(jnp.int32)
    ring = jnp.asarray([order.index(q) for q in range(chips)] + order, jnp.int32)

    steps = [(order[i], order[(i + 1) % chips]) for i in range(chips)]
    ahead = [(2 * a + c, 2 * b + c) for a, b in steps for c in range(2)]
    behind = [(b, a) for a, b in ahead]

    def to_ahead(x):
        return lax.ppermute(x, "exp", ahead)

    def to_behind(x):
        return lax.ppermute(x, "exp", behind)

    def to_core(x):
        return lax.ppermute(x, "exp", [(d, d ^ 1) for d in range(exp_size)])

    def to_request(x, shift, swap=0):
        pairs = [
            (i * exp_size + d, ((i + shift) % req_size) * exp_size + (d ^ swap))
            for i in range(req_size)
            for d in range(exp_size)
        ]
        return lax.ppermute(x, ("req", "exp"), pairs)

    weight_own, weight_sent, packed = prepare(
        req_size, part, here, expert_ids.T, gate_weights.T, out_weight, attn_out, residual
    )
    weight_met = to_core(weight_sent)
    chains = [(weight_own, weight_own), (weight_met, weight_met)]
    arrived = [[weight_own, weight_met]]
    for _ in range(1, depth):
        chains = [(to_ahead(low), to_behind(high)) for low, high in chains]
        (low_own, high_own), (low_met, high_met) = chains
        arrived += [[low_own, low_met], [high_own, high_met]]

    visits = [packed[0]] + [to_request(packed[shift], shift) for shift in range(1, req_size)]
    last = [to_ahead(arrived[-2][0]), to_behind(arrived[-1][1])]
    arrived[-2:], visits[1:] = lax.optimization_barrier((arrived[-2:], visits[1:]))
    visits += [to_core(v) for v in visits]

    early = [w for block in arrived[:-2] for w in block]
    late = last + [w for block in arrived[-2:] for w in block]
    whole = [w for block in arrived for w in block]
    places = [0] + [side * k for k in range(1, depth) for side in (-1, 1)]
    (acc,) = proj(wrows, places, here, ring, visits, whole)
    product = proj(wrows, [depth], here, ring, visits, last, acc)
    product, early = lax.optimization_barrier((product, early))
    tabs_early = tables(wrows, slots, topk, rows, here, early)
    tabs_late = tables(wrows, slots, topk, rows, here, late)

    got = {}
    for shift in reversed(range(req_size)):
        for swap in range(2):
            piece = product[swap * req_size + shift]
            if shift == 0:
                got[shift, swap] = piece if swap == 0 else to_core(piece)
            else:
                got[shift, swap] = to_request(piece, req_size - shift, swap)
    near = beside(here, [got[0, 0], got[0, 1]])
    far, tabs_early, tabs_late = lax.optimization_barrier(
        ([got[place, swap] for place in range(1, req_size) for swap in range(2)], tabs_early, tabs_late)
    )
    far = beside(here, far)
    gain = norm_gain.reshape(1, width)
    weights = [expert_gate[0], expert_up[0], expert_down[0]]

    lows, highs = [to_ahead(near)], [to_behind(near)]
    lows, highs, far = lax.optimization_barrier((lows, highs, far))
    lows.append(to_ahead(far))
    highs.append(to_behind(far))
    own_rows = weave(req_size, here, [near, far])
    results = {0: expert(0, 1, tabs_early, gain, weights, [own_rows, to_core(own_rows)])}
    lows, highs, results[0] = lax.optimization_barrier((lows, highs, results[0]))
    low, high = weave(req_size, here, lows), weave(req_size, here, highs)
    came = {}
    theirs = results[0][1]
    for k in range(1, depth):
        if k > 1:
            low, high, results[k - 1] = lax.optimization_barrier((low, high, results[k - 1]))
            if k == 2:
                low, high, shared_rows = lax.optimization_barrier((low, high, shared_rows))
            theirs = results[k - 1][1]
        if k == depth - 1:
            shared = shared_expert(
                gain, [shared_gate.T, shared_up.T, shared_down.T], shared_rows, results[k - 2][1]
            )
            backs = [to_request(shared[shift], req_size - shift) for shift in range(1, req_size)]
            low, high, shared, came[0] = lax.optimization_barrier((low, high, shared, came[0]))
        others = to_core(low), to_core(high)
        if k == depth - 1:
            others, theirs = lax.optimization_barrier((others, theirs))
        came[k - 1] = to_core(theirs)
        if k == 1:
            shared_rows = [own_rows]
            for shift in range(1, req_size):
                shared_rows.append(to_request(own_rows, shift))
        first, tabs = (2 * k - 1, tabs_early) if k < depth - 1 else (1, tabs_late)
        results[k] = expert(first, 2, tabs, gain, weights, [low, others[0], high, others[1]])
        if k < depth - 1:
            low, high = to_ahead(low), to_behind(high)
        else:
            low, high = to_ahead(low[: rows // 2]), to_behind(high[rows // 2 :])
    low, high, results[depth - 1] = lax.optimization_barrier((low, high, results[depth - 1]))
    results[depth] = expert(0, 1, tabs_late, gain, weights, [low, high, to_core(low), to_core(high)])

    cut = rows // 2
    came, results[depth] = lax.optimization_barrier((came, results[depth]))
    came[depth - 1], came[depth] = to_core(results[depth - 1][1]), to_core(results[depth][1])

    def step(after, k, low_chunk, low, high):
        low_mine, high_mine = results[k][0]
        low_terms = [(low_mine, low_chunk), (came[k], low_chunk)] + [(x, 0) for x in low]
        high_terms = [(high_mine, 1 - low_chunk), (came[k], 3 - low_chunk)] + [(x, 0) for x in high]
        low_sum = add(cut, after, *low_terms)
        high_sum = add(cut, [low_sum], *high_terms)
        return [high_sum], [to_behind(low_sum)], [to_ahead(high_sum)]

    (mine,), _ = results[depth]
    low_sum = add(cut, [], (mine, 1), (came[depth], 1))
    high_sum = add(cut, [low_sum], (mine, 0), (came[depth], 0))
    first = [to_behind(low_sum)], [to_ahead(high_sum)]
    second = [], []
    after = [high_sum]
    for k in range(depth - 1, 0, -1):
        if k == depth - 2:
            after, backs = lax.optimization_barrier((after, backs))
        after, *second = step(after, k, 0, *second)
        after, *first = step(after, k, 1, *first)
    (mine,), _ = results[0]
    terms = [shared[0], own_rows, mine, came[0]] + backs
    base = plain_call(base_kernel, "base", jax.ShapeDtypeStruct((rows, width), F32), terms)
    shape = base.shape
    part_sum = plain_call(
        half_sum_kernel, "part_sum", jax.ShapeDtypeStruct(shape, F32), [base, second[0][0], second[1][0]]
    )
    return plain_call(
        half_sum_kernel, "final", jax.ShapeDtypeStruct(shape, BF16), [part_sum, first[1][0], first[0][0]]
    )


def solution(mesh):
    return jax.shard_map(
        functools.partial(body, mesh.shape["req"], mesh.shape["exp"]),
        mesh=mesh,
        in_specs=(
            P(("req", "exp"), None),
            P(("req", "exp"), None),
            P("exp", None),
            P(),
            P(("req", "exp"), None),
            P(("req", "exp"), None),
            P("exp", None, None),
            P("exp", None, None),
            P("exp", None, None),
            P(None, "req"),
            P(None, "req"),
            P(None, "req"),
        ),
        out_specs=P(("req", "exp"), None),
        check_vma=False,
    )
```

```python
import functools

import jax
import jax.numpy as jnp
from jax import lax
from jax.experimental import pallas as pl
from jax.experimental.pallas import tpu as pltpu
from jax.sharding import PartitionSpec as P

F32 = jnp.float32
BF16 = jnp.bfloat16
VMEM_BYTES = 12 * 1024 * 1024
TILE = 512
HIDDEN_TILE = 768
DOWN_TILE = 1024
TABLE_ROWS = 16


def ring_order(chips):
    slow = 4
    fast = chips // slow
    order = [a * fast for a in range(slow)]
    for turn, a in enumerate(reversed(range(slow))):
        inner = range(1, fast) if turn % 2 == 0 else range(fast - 1, 0, -1)
        order += [a * fast + b for b in inner]
    return order


def mm(a, b):
    return jnp.dot(a, b, preferred_element_type=F32)


def vmem():
    return pl.BlockSpec(memory_space=pltpu.VMEM)


def smem():
    return pl.BlockSpec(memory_space=pltpu.SMEM)


def hbm():
    return pl.BlockSpec(memory_space=pl.ANY)


def params():
    return pltpu.CompilerParams(vmem_limit_bytes=VMEM_BYTES)


def prepare_kernel(count, part, where_ref, ids_hbm, factors_hbm, weight_hbm, attn_hbm, residual_hbm, own_ref, sent_ref, *refs):
    packs = refs[:count]
    ids_ref, factors_ref, sems = refs[count:]
    wrows, width = weight_hbm.shape
    topk, rows = ids_ref.shape
    core, request = where_ref[1], where_ref[2]
    moves = [(ids_hbm, ids_ref), (factors_hbm, factors_ref)]
    for ref, which in ((own_ref, core), (sent_ref, 1 - core)):
        start = pl.multiple_of(which * (width // 2) + request * part, 128)
        moves.append((weight_hbm.at[:, pl.ds(start, part)], ref.at[:wrows]))
    for shift, ref in enumerate(packs):
        moves.append((attn_hbm, ref.at[:, :width]))
        other = lax.rem(request + shift, count)
        for half in range(2):
            start = pl.multiple_of(half * (width // 2) + other * part, 128)
            target = ref.at[:, width + half * part : width + (half + 1) * part]
            moves.append((residual_hbm.at[:, pl.ds(start, part)], target))
    copies = [pltpu.make_async_copy(source, target, sems.at[i]) for i, (source, target) in enumerate(moves)]
    for copy in copies:
        copy.start()
    for copy in copies[:2]:
        copy.wait()
    per_row = part // rows
    factors = factors_ref[...]
    big = factors.astype(BF16).astype(F32)
    middle = (factors - big).astype(BF16).astype(F32)
    named = (ids_ref[...].astype(F32), big, middle, factors - big - middle)
    items = [kind[k : k + 1] for kind in named for k in range(topk)]
    items += [jnp.zeros((1, rows), F32)] * (-len(items) % per_row)
    lines = [jnp.concatenate(items[i : i + per_row], axis=1) for i in range(0, len(items), per_row)]
    lines.append(jnp.zeros((TABLE_ROWS - len(lines), part), F32))
    table = jnp.concatenate(lines, axis=0).astype(BF16)
    own_ref[wrows:] = table
    sent_ref[wrows:] = table
    for copy in copies[2:]:
        copy.wait()


def prepare(count, part, where, ids, factors, weight, attn, residual):
    rows, width = attn.shape
    shape = jax.ShapeDtypeStruct((weight.shape[0] + TABLE_ROWS, part), BF16)
    packed = jax.ShapeDtypeStruct((rows, width + 2 * part), BF16)
    arrays = [pltpu.with_memory_space_constraint(x, pltpu.HBM) for x in (ids, factors, weight, attn, residual)]
    out = pl.pallas_call(
        functools.partial(prepare_kernel, count, part),
        out_shape=[shape] * 2 + [packed] * count,
        in_specs=[smem()] + [hbm()] * 5,
        out_specs=[vmem()] * (2 + count),
        scratch_shapes=[
            pltpu.VMEM(ids.shape, ids.dtype),
            pltpu.VMEM(factors.shape, factors.dtype),
            pltpu.SemaphoreType.DMA((4 + 3 * count,)),
        ],
        compiler_params=params(),
        cost_estimate=pl.CostEstimate(flops=0, bytes_accessed=8 * attn.size, transcendentals=0),
        name="prepare",
    )(where, *arrays)
    return out[0], out[1], out[2:]


def small_call(kernel, name, shapes, operands, moved):
    return pl.pallas_call(
        kernel,
        out_shape=shapes,
        in_specs=[smem()] + [vmem()] * (len(operands) - 1),
        out_specs=[vmem()] * len(shapes),
        compiler_params=params(),
        cost_estimate=pl.CostEstimate(flops=0, bytes_accessed=moved, transcendentals=0),
        name=name,
    )(*operands)


def beside_kernel(where_ref, *refs):
    part = refs[0].shape[1]
    for i, ref in enumerate(refs[:-1]):
        refs[-1][:, i * part : (i + 1) * part] = ref[...]


def beside(where, pieces):
    rows, part = pieces[0].shape
    shape = jax.ShapeDtypeStruct((rows, len(pieces) * part), BF16)
    return small_call(beside_kernel, "beside", [shape], [where] + pieces, 4 * rows * part * len(pieces))[0]


def weave_kernel(count, where_ref, *refs):
    out_ref = refs[-1]
    part = out_ref.shape[1] // (2 * count)
    place = 0
    for ref in refs[:-1]:
        for at in range(ref.shape[1] // (2 * part)):
            request = lax.rem(where_ref[2] + place, count)
            place += 1
            for swap in range(2):
                core = where_ref[1] if swap == 0 else 1 - where_ref[1]
                start = pl.multiple_of(core * (count * part) + request * part, 128)
                out_ref[:, pl.ds(start, part)] = ref[:, (2 * at + swap) * part : (2 * at + swap + 1) * part]


def weave(count, where, pieces):
    rows = pieces[0].shape[0]
    width = sum(p.shape[1] for p in pieces)
    shape = jax.ShapeDtypeStruct((rows, width), BF16)
    return small_call(functools.partial(weave_kernel, count), "weave", [shape], [where] + pieces, 4 * rows * width)[0]


def proj_kernel(wrows, part, blocks, visits, final, where_ref, ring_ref, *refs):
    total = None
    rows_refs = refs[:visits]
    width = rows_refs[0].shape[1] - 2 * part
    at = visits
    chips = ring_ref.shape[0] // 2
    position = ring_ref[where_ref[0] // 2]
    first_core = where_ref[1] == 0
    for offset in blocks:
        chip = ring_ref[chips + lax.rem(position + offset + chips, chips)]
        start = pl.multiple_of(chip * 2 * wrows, 128)
        columns = jnp.concatenate([r[:, pl.ds(start, 2 * wrows)] for r in rows_refs], axis=0)
        mine, other = refs[at][:wrows], refs[at + 1][:wrows]
        at += 2
        weight = jnp.concatenate([jnp.where(first_core, mine, other), jnp.where(first_core, other, mine)], axis=0)
        term = mm(columns, weight)
        total = term if total is None else total + term
    if final:
        total = total + refs[at][...]
        start = pl.multiple_of(width + where_ref[1] * part, 128)
        rows = rows_refs[0].shape[0]
        for i, out_ref in enumerate(refs[at + 1 :]):
            residual = rows_refs[i][:, pl.ds(start, part)].astype(F32)
            out_ref[...] = (residual + total[i * rows : (i + 1) * rows]).astype(BF16)
    else:
        refs[at][...] = total


def proj(wrows, blocks, where, ring, visits, weights, acc=None):
    final = acc is not None
    rows, part = visits[0].shape[0], weights[0].shape[1]
    operands = [where, ring] + visits + weights + ([acc] if final else [])
    count = len(visits)
    if final:
        outs = [jax.ShapeDtypeStruct((rows, part), BF16)] * count
    else:
        outs = [jax.ShapeDtypeStruct((rows * count, part), F32)]
    return pl.pallas_call(
        functools.partial(proj_kernel, wrows, part, blocks, count, final),
        out_shape=outs,
        in_specs=[smem()] * 2 + [vmem()] * (len(operands) - 2),
        out_specs=[vmem()] * len(outs),
        compiler_params=params(),
        cost_estimate=pl.CostEstimate(
            flops=8 * rows * count * part * wrows * len(blocks),
            bytes_accessed=4 * part * wrows * len(blocks) + 8 * rows * count * part,
            transcendentals=0,
        ),
        name="proj_final" if final else "proj_part",
    )(*operands)


def tables_kernel(wrows, slots, topk, rows, where_ref, *refs):
    pick_ref, put_ref, factor_ref = refs[-3:]
    both = 2 * rows
    expert_id = where_ref[0].astype(F32)
    row_of = lax.broadcasted_iota(jnp.int32, (both, both), 0)
    row_at = lax.broadcasted_iota(jnp.int32, (both, both), 1)
    slot_of = lax.broadcasted_iota(jnp.int32, (slots, both), 0).astype(F32)
    slot_at = lax.broadcasted_iota(jnp.int32, (both, slots), 1).astype(F32)
    for block in range(pick_ref.shape[0]):
        named = [refs[2 * block + i][wrows:].astype(F32) for i in range(2)]
        per_row = named[0].shape[1] // rows
        selected, factor = [], []
        for n in named:
            item = [n[i // per_row : i // per_row + 1, (i % per_row) * rows : (i % per_row + 1) * rows] for i in range(4 * topk)]
            hits = [item[k] == expert_id for k in range(topk)]
            values = [item[topk + k] + item[2 * topk + k] + item[3 * topk + k] for k in range(topk)]
            selected.append(sum(h.astype(F32) for h in hits))
            factor.append(sum(jnp.where(h, v, 0.0) for h, v in zip(hits, values)))
        selected = jnp.concatenate(selected, axis=1)
        factor = jnp.concatenate(factor, axis=1)
        spread = jnp.broadcast_to(selected, (both, both))
        before = jnp.sum(jnp.where(row_at < row_of, spread, 0.0), axis=1, keepdims=True)
        selected_down = jnp.sum(jnp.where(row_at == row_of, spread, 0.0), axis=1, keepdims=True)
        slot_down = jnp.where(selected_down > 0.0, before, -1.0)
        put_ref[block] = (slot_at == slot_down).astype(F32).astype(BF16)
        slot = jnp.sum(jnp.where(row_at == row_of, jnp.broadcast_to(slot_down, (both, both)), 0.0), axis=0, keepdims=True)
        taken = slot_of == slot
        pick_ref[block] = taken.astype(F32).astype(BF16)
        factor_ref[block] = jnp.sum(jnp.where(taken, factor, 0.0), axis=1, keepdims=True)


def tables(wrows, slots, topk, rows, where, blocks):
    chips = len(blocks) // 2
    both = 2 * rows
    return pl.pallas_call(
        functools.partial(tables_kernel, wrows, slots, topk, rows),
        out_shape=[
            jax.ShapeDtypeStruct((chips, slots, both), BF16),
            jax.ShapeDtypeStruct((chips, both, slots), BF16),
            jax.ShapeDtypeStruct((chips, slots, 1), F32),
        ],
        in_specs=[smem()] + [vmem()] * len(blocks),
        out_specs=[vmem()] * 3,
        compiler_params=params(),
        cost_estimate=pl.CostEstimate(flops=0, bytes_accessed=8 * chips * slots * both, transcendentals=0),
        name="tables",
    )(where, *blocks)


def expert_kernel(first, blocks, pieces, gain_ref, pick_ref, put_ref, factor_ref, gate_ref, up_ref, down_ref, *refs):
    slots, rows = pick_ref.shape[1:]
    own = rows // 2
    width = gain_ref.shape[1]
    hidden_units = gate_ref.shape[1]
    inputs = refs[: blocks * pieces]
    mine = refs[blocks * pieces : blocks * pieces + blocks]
    theirs, normed, hidden = refs[-3:]

    for b in range(blocks):
        block = jnp.concatenate([inputs[b * pieces + i][...] for i in range(pieces)], axis=0)
        taken = mm(pick_ref[first + b], block)
        scale = lax.rsqrt(jnp.sum(taken * taken, axis=1, keepdims=True) * (1.0 / width) + 1e-06)
        normed[b * slots : (b + 1) * slots, :] = (taken * scale * gain_ref[...]).astype(BF16)

    for start in range(0, hidden_units, HIDDEN_TILE):
        columns = slice(start, min(start + HIDDEN_TILE, hidden_units))
        gate_part = mm(normed[...], gate_ref[:, columns])
        up_part = mm(normed[...], up_ref[:, columns])
        hidden[:, columns] = (jax.nn.silu(gate_part) * up_part).astype(BF16)

    for start in range(0, width, DOWN_TILE):
        columns = slice(start, start + DOWN_TILE)
        result = mm(hidden[...], down_ref[:, columns])
        for b in range(blocks):
            weighted = (result[b * slots : (b + 1) * slots] * factor_ref[first + b]).astype(BF16)
            placed = mm(put_ref[first + b], weighted).astype(BF16)
            mine[b][:, columns] = placed[:own]
            theirs[b * own : (b + 1) * own, columns] = placed[own:]


def expert(first, blocks, tabs, gain, weights, inputs):
    slots, rows = tabs[0].shape[1:]
    width, hidden_units = weights[0].shape
    own = rows // 2
    m = blocks * slots
    weights = [pltpu.with_memory_space_constraint(w, pltpu.VMEM) for w in weights]
    out = pl.pallas_call(
        functools.partial(expert_kernel, first, blocks, len(inputs) // blocks),
        out_shape=[jax.ShapeDtypeStruct((own, width), BF16)] * blocks
        + [jax.ShapeDtypeStruct((blocks * own, width), BF16)],
        in_specs=[vmem()] * (7 + len(inputs)),
        out_specs=[vmem()] * (blocks + 1),
        scratch_shapes=[
            pltpu.VMEM((m, width), BF16),
            pltpu.VMEM((m, hidden_units), BF16),
        ],
        compiler_params=params(),
        cost_estimate=pl.CostEstimate(
            flops=2 * m * width * hidden_units,
            bytes_accessed=8 * blocks * rows * width,
            transcendentals=m * hidden_units,
        ),
        name="expert",
    )(gain, *tabs, *weights, *inputs)
    return out[:-1], out[-1]


def shared_kernel(count, gain_ref, gate_hbm, up_hbm, down_hbm, *refs):
    inputs, outs = refs[:count], refs[count + 1 : 2 * count + 1]
    gate_ref, up_ref, down_ref, normed, hidden, sems = refs[2 * count + 1 :]
    units, width = gate_ref.shape
    rows = inputs[0].shape[0]
    tiles = [(start, min(256, units - start)) for start in range(0, units, 256)]
    copies = []
    for i, (start, size) in enumerate(tiles):
        span = pl.ds(start, size)
        for j, (source, target) in enumerate(((gate_hbm, gate_ref), (up_hbm, up_ref))):
            copies.append(pltpu.make_async_copy(source.at[span], target.at[span], sems.at[2 * i + j]))
    copies.append(pltpu.make_async_copy(down_hbm, down_ref, sems.at[2 * len(tiles)]))
    for copy in copies:
        copy.start()
    for i, ref in enumerate(inputs):
        x = ref[...].astype(F32)
        scale = lax.rsqrt(jnp.sum(x * x, axis=1, keepdims=True) * (1.0 / width) + 1e-06)
        normed[i * rows : (i + 1) * rows] = (x * scale * gain_ref[...]).astype(BF16)
    across = (((1,), (1,)), ((), ()))
    for i, (start, size) in enumerate(tiles):
        span = slice(start, start + size)
        copies[2 * i].wait()
        copies[2 * i + 1].wait()
        gate_part = lax.dot_general(normed[...], gate_ref[span], across, preferred_element_type=F32)
        up_part = lax.dot_general(normed[...], up_ref[span], across, preferred_element_type=F32)
        hidden[:, span] = (jax.nn.silu(gate_part) * up_part).astype(BF16)
    copies[-1].wait()
    for start in range(0, width, TILE):
        span = slice(start, start + TILE)
        result = mm(hidden[...], down_ref[:, span])
        for i, ref in enumerate(outs):
            ref[:, span] = result[i * rows : (i + 1) * rows].astype(ref.dtype)


def shared_expert(gain, weights, inputs, after):
    count = len(inputs)
    rows, width = inputs[0].shape
    units = weights[0].shape[0]
    weights = [pltpu.with_memory_space_constraint(w, pltpu.HBM) for w in weights]
    shapes = [jax.ShapeDtypeStruct((rows, width), F32)] + [jax.ShapeDtypeStruct((rows, width), BF16)] * (count - 1)
    return pl.pallas_call(
        functools.partial(shared_kernel, count),
        out_shape=shapes,
        in_specs=[vmem()] + [hbm()] * 3 + [vmem()] * count + [hbm()],
        out_specs=[vmem()] * count,
        scratch_shapes=[pltpu.VMEM((units, width), BF16)] * 3
        + [
            pltpu.VMEM((count * rows, width), BF16),
            pltpu.VMEM((count * rows, units), BF16),
            pltpu.SemaphoreType.DMA((2 * -(-units // 256) + 1,)),
        ],
        compiler_params=pltpu.CompilerParams(vmem_limit_bytes=24 * 1024 * 1024),
        cost_estimate=pl.CostEstimate(
            flops=12 * count * rows * width * units,
            bytes_accessed=6 * units * width + 4 * count * rows * width,
            transcendentals=count * rows * units,
        ),
        name="shared",
    )(gain, *weights, *inputs, after)


def base_kernel(*refs):
    total = refs[0][...]
    for ref in refs[1:-1]:
        total = total + ref[...].astype(F32)
    refs[-1][...] = total


def half_sum_kernel(base_ref, top_ref, bottom_ref, out_ref):
    rows = top_ref.shape[0]
    for span, ref in ((slice(0, rows), top_ref), (slice(rows, 2 * rows), bottom_ref)):
        out_ref[span] = (base_ref[span] + ref[...].astype(F32)).astype(out_ref.dtype)


def plain_call(kernel, name, shape, operands):
    return pl.pallas_call(
        kernel,
        out_shape=shape,
        in_specs=[vmem()] * len(operands),
        out_specs=vmem(),
        compiler_params=params(),
        cost_estimate=pl.CostEstimate(flops=0, bytes_accessed=8 * operands[0].size, transcendentals=0),
        name=name,
    )(*operands)


def add_kernel(count, *refs):
    total = refs[0][...].astype(F32)
    for ref in refs[1:count]:
        total = total + ref[...].astype(F32)
    refs[-1][...] = total.astype(BF16)


def add(rows, after, *terms):
    width = terms[0][0].shape[1]

    def block(index):
        return pl.BlockSpec((rows, width), lambda i: (index, 0))

    return pl.pallas_call(
        functools.partial(add_kernel, len(terms)),
        grid=(1,),
        out_shape=jax.ShapeDtypeStruct((rows, width), BF16),
        in_specs=[block(index) for _, index in terms] + [hbm()] * len(after),
        out_specs=block(0),
        compiler_params=params(),
        cost_estimate=pl.CostEstimate(
            flops=rows * width * len(terms), bytes_accessed=2 * rows * width * (len(terms) + 1), transcendentals=0
        ),
        name="add",
    )(*[array for array, _ in terms], *after)


def body(
    req_size,
    exp_size,
    attn_out,
    residual,
    out_weight,
    norm_gain,
    expert_ids,
    gate_weights,
    expert_gate,
    expert_up,
    expert_down,
    shared_gate,
    shared_up,
    shared_down,
):
    rows, width = attn_out.shape
    half = width // 2
    part = half // req_size
    topk = expert_ids.shape[1]
    wrows = out_weight.shape[0]
    capacity = min(rows, 3 * rows * topk // (2 * exp_size))
    slots = -(-2 * capacity // 16) * 16
    chips = exp_size // 2
    depth = chips // 2
    order = ring_order(chips)
    me = lax.axis_index("exp")
    request = lax.axis_index("req")
    here = jnp.stack([me, me % 2, lax.axis_index("req")]).astype(jnp.int32)
    ring = jnp.asarray([order.index(q) for q in range(chips)] + order, jnp.int32)

    steps = [(order[i], order[(i + 1) % chips]) for i in range(chips)]
    ahead = [(2 * a + c, 2 * b + c) for a, b in steps for c in range(2)]
    behind = [(b, a) for a, b in ahead]

    def to_ahead(x):
        return lax.ppermute(x, "exp", ahead)

    def to_behind(x):
        return lax.ppermute(x, "exp", behind)

    def to_core(x):
        return lax.ppermute(x, "exp", [(d, d ^ 1) for d in range(exp_size)])

    def to_request(x, shift, swap=0):
        pairs = [
            (i * exp_size + d, ((i + shift) % req_size) * exp_size + (d ^ swap))
            for i in range(req_size)
            for d in range(exp_size)
        ]
        return lax.ppermute(x, ("req", "exp"), pairs)

    weight_own, weight_sent, packed = prepare(
        req_size, part, here, expert_ids.T, gate_weights.T, out_weight, attn_out, residual
    )
    weight_met = to_core(weight_sent)
    chains = [(weight_own, weight_own), (weight_met, weight_met)]
    arrived = [[weight_own, weight_met]]
    for _ in range(1, depth):
        chains = [(to_ahead(low), to_behind(high)) for low, high in chains]
        (low_own, high_own), (low_met, high_met) = chains
        arrived += [[low_own, low_met], [high_own, high_met]]

    visits = [packed[0]] + [to_request(packed[shift], shift) for shift in range(1, req_size)]
    last = [to_ahead(arrived[-2][0]), to_behind(arrived[-1][1])]
    arrived[-2:], visits[1:] = lax.optimization_barrier((arrived[-2:], visits[1:]))
    visits += [to_core(v) for v in visits]

    early = [w for block in arrived[:-2] for w in block]
    late = last + [w for block in arrived[-2:] for w in block]
    whole = [w for block in arrived for w in block]
    places = [0] + [side * k for k in range(1, depth) for side in (-1, 1)]
    (acc,) = proj(wrows, places, here, ring, visits, whole)
    product = proj(wrows, [depth], here, ring, visits, last, acc)
    product, early = lax.optimization_barrier((product, early))
    tabs_early = tables(wrows, slots, topk, rows, here, early)
    tabs_late = tables(wrows, slots, topk, rows, here, late)

    got = {}
    for shift in reversed(range(req_size)):
        for swap in range(2):
            piece = product[swap * req_size + shift]
            if shift == 0:
                got[shift, swap] = piece if swap == 0 else to_core(piece)
            else:
                got[shift, swap] = to_request(piece, req_size - shift, swap)
    near = beside(here, [got[0, 0], got[0, 1]])
    far, tabs_early, tabs_late = lax.optimization_barrier(
        ([got[place, swap] for place in range(1, req_size) for swap in range(2)], tabs_early, tabs_late)
    )
    far = beside(here, far)
    gain = norm_gain.reshape(1, width)
    weights = [expert_gate[0], expert_up[0], expert_down[0]]

    lows, highs = [to_ahead(near)], [to_behind(near)]
    lows, highs, far = lax.optimization_barrier((lows, highs, far))
    lows.append(to_ahead(far))
    highs.append(to_behind(far))
    own_rows = weave(req_size, here, [near, far])
    results = {0: expert(0, 1, tabs_early, gain, weights, [own_rows, to_core(own_rows)])}
    lows, highs, results[0] = lax.optimization_barrier((lows, highs, results[0]))
    low, high = weave(req_size, here, lows), weave(req_size, here, highs)
    came = {}
    theirs = results[0][1]
    for k in range(1, depth):
        if k > 1:
            low, high, results[k - 1] = lax.optimization_barrier((low, high, results[k - 1]))
            if k == 2:
                low, high, shared_rows = lax.optimization_barrier((low, high, shared_rows))
            theirs = results[k - 1][1]
        if k == depth - 1:
            shared = shared_expert(
                gain, [shared_gate.T, shared_up.T, shared_down.T], shared_rows, results[k - 2][1]
            )
            backs = [to_request(shared[shift], req_size - shift) for shift in range(1, req_size)]
            low, high, shared, came[0] = lax.optimization_barrier((low, high, shared, came[0]))
        others = to_core(low), to_core(high)
        if k == depth - 1:
            others, theirs = lax.optimization_barrier((others, theirs))
        came[k - 1] = to_core(theirs)
        if k == 1:
            shared_rows = [own_rows]
            for shift in range(1, req_size):
                shared_rows.append(to_request(own_rows, shift))
        first, tabs = (2 * k - 1, tabs_early) if k < depth - 1 else (1, tabs_late)
        results[k] = expert(first, 2, tabs, gain, weights, [low, others[0], high, others[1]])
        if k < depth - 1:
            low, high = to_ahead(low), to_behind(high)
        else:
            low, high = to_ahead(low[: rows // 2]), to_behind(high[rows // 2 :])
    low, high, results[depth - 1] = lax.optimization_barrier((low, high, results[depth - 1]))
    results[depth] = expert(0, 1, tabs_late, gain, weights, [low, high, to_core(low), to_core(high)])

    cut = rows // 2
    came, results[depth] = lax.optimization_barrier((came, results[depth]))
    came[depth - 1], came[depth] = to_core(results[depth - 1][1]), to_core(results[depth][1])

    def step(after, k, low_chunk, low, high):
        low_mine, high_mine = results[k][0]
        low_terms = [(low_mine, low_chunk), (came[k], low_chunk)] + [(x, 0) for x in low]
        high_terms = [(high_mine, 1 - low_chunk), (came[k], 3 - low_chunk)] + [(x, 0) for x in high]
        low_sum = add(cut, after, *low_terms)
        high_sum = add(cut, [low_sum], *high_terms)
        return [high_sum], [to_behind(low_sum)], [to_ahead(high_sum)]

    (mine,), _ = results[depth]
    low_sum = add(cut, [], (mine, 1), (came[depth], 1))
    high_sum = add(cut, [low_sum], (mine, 0), (came[depth], 0))
    first = [to_behind(low_sum)], [to_ahead(high_sum)]
    second = [], []
    after = [high_sum]
    for k in range(depth - 1, 0, -1):
        if k == depth - 2:
            after, backs = lax.optimization_barrier((after, backs))
        after, *second = step(after, k, 0, *second)
        after, *first = step(after, k, 1, *first)
    (mine,), _ = results[0]
    terms = [shared[0], own_rows, mine, came[0]] + backs
    base = plain_call(base_kernel, "base", jax.ShapeDtypeStruct((rows, width), F32), terms)
    shape = base.shape
    part_sum = plain_call(
        half_sum_kernel, "part_sum", jax.ShapeDtypeStruct(shape, F32), [base, second[0][0], second[1][0]]
    )
    return plain_call(
        half_sum_kernel, "final", jax.ShapeDtypeStruct(shape, BF16), [part_sum, first[1][0], first[0][0]]
    )


def solution(mesh):
    return jax.shard_map(
        functools.partial(body, mesh.shape["req"], mesh.shape["exp"]),
        mesh=mesh,
        in_specs=(
            P(("req", "exp"), None),
            P(("req", "exp"), None),
            P("exp", None),
            P(),
            P(("req", "exp"), None),
            P(("req", "exp"), None),
            P("exp", None, None),
            P("exp", None, None),
            P("exp", None, None),
            P(None, "req"),
            P(None, "req"),
            P(None, "req"),
        ),
        out_specs=P(("req", "exp"), None),
        check_vma=False,
    )
```
